32 devices in a mesh: rows: 8 (over z, y), imgs: 4 (over x, core).
Axes of the slice: x: 2, y: 2, z: 4, core: 2. Of those that a mesh axis runs over, the one named last changes fastest.
Arguments:
- image_in: bfloat16 [16, 32, 32, 384], P('imgs', 'rows'), may hold values from -34 to 34
- condition: bfloat16 [16, 148], P('imgs'), may hold values from -5 to 5
- group_counts: int32 [4], replicated, may hold values from 1 to 4, as said below
- out_cotangent: bfloat16 [16, 64, 64, 192], P('imgs', 'rows'), may hold values from -6 to 6
- power_vectors: float32 [3, 192], replicated, may hold values from -5 to 5
- conv1_weight: float32 [3456, 192], P('rows'), may hold values from -0.109375 to 0.109375
- conv2_weight: float32 [1728, 192], P('rows'), may hold values from -0.15625 to 0.15625
- skip_weight: float32 [384, 192], P('rows'), may hold values from -0.3125 to 0.3125
- cond_weight: float32 [148, 1152], P(None, 'rows'), may hold values from -0.25 to 0.25
- out_bias: float32 [192], P('rows'), may hold values from -1.5 to 1.5
- conv1_first: float32 [3456, 192], P('rows'), may hold values from -1024 to 1024
- conv2_first: float32 [1728, 192], P('rows'), may hold values from -1024 to 1024
- skip_first: float32 [384, 192], P('rows'), may hold values from -1024 to 1024
- cond_first: float32 [148, 1152], P(None, 'rows'), may hold values from -1024 to 1024
- bias_first: float32 [192], P('rows'), may hold values from -1024 to 1024
- conv1_second: float32 [3456, 192], P('rows'), may hold values from 0 to 65536, as said below
- conv2_second: float32 [1728, 192], P('rows'), may hold values from 0 to 65536, as said below
- skip_second: float32 [384, 192], P('rows'), may hold values from 0 to 65536, as said below
- cond_second: float32 [148, 1152], P(None, 'rows'), may hold values from 0 to 65536, as said below
- bias_second: float32 [192], P('rows'), may hold values from 0 to 65536, as said below
Outputs:
- out_image: bfloat16 [16, 64, 64, 192], P('imgs', 'rows')
- image_grad: float32 [16, 32, 32, 384], P('imgs', 'rows')
- conv1_new: float32 [3456, 192], P('rows')
- conv1_moment: float32 [3456, 192], P('rows')
- conv1_square: float32 [3456, 192], P('rows')
- conv2_new: float32 [1728, 192], P('rows')
- conv2_moment: float32 [1728, 192], P('rows')
- conv2_square: float32 [1728, 192], P('rows')
- skip_new: float32 [384, 192], P('rows')
- skip_moment: float32 [384, 192], P('rows')
- skip_square: float32 [384, 192], P('rows')
- cond_new: float32 [148, 1152], P(None, 'rows')
- cond_moment: float32 [148, 1152], P(None, 'rows')
- cond_square: float32 [148, 1152], P(None, 'rows')
- bias_new: float32 [192], P('rows')
- bias_moment: float32 [192], P('rows')
- bias_square: float32 [192], P('rows')
The draws below stay inside these ranges and needn't reach their ends.
Inputs may be any that keep to these rules, and one draw needn't show every extreme that they name: Image group g holds live images in its first group_counts[g] slots; some group is full and some has the fewest. `conv1_second`: Positive. `conv2_second`: Positive. `skip_second`: Positive. `cond_second`: Positive. `bias_second`: Positive.
All inputs are finite; a program needn't handle non-finite values.
Results may differ from the reference program's by a relative error of at most 0.0015.
The reference program's roundings to bfloat16 on the way count: a program that leaves them out, or rounds other values in their place, can miss the bound.
Values may be sent and summed in bfloat16 or wider, within the bound.
No kernel may reach another device: no remote copies, remote signals or barrier semaphores. Data moves between devices by JAX's collectives and lax.ppermute only.
A program may use at most 128 MiB of HBM per device.

```python
import math
import jax
import jax.numpy as jnp
from jax import lax

C_IN = 384
C_OUT = 192
H = 64
STEP = 10
IMG_DEV = 4
COND = 148
H_IN = 32
TAPS_IN = 3456
TAPS_OUT = 1728
CW = 1152
GROUPS = 4
BATCH = 16


def grad_size(factor):
    return factor * math.sqrt(0.7 * BATCH * H * H)


def first_moment(key, shape, factor):
    values = jax.random.truncated_normal(key, -5.0, 5.0, shape, jnp.float32)
    return values * (0.11 * grad_size(factor))


def second_moment(key, shape, factor):
    spread = jax.random.uniform(key, shape, jnp.float32, math.log(0.5), math.log(2.0))
    return jnp.exp(spread) * (0.002 * grad_size(factor) * grad_size(factor))


def draw_image_in(key, part):
    shape = (BATCH, H_IN, H_IN, C_IN)
    heights = jnp.arange(H_IN, dtype=jnp.float32) / (H_IN - 1)
    image_scale = jnp.exp(jax.random.uniform(jax.random.fold_in(key, 3), (BATCH,), jnp.float32, math.log(0.7), math.log(1.4)))
    noise = jax.random.truncated_normal(jax.random.fold_in(key, 1), -5.0, 5.0, shape, jnp.float32)
    offset = jax.random.uniform(jax.random.fold_in(key, 2), (C_IN,), jnp.float32, -1.0, 1.0)
    ramp = 0.4 * jnp.power(10.0, heights)
    return ((noise + offset[None, None, None, :]) * ramp[None, :, None, None] * image_scale[:, None, None, None]).astype(jnp.bfloat16)


def draw_group_counts(key, part):
    fewest = max(1, IMG_DEV // 4)
    counts_drawn = jax.random.randint(jax.random.fold_in(key, 1), (GROUPS,), fewest, IMG_DEV + 1)
    picked = jax.random.permutation(jax.random.fold_in(key, 2), GROUPS)
    counts_drawn = counts_drawn.at[picked[0]].set(IMG_DEV)
    counts_drawn = counts_drawn.at[picked[1]].set(fewest)
    return counts_drawn.astype(jnp.int32)


def draw_conv1_first(key, part):
    return first_moment(key, (TAPS_IN, C_OUT), 0.6)


def draw_conv2_first(key, part):
    return first_moment(key, (TAPS_OUT, C_OUT), 0.6)


def draw_skip_first(key, part):
    return first_moment(key, (C_IN, C_OUT), 1.2)


def draw_cond_first(key, part):
    return first_moment(key, (COND, CW), 0.5)


def draw_bias_first(key, part):
    return first_moment(key, (C_OUT,), 1.0)


def draw_conv1_second(key, part):
    return second_moment(key, (TAPS_IN, C_OUT), 0.6)


def draw_conv2_second(key, part):
    return second_moment(key, (TAPS_OUT, C_OUT), 0.6)


def draw_skip_second(key, part):
    return second_moment(key, (C_IN, C_OUT), 1.2)


def draw_cond_second(key, part):
    return second_moment(key, (COND, CW), 0.5)


def draw_bias_second(key, part):
    return second_moment(key, (C_OUT,), 1.0)


def steps_of(stream_key, dims, split, smallest, high):
    def one(axis_at, shards_of):
        steps = jax.random.uniform(jax.random.fold_in(jax.random.fold_in(stream_key, 6), axis_at), (shards_of,), jnp.float32, smallest / len(split), high / len(split))
        return jnp.repeat(jnp.exp(steps), dims[axis_at] // shards_of).reshape((-1,) + (1,) * (len(dims) - axis_at - 1))

    gain = one(*split[0])
    for cut in split[1:]:
        gain = gain * one(*cut)
    return gain


def normal_values(key, shape, scale, limit, split=(), kind=jnp.bfloat16):
    gain = steps_of(key, shape, split, -0.22, 0.18) if split else 1.0
    values = jax.random.normal(key, shape, jnp.float32) * scale * gain
    return jnp.minimum(jnp.maximum(values, -limit), limit).astype(kind)


def setup_inputs(seed: int = 0) -> dict:
    seeds = jax.random.split(jax.random.key(seed), 21)
    return {
        "image_in": draw_image_in(jax.random.fold_in(seeds[20], 71), 0),
        "condition": normal_values(seeds[1], (BATCH, COND), 1.0, 5.0, ((0, 4),)),
        "group_counts": draw_group_counts(jax.random.fold_in(seeds[20], 71), 0),
        "out_cotangent": normal_values(seeds[3], (BATCH, H, H, C_OUT), 1.0, 6.0, ((0, 4), (1, 8))),
        "power_vectors": normal_values(seeds[4], (3, C_OUT), 1.0, 5.0, (), jnp.float32),
        "conv1_weight": normal_values(seeds[5], (TAPS_IN, C_OUT), TAPS_IN ** -0.5, 0.109375, ((0, 8),), jnp.float32),
        "conv2_weight": normal_values(seeds[6], (TAPS_OUT, C_OUT), TAPS_OUT ** -0.5, 0.15625, ((0, 8),), jnp.float32),
        "skip_weight": normal_values(seeds[7], (C_IN, C_OUT), C_IN ** -0.5, 0.3125, ((0, 8),), jnp.float32),
        "cond_weight": normal_values(seeds[8], (COND, CW), (4 * COND) ** -0.5, 0.25, ((1, 8),), jnp.float32),
        "out_bias": normal_values(seeds[9], (C_OUT,), 0.3, 1.5, ((0, 8),), jnp.float32),
        "conv1_first": draw_conv1_first(jax.random.fold_in(seeds[20], 71), 0),
        "conv2_first": draw_conv2_first(jax.random.fold_in(seeds[20], 71), 0),
        "skip_first": draw_skip_first(jax.random.fold_in(seeds[20], 71), 0),
        "cond_first": draw_cond_first(jax.random.fold_in(seeds[20], 71), 0),
        "bias_first": draw_bias_first(jax.random.fold_in(seeds[20], 71), 0),
        "conv1_second": draw_conv1_second(jax.random.fold_in(seeds[20], 71), 0),
        "conv2_second": draw_conv2_second(jax.random.fold_in(seeds[20], 71), 0),
        "skip_second": draw_skip_second(jax.random.fold_in(seeds[20], 71), 0),
        "cond_second": draw_cond_second(jax.random.fold_in(seeds[20], 71), 0),
        "bias_second": draw_bias_second(jax.random.fold_in(seeds[20], 71), 0),
    }


@jax.custom_vjp
def low(v):
    return lax.optimization_barrier(v.astype(jnp.bfloat16)).astype(jnp.float32)

@jax.custom_vjp
def low_back(v):
    return v

def low_keep(v):
    return (low(v), None)

def low_pass(kept, grad):
    return (grad,)

def back_keep(v):
    return (v, None)

def back_low(kept, grad):
    return (low(grad),)
low.defvjp(low_keep, low_pass)
low_back.defvjp(back_keep, back_low)
precise = lax.Precision.HIGHEST
NORM_EPS = 1e-05
BETA_ONE = 0.9
BETA_TWO = 0.999
ADAM_EPS = 1e-08
DECAY_RATE = 0.01
LEARN_RATES = (0.02, 0.02, 0.05, 0.03, 0.15)

def upsample(values):
    return jnp.repeat(jnp.repeat(values, 2, axis=1), 2, axis=2)

def convolve(values, kernel):
    return lax.conv_general_dilated(values, kernel, (1, 1), 'SAME', dimension_numbers=('NHWC', 'HWIO', 'NHWC'), precision=precise)

def power_outer(weight_low, vector):
    column = jnp.dot(weight_low, vector, precision=precise)
    left_vec = column * lax.rsqrt(jnp.sum(column * column))
    row_vec = jnp.dot(left_vec, weight_low, precision=precise)
    right_vec = row_vec * lax.rsqrt(jnp.sum(row_vec * row_vec))
    return jnp.outer(left_vec, right_vec)

def batch_norm(values, live_mask, count_all, scales, shifts):
    mean_val = lax.optimization_barrier(jnp.sum(live_mask * values, axis=(0, 1, 2))) / count_all
    square_val = lax.optimization_barrier(jnp.sum(live_mask * values * values, axis=(0, 1, 2))) / count_all
    rstd_val = lax.rsqrt(square_val - mean_val * mean_val + NORM_EPS)
    normed = (values - mean_val) * rstd_val
    return jax.nn.silu(scales[:, None, None, :] * normed + shifts[:, None, None, :])

def adamw(weight, first_old, second, gradient, learn_rate):
    first_new = BETA_ONE * first_old + (1.0 - BETA_ONE) * gradient
    second_new = BETA_TWO * second + (1.0 - BETA_TWO) * gradient * gradient
    first_hat = first_new / (1.0 - BETA_ONE ** STEP)
    second_hat = second_new / (1.0 - BETA_TWO ** STEP)
    weight_new = weight - learn_rate * (first_hat / (jnp.sqrt(second_hat) + ADAM_EPS) + DECAY_RATE * weight)
    return (weight_new, first_new, second_new)

def reference(image_in, condition, group_counts, out_cotangent, power_vectors, conv1_weight, conv2_weight, skip_weight, cond_weight, out_bias, conv1_first, conv2_first, skip_first, cond_first, bias_first, conv1_second, conv2_second, skip_second, cond_second, bias_second):
    slot_ids = jnp.arange(BATCH)
    owners = slot_ids // IMG_DEV
    live_mask = (slot_ids % IMG_DEV < group_counts[owners]).astype(jnp.float32)[:, None, None, None]
    total_live = jnp.sum(group_counts).astype(jnp.float32)
    count_low = total_live * (H_IN * H_IN)
    count_high = total_live * (H * H)
    cond_vals = condition.astype(jnp.float32)
    cotangent = out_cotangent.astype(jnp.float32) * live_mask
    outer_one = power_outer(low(conv1_weight), power_vectors[0])
    outer_two = power_outer(low(conv2_weight), power_vectors[1])
    outer_skip = power_outer(low(skip_weight), power_vectors[2])

    def forward(weight_one, weight_two, weight_skip, weight_cond, bias_vec, images):
        low_one = low(weight_one)
        low_two = low(weight_two)
        low_skip = low(weight_skip)
        sigma_one = jnp.sum(low_one * outer_one)
        sigma_two = jnp.sum(low_two * outer_two)
        sigma_skip = jnp.sum(low_skip * outer_skip)
        projected = jnp.dot(cond_vals, low(weight_cond), precision=precise)
        act_one = low(batch_norm(images, live_mask, count_low, 1.0 + projected[:, :C_IN], projected[:, C_IN:2 * C_IN]))
        hidden = low_back(convolve(upsample(act_one), low_one.reshape(3, 3, C_IN, C_OUT))) * (1.0 / sigma_one)
        act_two = low(batch_norm(hidden, live_mask, count_high, 1.0 + projected[:, 2 * C_IN:2 * C_IN + C_OUT], projected[:, 2 * C_IN + C_OUT:]))
        branch = low_back(convolve(act_two, low_two.reshape(3, 3, C_OUT, C_OUT))) * (1.0 / sigma_two)
        skip_raw = low_back(jnp.einsum('brwc,co->brwo', images, low_skip, precision=precise))
        return branch + upsample(skip_raw * (1.0 / sigma_skip)) + low(bias_vec)
    result, pullback = jax.vjp(forward, conv1_weight, conv2_weight, skip_weight, cond_weight, out_bias, image_in.astype(jnp.float32))
    grad_one, grad_two, grad_skip, grad_cond, grad_bias, image_grad = pullback(cotangent)
    one_new = adamw(conv1_weight, conv1_first, conv1_second, grad_one, LEARN_RATES[0])
    two_new = adamw(conv2_weight, conv2_first, conv2_second, grad_two, LEARN_RATES[1])
    skip_new = adamw(skip_weight, skip_first, skip_second, grad_skip, LEARN_RATES[2])
    cond_new = adamw(cond_weight, cond_first, cond_second, grad_cond, LEARN_RATES[3])
    bias_new = adamw(out_bias, bias_first, bias_second, grad_bias, LEARN_RATES[4])
    return (result.astype(jnp.bfloat16), image_grad, one_new[0], one_new[1], one_new[2], two_new[0], two_new[1], two_new[2], skip_new[0], skip_new[1], skip_new[2], cond_new[0], cond_new[1], cond_new[2], bias_new[0], bias_new[1], bias_new[2])
```

```python
import jax
import jax.numpy as jnp
import numpy as np
from jax import lax
from jax.sharding import Mesh
from jax.sharding import PartitionSpec as P

STEP = 10
precise = lax.Precision.HIGHEST
NORM_EPS = 1e-05
BETA_ONE = 0.9
BETA_TWO = 0.999
ADAM_EPS = 1e-08
DECAY_RATE = 0.01
LEARN_RATES = (0.02, 0.02, 0.05, 0.03, 0.15)
ALL = ("rows", "x", "core")


def upsample(values):
    return jnp.repeat(jnp.repeat(values, 2, axis=1), 2, axis=2)


def pool_pairs(values):
    shape = values.shape
    return jnp.sum(
        values.reshape(shape[0], shape[1] // 2, 2, shape[2] // 2, 2, shape[3]), axis=(2, 4)
    )


def conv_rows(halo_in, kernel):
    return lax.conv_general_dilated(
        halo_in,
        kernel,
        (1, 1),
        ((0, 0), (1, 1)),
        dimension_numbers=("NHWC", "HWIO", "NHWC"),
        preferred_element_type=jnp.float32,
    )


def flipped(kernel):
    return jnp.transpose(jnp.flip(kernel, (0, 1)), (0, 1, 3, 2))


def silu_slope(values):
    sigmoid_val = jax.nn.sigmoid(values)
    return sigmoid_val * (1.0 + values * (1.0 - sigmoid_val))


def tap_grads(halo_in, grad_out):
    padded = jnp.pad(halo_in, ((0, 0), (0, 0), (1, 1), (0, 0)))
    height = grad_out.shape[1]
    width_out = grad_out.shape[2]
    tap_parts = [
        jnp.einsum(
            "irwc,irwo->co",
            padded[:, tap_row : tap_row + height, tap_col : tap_col + width_out],
            grad_out,
            preferred_element_type=jnp.float32,
        )
        for tap_row in range(3)
        for tap_col in range(3)
    ]
    return jnp.concatenate(tap_parts, axis=0)


def adamw(weight, first_old, second, gradient, learn_rate):
    first_new = BETA_ONE * first_old + (1.0 - BETA_ONE) * gradient
    second_new = BETA_TWO * second + (1.0 - BETA_TWO) * gradient * gradient
    first_hat = first_new / (1.0 - BETA_ONE**STEP)
    second_hat = second_new / (1.0 - BETA_TWO**STEP)
    weight_new = weight - learn_rate * (
        first_hat / (jnp.sqrt(second_hat) + ADAM_EPS) + DECAY_RATE * weight
    )
    return (weight_new, first_new, second_new)


def swap_rows(first, last, row_pos):
    devices = lax.axis_size("rows")
    even = row_pos % 2 == 0
    near = [(i, i ^ 1) for i in range(devices)]
    far = [(i, i + 1) for i in range(1, devices - 1, 2)] + [
        (i + 1, i) for i in range(1, devices - 1, 2)
    ]
    got_near = lax.ppermute(jnp.where(even, last, first), "rows", near)
    got_far = lax.ppermute(jnp.where(even, first, last), "rows", far)
    return jnp.where(even, got_far, got_near), jnp.where(even, got_near, got_far)


def share(chunks):
    got = lax.all_to_all(chunks[:, None, :], ALL, 0, 0)
    return got[:, 0, :]


def share_same(vector):
    devices = lax.axis_size(ALL)
    return share(jnp.broadcast_to(vector[None, :], (devices, vector.shape[0])))


def core_swap(values):
    return lax.ppermute(values, "core", [(0, 1), (1, 0)])


def gather_weight(weight):
    devices = lax.axis_size("rows")
    low = weight.astype(jnp.bfloat16)
    count, width = low.shape
    core = lax.axis_index("core")
    half = lax.dynamic_slice_in_dim(low, core * (count // 2), count // 2, 0)
    mine = lax.all_to_all(
        jnp.broadcast_to(half[None], (devices, count // 2, width)), "rows", 0, 0
    )
    other = core_swap(mine)
    pair = jnp.where(
        core == 0,
        jnp.stack([mine, other], axis=1),
        jnp.stack([other, mine], axis=1),
    )
    return pair.reshape(devices * count, width)


def scatter_sum(grads):
    devices, count, width = grads.shape
    n_x = lax.axis_size("x")
    core = lax.axis_index("core")
    half = count // 2
    halves = grads.reshape(devices, 2, half, width)
    mine = lax.dynamic_index_in_dim(halves, core, 1, keepdims=False)
    other = lax.dynamic_index_in_dim(halves, 1 - core, 1, keepdims=False)
    held = mine + core_swap(other)
    part = -(-half // n_x)
    held = jnp.pad(held, ((0, 0), (0, part * n_x - half), (0, 0)))
    got = lax.all_to_all(held.reshape(devices * n_x, part, width), ("rows", "x"), 0, 0)
    total = jnp.sum(got, axis=0)
    whole = lax.all_gather(total, ("core", "x"), axis=0, tiled=True)
    return whole.reshape(2, part * n_x, width)[:, :half].reshape(count, width)


def power_parts(weight, vector):
    low = weight.astype(jnp.bfloat16).astype(jnp.float32)
    column = jnp.sum(low * vector[None, :], axis=1)
    return column, jnp.sum(column[:, None] * low, axis=0), jnp.sum(column * column)


def body(
    image_in,
    condition,
    group_counts,
    out_cotangent,
    power_vectors,
    conv1_weight,
    conv2_weight,
    skip_weight,
    cond_weight,
    out_bias,
    conv1_first,
    conv2_first,
    skip_first,
    cond_first,
    bias_first,
    conv1_second,
    conv2_second,
    skip_second,
    cond_second,
    bias_second,
):
    rows_n = lax.axis_size("rows")
    groups_n = lax.axis_size("x") * lax.axis_size("core")
    row_pos = lax.axis_index("rows")
    group_pos = lax.axis_index(("x", "core"))
    images_n, low_rows, width_in, chan_in = image_in.shape
    chan_out = out_cotangent.shape[3]
    width_out = 2 * width_in
    f32 = jnp.float32

    own_count = jnp.sum(jnp.where(jnp.arange(groups_n) == group_pos, group_counts, 0))
    live_mask = (jnp.arange(images_n) < own_count).astype(f32)[:, None, None, None]
    total_live = jnp.sum(group_counts).astype(f32)
    count_low = total_live * (width_in * width_in)
    count_high = total_live * (width_out * width_out)

    before_img, after_img = swap_rows(image_in[:, :1], image_in[:, -1:], row_pos)
    before_cot, after_cot = swap_rows(out_cotangent[:, :2], out_cotangent[:, -2:], row_pos)

    images = image_in.astype(f32)
    left_one, row_one, norm_one = power_parts(conv1_weight, power_vectors[0])
    left_two, row_two, norm_two = power_parts(conv2_weight, power_vectors[1])
    left_skip, row_skip, norm_skip = power_parts(skip_weight, power_vectors[2])
    proj_cols = jnp.dot(
        condition, cond_weight.astype(jnp.bfloat16), preferred_element_type=f32
    )
    cols = proj_cols.shape[1]
    gathered = share_same(
        jnp.concatenate(
            [
                jnp.sum(live_mask * images, axis=(0, 1, 2)),
                jnp.sum(live_mask * images * images, axis=(0, 1, 2)),
                row_one,
                row_two,
                row_skip,
                jnp.stack([norm_one, norm_two, norm_skip]),
                out_bias.astype(jnp.bfloat16).astype(f32),
                proj_cols.reshape(-1),
            ]
        )
    )
    sums = jnp.sum(gathered[:, : 2 * chan_in], axis=0)
    group_rows = lax.dynamic_index_in_dim(
        gathered.reshape(rows_n, groups_n, -1), group_pos, 1, keepdims=False
    )
    spectral = jnp.sum(
        group_rows[:, 2 * chan_in : 2 * chan_in + 3 * chan_out + 3], axis=0
    )
    at = 2 * chan_in + 3 * chan_out + 3
    bias_n = out_bias.shape[0]
    low_bias = group_rows[:, at : at + bias_n].reshape(-1)
    projected = jnp.transpose(
        group_rows[:, at + bias_n :].reshape(rows_n, images_n, cols), (1, 0, 2)
    ).reshape(images_n, rows_n * cols)

    def spectral_of(k, left):
        row = spectral[k * chan_out : (k + 1) * chan_out]
        inv_norm = lax.rsqrt(spectral[3 * chan_out + k])
        row = row * inv_norm
        inv_sigma = lax.rsqrt(jnp.sum(row * row))
        return left * inv_norm, row * inv_sigma, inv_sigma

    left_one, right_one, inv_one = spectral_of(0, left_one)
    left_two, right_two, inv_two = spectral_of(1, left_two)
    left_skip, right_skip, inv_skip = spectral_of(2, left_skip)

    low_one = gather_weight(conv1_weight)
    low_two = gather_weight(conv2_weight)
    low_skip = gather_weight(skip_weight)
    kernel_one = low_one.reshape(3, 3, chan_in, chan_out)
    kernel_two = low_two.reshape(3, 3, chan_out, chan_out)

    gain_one = 1.0 + projected[:, :chan_in]
    shift_one = projected[:, chan_in : 2 * chan_in]
    gain_two = 1.0 + projected[:, 2 * chan_in : 2 * chan_in + chan_out]
    shift_two = projected[:, 2 * chan_in + chan_out :]

    def valid(rows, halo):
        pos = jnp.arange(rows + 2 * halo) - halo + row_pos * rows
        return ((pos >= 0) & (pos < rows * rows_n))[None, :, None, None]

    mean_one = sums[:chan_in] / count_low
    rstd_one = lax.rsqrt(sums[chan_in:] / count_low - mean_one * mean_one + NORM_EPS)
    images_ext = jnp.concatenate([before_img, image_in, after_img], axis=1).astype(f32)
    normed_ext = (images_ext - mean_one) * rstd_one
    pre_ext = gain_one[:, None, None, :] * normed_ext + shift_one[:, None, None, :]
    act_one = jnp.where(valid(low_rows, 1), jax.nn.silu(pre_ext), 0.0).astype(jnp.bfloat16)
    normed_one = normed_ext[:, 1:-1]
    pre_one = pre_ext[:, 1:-1]
    up_ext = upsample(act_one)
    hidden_raw = conv_rows(up_ext, kernel_one)
    hidden = hidden_raw * inv_one
    own = hidden[:, 1:-1]
    gathered = share_same(
        jnp.concatenate(
            [
                jnp.sum(live_mask * own, axis=(0, 1, 2)),
                jnp.sum(live_mask * own * own, axis=(0, 1, 2)),
                condition.astype(f32).reshape(-1),
            ]
        )
    )
    sums = jnp.sum(gathered[:, : 2 * chan_out], axis=0)
    condition_all = gathered[:groups_n, 2 * chan_out :].reshape(
        groups_n * images_n, condition.shape[1]
    )
    mean_two = sums[:chan_out] / count_high
    rstd_two = lax.rsqrt(sums[chan_out:] / count_high - mean_two * mean_two + NORM_EPS)
    normed_two = (hidden - mean_two) * rstd_two
    pre_two = gain_two[:, None, None, :] * normed_two + shift_two[:, None, None, :]
    row_valid = valid(2 * low_rows, 1)
    act_two = jnp.where(row_valid, jax.nn.silu(pre_two), 0.0).astype(jnp.bfloat16)

    cot_ext = (
        jnp.concatenate([before_cot, out_cotangent, after_cot], axis=1).astype(f32) * live_mask
    )
    cotangent = cot_ext[:, 2:-2]
    branch_ext = (cot_ext * inv_two).astype(jnp.bfloat16)
    grad_branch = branch_ext[:, 2:-2]
    actgrad_two = conv_rows(branch_ext, flipped(kernel_two))
    pregrad_two = actgrad_two * silu_slope(pre_two)
    normgrad_two = gain_two[:, None, None, :] * pregrad_two
    own_grad = normgrad_two[:, 1:-1]
    grad_bias = jnp.sum(cotangent, axis=(0, 1, 2))
    gathered = share_same(
        jnp.concatenate(
            [
                jnp.sum(own_grad, axis=(0, 1, 2)),
                jnp.sum(own_grad * normed_two[:, 1:-1], axis=(0, 1, 2)),
                grad_bias,
            ]
        )
    )
    sums = jnp.sum(gathered, axis=0)
    total_two = sums[:chan_out]
    cross_two = sums[chan_out : 2 * chan_out]
    grad_bias = lax.dynamic_slice_in_dim(sums, 2 * chan_out + row_pos * bias_n, bias_n, 0)

    pooled = pool_pairs(cotangent)
    grad_skip = (pooled * inv_skip).astype(jnp.bfloat16)
    skip_raw = jnp.einsum("irwc,co->irwo", image_in, low_skip, preferred_element_type=f32)
    branch_raw = conv_rows(act_two, kernel_two)
    out_image = (
        branch_raw * inv_two + upsample(skip_raw * inv_skip) + low_bias
    ).astype(jnp.bfloat16)
    scale_two = jnp.sum(cotangent * branch_raw)
    scale_skip = jnp.sum(pooled * skip_raw)

    grad_two = tap_grads(act_two, grad_branch)
    grad_skip_w = jnp.einsum("irwc,irwo->co", image_in, grad_skip, preferred_element_type=f32)
    rows_two = conv2_weight.shape[0]
    rows_skip = skip_weight.shape[0]
    total_grads = scatter_sum(
        jnp.concatenate(
            [
                grad_two.reshape(rows_n, rows_two, chan_out),
                grad_skip_w.reshape(rows_n, rows_skip, chan_out),
            ],
            axis=1,
        )
    )

    hidden_grad = jnp.where(
        row_valid,
        live_mask
        * rstd_two
        * (normgrad_two - total_two / count_high - normed_two * (cross_two / count_high)),
        0.0,
    )
    hidgrad_raw = (hidden_grad * inv_one).astype(jnp.bfloat16)
    scale_one = jnp.sum(hidden_grad[:, 1:-1] * hidden_raw[:, 1:-1])
    grad_one = tap_grads(up_ext[:, 1:-1], hidgrad_raw[:, 1:-1])
    rows_one = conv1_weight.shape[0]
    total_one_w = scatter_sum(grad_one.reshape(rows_n, rows_one, chan_out))

    actgrad_one = pool_pairs(conv_rows(hidgrad_raw, flipped(kernel_one)))
    pregrad_one = actgrad_one * silu_slope(pre_one)
    normgrad_one = gain_one[:, None, None, :] * pregrad_one
    image_terms = jnp.concatenate(
        [
            jnp.sum(pregrad_one * normed_one, axis=(1, 2)),
            jnp.sum(pregrad_one, axis=(1, 2)),
            jnp.sum(pregrad_two[:, 1:-1] * normed_two[:, 1:-1], axis=(1, 2)),
            jnp.sum(pregrad_two[:, 1:-1], axis=(1, 2)),
        ],
        axis=1,
    )
    common = jnp.concatenate(
        [
            jnp.sum(normgrad_one, axis=(0, 1, 2)),
            jnp.sum(normgrad_one * normed_one, axis=(0, 1, 2)),
            jnp.stack([scale_one, scale_two, scale_skip]),
        ]
    )
    terms = jnp.transpose(image_terms.reshape(images_n, rows_n, cols), (1, 0, 2))
    chunks = jnp.concatenate(
        [
            jnp.broadcast_to(common[None], (rows_n, common.shape[0])),
            terms.reshape(rows_n, images_n * cols),
        ],
        axis=1,
    )
    gathered = share(jnp.repeat(chunks, groups_n, axis=0))
    size = common.shape[0]
    sums = jnp.sum(gathered[:, :size], axis=0)
    total_one = sums[:chan_in]
    cross_one = sums[chan_in : 2 * chan_in]
    scale_one_all, scale_two_all, scale_skip_all = sums[-3], sums[-2], sums[-1]
    terms = jnp.sum(gathered[:, size:].reshape(rows_n, groups_n * images_n, cols), axis=0)
    grad_cond = jnp.dot(condition_all.T, terms, precision=precise)

    image_grad = live_mask * rstd_one * (
        normgrad_one - total_one / count_low - normed_one * (cross_one / count_low)
    ) + jnp.einsum("irwo,co->irwc", grad_skip, low_skip, preferred_element_type=f32)

    fixed_one = total_one_w - scale_one_all * inv_one * inv_one * jnp.outer(left_one, right_one)
    fixed_two = total_grads[:rows_two] - scale_two_all * inv_two * inv_two * jnp.outer(
        left_two, right_two
    )
    fixed_skip = total_grads[rows_two:] - scale_skip_all * inv_skip * inv_skip * jnp.outer(
        left_skip, right_skip
    )
    one_new = adamw(conv1_weight, conv1_first, conv1_second, fixed_one, LEARN_RATES[0])
    two_new = adamw(conv2_weight, conv2_first, conv2_second, fixed_two, LEARN_RATES[1])
    skip_new = adamw(skip_weight, skip_first, skip_second, fixed_skip, LEARN_RATES[2])
    cond_new = adamw(cond_weight, cond_first, cond_second, grad_cond, LEARN_RATES[3])
    bias_new = adamw(out_bias, bias_first, bias_second, grad_bias, LEARN_RATES[4])
    return (out_image, image_grad, *one_new, *two_new, *skip_new, *cond_new, *bias_new)


def solution(mesh):
    rows_n, imgs_n = mesh.devices.shape
    fine = Mesh(np.asarray(mesh.devices).reshape(rows_n, imgs_n // 2, 2), ALL)
    groups = ("x", "core")
    picture = P(groups, "rows", None, None)
    weight = P("rows", None)
    column = P(None, "rows")
    masters = (weight, weight, weight, column, P("rows"))
    return jax.shard_map(
        body,
        mesh=fine,
        in_specs=(picture, P(groups, None), P(), picture, P(), *masters, *masters, *masters),
        out_specs=(
            picture,
            picture,
            *(weight,) * 9,
            *(column,) * 3,
            *(P("rows"),) * 3,
        ),
        check_vma=False,
    )
```

```python
import functools

import jax
import jax.numpy as jnp
import numpy as np
from jax import lax
from jax.experimental import pallas as pl
from jax.experimental.pallas import tpu as pltpu
from jax.sharding import Mesh
from jax.sharding import PartitionSpec as P

STEP = 10
precise = lax.Precision.HIGHEST
NORM_EPS = 1e-05
BETA_ONE = 0.9
BETA_TWO = 0.999
ADAM_EPS = 1e-08
DECAY_RATE = 0.01
LEARN_RATES = (0.02, 0.02, 0.05, 0.03, 0.15)
ALL = ("rows", "x", "core")
F32, BF16 = jnp.float32, jnp.bfloat16
LANES = 128
VMEM_LIMIT = 40 * 2**20


def shape(dims, kind=F32):
    return jax.ShapeDtypeStruct(tuple(dims), kind)


def run(kernel, outs, args, scratch=(), scalars=1, flops=0, limit=VMEM_LIMIT):
    spec = pl.BlockSpec(memory_space=pltpu.VMEM)
    specs = [pl.BlockSpec(memory_space=pltpu.SMEM)] * scalars + [spec] * (len(args) - scalars)
    moved = sum(a.size * a.dtype.itemsize for a in args)
    moved += sum(np.prod(o.shape) * np.dtype(o.dtype).itemsize for o in outs)
    return pl.pallas_call(
        kernel,
        out_shape=tuple(outs),
        in_specs=specs,
        out_specs=tuple(spec for _ in outs),
        scratch_shapes=scratch,
        cost_estimate=pl.CostEstimate(
            flops=int(flops), bytes_accessed=int(moved), transcendentals=0
        ),
        compiler_params=pltpu.CompilerParams(vmem_limit_bytes=limit),
    )(*args)


def round_up(value, step):
    return -(-value // step) * step


class Sizes:
    def __init__(self, image, cot, condition, masters, rows_n, groups_n):
        self.images, self.rows, self.width, self.chan = image
        self.out = cot[3]
        self.slot = round_up(self.out, LANES)
        self.ext = 2 * self.rows + 2
        self.cond = condition[1]
        self.n_one, self.n_two, self.n_skip = masters[0][0], masters[1][0], masters[2][0]
        self.cols = masters[3][1]
        self.n_bias = masters[4][0]
        self.rows_n, self.groups = rows_n, groups_n
        self.devices = rows_n * groups_n
        self.h_one = round_up(-(-self.n_one // 2), 8)
        self.h_two = round_up(-(-self.n_two // 2), 8)
        self.h_skip = round_up(-(-self.n_skip // 2), 8)
        self.at_power = 2 * self.chan
        self.at_norm = self.at_power + 3 * self.slot
        self.at_bias = self.at_norm + 8
        self.at_proj = round_up(self.at_bias + self.n_bias, LANES)
        self.pay_one = round_up(self.at_proj + self.images * self.cols, LANES)
        self.at_cond = 2 * self.slot
        self.pay_two = round_up(self.at_cond + self.images * self.cond, LANES)
        self.pay_three = 3 * self.slot
        self.at_scale = 2 * self.chan
        self.at_terms = self.at_scale + LANES
        self.pay_four = round_up(self.at_terms + self.images * self.cols, LANES)
        self.edge = 3 * self.width + 2 * 2 * self.width * (1 + 1)


def position():
    return lax.axis_index("rows"), lax.axis_index("x"), lax.axis_index("core")


def group_position():
    return lax.axis_index("x") * lax.axis_size("core") + lax.axis_index("core")


def live_of(counts, image):
    return jnp.where(image < counts[group_position()], 1.0, 0.0).astype(F32)


def live_total(counts, sizes):
    total = counts[0]
    for g in range(1, sizes.groups):
        total = total + counts[g]
    return total.astype(F32)


def inside(row, sizes, scale):
    at = lax.axis_index("rows") * (scale * sizes.rows) + row
    return jnp.where((at >= 0) & (at < scale * sizes.rows * sizes.rows_n), 1.0, 0.0).astype(F32)


def sigmoid(values):
    return 1.0 / (1.0 + jnp.exp(-values))


def shifted(values, step):
    width = values.shape[0]
    rolled = pltpu.roll(values, (-step) % width, 0)
    where = lax.broadcasted_iota(jnp.int32, values.shape, 0)
    edge = 0 if step < 0 else width - 1
    return jnp.where(where == edge, 0.0, rolled)


def dot(a, b, dims=((1,), (0,)), precision=None):
    return lax.dot_general(a, b, (dims, ((), ())), preferred_element_type=F32, precision=precision)


def prep_kernel(sizes, counts, image, cot, cond, vec, vec_t, one_t, two_t, skip, cond_t, bias,
                pay, half_one, half_two, near, far, left_one, left_two, left_skip, line):
    s = sizes
    row_pos, _, core = position()
    even = lax.rem(row_pos, 2) == 0
    last, w = s.rows - 1, s.width

    def edges(ref, low_row, high_row):
        for t in range(3):
            ref[:, t * w : (t + 1) * w, :] = image[:, low_row, :, t * LANES : (t + 1) * LANES]
        at = 3 * w
        for k in range(2):
            ref[:, at : at + 2 * w, :] = cot[:, high_row + k, :, :LANES]
            at += 2 * w
        for k in range(2):
            ref[:, at : at + 2 * w, : s.out - LANES] = cot[:, high_row + k, :, LANES:]
            at += 2 * w

    @pl.when(even)
    def _():
        edges(near, last, 2 * s.rows - 2)
        edges(far, 0, 0)

    @pl.when(jnp.logical_not(even))
    def _():
        edges(near, 0, 0)
        edges(far, last, 2 * s.rows - 2)

    line[...] = jnp.zeros_like(line)
    sums = jnp.zeros((8, s.chan), F32)
    squares = jnp.zeros((8, s.chan), F32)
    for b in range(s.images):
        part = jnp.zeros((8, s.chan), F32)
        part_sq = jnp.zeros((8, s.chan), F32)
        for i in range(s.rows):
            x = image[b, i].astype(F32).reshape(w // 8, 8, s.chan)
            part += jnp.sum(x, axis=0)
            part_sq += jnp.sum(x * x, axis=0)
        sums += part * live_of(counts, b)
        squares += part_sq * live_of(counts, b)
    line[0:1, : s.chan] = jnp.sum(sums, axis=0, keepdims=True)
    line[0:1, s.chan : 2 * s.chan] = jnp.sum(squares, axis=0, keepdims=True)

    def power(k, low, left_row):
        column = jnp.sum(low * vec[k : k + 1, :], axis=1, keepdims=True)
        row = jnp.sum(low * column, axis=0, keepdims=True)
        at = s.at_power + k * s.slot
        line[0:1, at : at + s.out] = row
        line[0:1, s.at_norm + k : s.at_norm + k + 1] = jnp.sum(column * column, axis=0, keepdims=True)
        return column

    low_t = one_t[...].astype(BF16).astype(F32)
    left_one[...] = jnp.sum(low_t * vec_t[:, 0:1], axis=0, keepdims=True)
    low = jnp.transpose(low_t)
    power(0, low, left_one)
    n, h = s.n_one, s.h_one
    half = jnp.where(core == 0, low[:h], low[n - h :]).astype(BF16)
    for r in range(s.rows_n):
        half_one[r] = half
    low_t = two_t[...].astype(BF16).astype(F32)
    left_two[...] = jnp.sum(low_t * vec_t[:, 1:2], axis=0, keepdims=True)
    low = jnp.transpose(low_t)
    power(1, low, left_two)
    n, h = s.n_two, s.h_two
    half_a = jnp.where(core == 0, low[:h], low[n - h :])
    low = skip[...].astype(BF16).astype(F32)
    left_skip[...] = power(2, low, None)
    n, h = s.n_skip, s.h_skip
    half_b = jnp.where(core == 0, low[:h], low[n - h :])
    half = jnp.concatenate([half_a, half_b], axis=0).astype(BF16)
    for r in range(s.rows_n):
        half_two[r] = half

    line[0:1, s.at_bias : s.at_bias + s.n_bias] = bias[...].astype(BF16).astype(F32)
    proj = dot(cond[...], cond_t[...].astype(BF16), ((1,), (1,)))
    for b in range(s.images):
        at = s.at_proj + b * s.cols
        line[0:1, at : at + s.cols] = proj[b : b + 1]
    whole = line[...]
    for d in range(s.devices):
        pay[d] = whole


def act_kernel(sizes, counts, got, image, near, far, slots, proj, stats, spec):
    s = sizes
    row_pos, _, _ = position()
    even = lax.rem(row_pos, 2) == 0
    group = group_position()
    sums = jnp.sum(got[:, :, : 2 * s.chan], axis=0)
    count = live_total(counts, s) * (s.width * s.width)
    mean = sums[:, : s.chan] / count
    rstd = lax.rsqrt(sums[:, s.chan :] / count - mean * mean + NORM_EPS)
    stats[0:1, :] = mean
    stats[1:2, :] = rstd

    spec[...] = jnp.zeros_like(spec)
    total = got[group, :, s.at_power : s.at_proj]
    for r in range(1, s.rows_n):
        total = total + got[r * s.groups + group, :, s.at_power : s.at_proj]
    for k in range(3):
        at = 3 * s.slot + k
        inv_norm = lax.rsqrt(total[:, at : at + 1])
        row = total[:, k * s.slot : k * s.slot + s.out] * inv_norm
        inv_sigma = lax.rsqrt(jnp.sum(row * row, axis=1, keepdims=True))
        spec[k : k + 1, : s.out] = row * inv_sigma
        spec[3 + k : 4 + k, :] = jnp.broadcast_to(inv_sigma, (1, s.slot))
        spec[8 + k : 9 + k, :] = jnp.broadcast_to(inv_norm, (1, s.slot))
    for r in range(s.rows_n):
        piece = got[r * s.groups + group, :, s.at_bias : s.at_bias + s.n_bias]
        spec[6:7, r * s.n_bias : (r + 1) * s.n_bias] = piece
        for b in range(s.images):
            at = s.at_proj + b * s.cols
            proj[b : b + 1, r * s.cols : (r + 1) * s.cols] = got[
                r * s.groups + group, :, at : at + s.cols
            ]

    w = s.width

    def one(b, e, x, keep):
        gain = 1.0 + proj[pl.ds(b, 1), : s.chan]
        shift = proj[pl.ds(b, 1), s.chan : 2 * s.chan]
        pre = gain * ((x - mean) * rstd) + shift
        act = pre * sigmoid(pre)
        if keep is not None:
            act = act * keep
        low = act.astype(BF16)
        slots[b, e, :, s.chan : 2 * s.chan] = low
        slots[b, e, :, 2 * s.chan : 3 * s.chan] = low
        slots[b, e, :, : s.chan] = shifted(act, -1).astype(BF16)
        slots[b, e, :, 3 * s.chan :] = shifted(act, 1).astype(BF16)

    def edge(ref, b):
        return jnp.concatenate(
            [ref[b, t * w : (t + 1) * w, :].astype(F32) for t in range(3)], axis=1
        )

    @pl.loop(0, s.images)
    def _(b):
        a, c = edge(near, b), edge(far, b)
        one(b, 0, jnp.where(even, c, a), inside(-1, s, 1))
        for i in range(s.rows):
            one(b, i + 1, image[b, i].astype(F32), None)
        one(b, s.rows + 1, jnp.where(even, a, c), inside(s.rows, s, 1))


def conv_one_kernel(sizes, counts, slots, mine, other, cond, hidden, weight, pay, line, wide):
    s = sizes
    _, _, core = position()
    first = core == 0
    for r in range(s.rows_n):
        a, b = mine[r].astype(F32), other[r].astype(F32)
        at = r * s.n_one
        wide[at : at + s.h_one, :] = jnp.where(first, a, b)
        at += s.n_one - s.h_one
        wide[at : at + s.h_one, :] = jnp.where(first, b, a)
    for t in range(9):
        weight[t * s.chan : (t + 1) * s.chan] = wide[t * s.chan : (t + 1) * s.chan, :].astype(BF16)
    depth = 3 * s.chan
    rows = s.rows + 1
    sums = jnp.zeros((8, s.out), F32)
    squares = jnp.zeros((8, s.out), F32)
    for phase in range(4):
        a, b = divmod(phase, 2)
        total = None
        for dy in range(3):
            start = (a + dy - 1) // 2 + 1 - a
            lhs = slots[:, start : start + rows, :, b * s.chan : b * s.chan + depth]
            part = dot(
                lhs.reshape(s.images * rows * s.width, depth),
                weight[dy * depth : (dy + 1) * depth, :],
            )
            total = part if total is None else total + part
        total = total.reshape(s.images, rows, s.width, s.out)
        for i in range(s.images):
            part = jnp.zeros((8, s.out), F32)
            part_sq = jnp.zeros((8, s.out), F32)
            for k in range(rows):
                e = 2 * k + 1 - a
                value = total[i, k]
                hidden[i, e, b] = value
                if 0 < e < s.ext - 1:
                    x = value.reshape(s.width // 8, 8, s.out)
                    part += jnp.sum(x, axis=0)
                    part_sq += jnp.sum(x * x, axis=0)
            sums += part * live_of(counts, i)
            squares += part_sq * live_of(counts, i)
    line[...] = jnp.zeros_like(line)
    line[0:1, : s.out] = jnp.sum(sums, axis=0, keepdims=True)
    line[0:1, s.slot : s.slot + s.out] = jnp.sum(squares, axis=0, keepdims=True)
    for i in range(s.images):
        at = s.at_cond + i * s.cond
        line[0:1, at : at + s.cond] = cond[i : i + 1, :].astype(F32)
    whole = line[...]
    for d in range(s.devices):
        pay[d] = whole


def cot_kernel(sizes, counts, cot, near, far, image, mine, other, spec, dact, phases, grad_low,
               grad_skip, skip_part, two, skip_w, misc, slots, wide, pair, flip):
    s = sizes
    row_pos, _, core = position()
    even = lax.rem(row_pos, 2) == 0
    first = core == 0
    w = s.width
    for r in range(s.rows_n):
        a, b = mine[r].astype(F32), other[r].astype(F32)
        lo, hi = jnp.where(first, a, b), jnp.where(first, b, a)
        at = r * s.n_two
        wide[at : at + s.h_two, :] = lo[: s.h_two]
        at += s.n_two - s.h_two
        wide[at : at + s.h_two, :] = hi[: s.h_two]
        at = 9 * s.out + r * s.n_skip
        wide[at : at + s.h_skip, :] = lo[s.h_two :]
        at += s.n_skip - s.h_skip
        wide[at : at + s.h_skip, :] = hi[s.h_two :]
    two[...] = jnp.zeros_like(two)
    flip[...] = jnp.zeros_like(flip)
    for t in range(9):
        dy, dx = divmod(t, 3)
        tap = wide[t * s.out : (t + 1) * s.out, :]
        two[dy, dx * s.slot : dx * s.slot + s.out, :] = tap.astype(BF16)
        back = jnp.transpose(tap).astype(BF16)
        flip[2 - dy, (2 - dx) * s.slot : (2 - dx) * s.slot + s.out, :] = back
    skip_w[...] = wide[9 * s.out : 9 * s.out + s.chan, :].astype(BF16)

    slots[...] = jnp.zeros_like(slots)
    inv_two = spec[4:5, : s.out]
    inv_skip = spec[5:6, : s.out]

    def split(b, q, row, own):
        pair[0] = row[:, :LANES]
        pair[1, :, : s.out - LANES] = row[:, LANES:]
        both = []
        for ph in range(2):
            value = jnp.concatenate(
                [pair[0, pl.ds(ph, w, 2), :], pair[1, pl.ds(ph, w, 2), :][:, : s.out - LANES]],
                axis=1,
            )
            low = (value * inv_two).astype(BF16)
            both.append(value)
            if own is not None:
                phases[b, own, ph] = value.astype(BF16)
                grad_low[b, own, ph] = low
            at = (1 + ph) * s.slot
            slots[b, q, :, at : at + s.out] = low
            if ph == 1:
                slots[b, q, :, : s.out] = shifted(low.astype(F32), -1).astype(BF16)
            else:
                slots[b, q, :, 3 * s.slot : 3 * s.slot + s.out] = shifted(
                    low.astype(F32), 1
                ).astype(BF16)
        return both[0] + both[1]

    def edge_row(ref, b, k):
        at = 3 * w + k * 2 * w
        return jnp.concatenate(
            [
                ref[b, at : at + 2 * w, :].astype(F32),
                ref[b, at + 4 * w : at + 6 * w, : s.out - LANES].astype(F32),
            ],
            axis=1,
        )

    misc[...] = jnp.zeros_like(misc)

    @pl.loop(0, s.images)
    def _(b):
        live = live_of(counts, b)
        above = inside(-1, s, 1) * live
        below = inside(s.rows, s, 1) * live
        for k in range(2):
            a, c = edge_row(near, b, k), edge_row(far, b, k)
            split(b, k, jnp.where(even, c, a) * above, None)
            split(b, 2 * s.rows + 2 + k, jnp.where(even, a, c) * below, None)
        bias = jnp.zeros((1, s.out), F32)
        skip_sum = jnp.zeros((1, s.out), F32)
        for i in range(s.rows):
            pooled = split(b, 2 * i + 2, cot[b, 2 * i].astype(F32) * live, 2 * i)
            pooled += split(b, 2 * i + 3, cot[b, 2 * i + 1].astype(F32) * live, 2 * i + 1)
            grad_skip[b, i] = (pooled * inv_skip).astype(BF16)
            bias += jnp.sum(pooled, axis=0, keepdims=True)
            raw = dot(image[b, i], skip_w[...])
            skip_part[b, i] = raw * inv_skip
            skip_sum += jnp.sum(pooled * raw, axis=0, keepdims=True)
        misc[0:1, : s.out] += bias
        misc[1:2, : s.out] += skip_sum

    depth = 3 * s.slot
    for ph in range(2):
        total = None
        for dy in range(3):
            lhs = slots[:, dy : dy + s.ext, :, ph * s.slot : ph * s.slot + depth]
            part = dot(lhs.reshape(s.images * s.ext * w, depth), flip[dy])
            total = part if total is None else total + part
        dact[:, :, ph] = total.reshape(s.images, s.ext, w, s.out)


def norm_two_kernel(sizes, counts, got, hidden, dact, spec, proj, misc, slots, dnorm, stats,
                    terms, pay, line):
    s = sizes
    w = s.width
    inv = spec[3:4, : s.out]
    sums = jnp.sum(got[:, :, : 2 * s.slot], axis=0)
    count = live_total(counts, s) * (4 * w * w)
    mean = sums[:, : s.out] * inv / count
    square = sums[:, s.slot : s.slot + s.out] * inv * inv / count
    rstd = lax.rsqrt(square - mean * mean + NORM_EPS)
    stats[0:1, : s.out] = mean
    stats[1:2, : s.out] = rstd
    scale = inv * rstd
    offset = mean * rstd
    slots[...] = jnp.zeros_like(slots)
    base = 2 * s.chan

    def one(b, e, keep):
        gain = 1.0 + proj[pl.ds(b, 1), base : base + s.out]
        shift = proj[pl.ds(b, 1), base + s.out : base + 2 * s.out]
        dsum = jnp.zeros((8, s.out), F32)
        dgain = jnp.zeros((8, s.out), F32)
        for ph in range(2):
            normed = hidden[b, e, ph] * scale - offset
            pre = gain * normed + shift
            sig = sigmoid(pre)
            act = pre * sig
            if keep is not None:
                act = act * keep
            at = (1 + ph) * s.slot
            slots[b, e, :, at : at + s.out] = act.astype(BF16)
            if ph == 1:
                slots[b, e, :, : s.out] = shifted(act, -1).astype(BF16)
            else:
                slots[b, e, :, 3 * s.slot : 3 * s.slot + s.out] = shifted(act, 1).astype(BF16)
            dpre = dact[b, e, ph] * (sig * (1.0 + pre * (1.0 - sig)))
            dnorm[b, e, ph] = gain * dpre
            if keep is None:
                dsum += jnp.sum(dpre.reshape(w // 8, 8, s.out), axis=0)
                dgain += jnp.sum((dpre * normed).reshape(w // 8, 8, s.out), axis=0)
        return dsum, dgain

    terms[...] = jnp.zeros_like(terms)

    @pl.loop(0, s.images)
    def _(b):
        one(b, 0, inside(-1, s, 2))
        dsum = jnp.zeros((8, s.out), F32)
        dgain = jnp.zeros((8, s.out), F32)
        for e in range(1, s.ext - 1):
            a, c = one(b, e, None)
            dsum += a
            dgain += c
        one(b, s.ext - 1, inside(2 * s.rows, s, 2))
        terms[pl.ds(b, 1), : s.out] = jnp.sum(dgain, axis=0, keepdims=True)
        terms[pl.ds(b, 1), s.out : 2 * s.out] = jnp.sum(dsum, axis=0, keepdims=True)

    total = jnp.zeros((1, s.out), F32)
    cross = jnp.zeros((1, s.out), F32)
    for b in range(s.images):
        gain = 1.0 + proj[b : b + 1, base : base + s.out]
        cross += gain * terms[b : b + 1, : s.out]
        total += gain * terms[b : b + 1, s.out : 2 * s.out]
    line[...] = jnp.zeros_like(line)
    line[0:1, : s.out] = total
    line[0:1, s.slot : s.slot + s.out] = cross
    line[0:1, 2 * s.slot : 2 * s.slot + s.out] = misc[0:1, : s.out]
    whole = line[...]
    for d in range(s.devices):
        pay[d] = whole


def conv_two_kernel(sizes, slots, two, phases, grad_low, grad_skip, skip_part, image, spec,
                    out, mine, other, scale, pair, grads):
    s = sizes
    _, _, core = position()
    w = s.width
    depth = 3 * s.slot
    own = 2 * s.rows
    inv_two = spec[4:5, : s.out]
    bias = spec[6:7, : s.out]
    dots = jnp.zeros((1, s.out), F32)
    results = []
    for ph in range(2):
        total = None
        for dy in range(3):
            lhs = slots[:, dy : dy + own, :, ph * s.slot : ph * s.slot + depth]
            part = dot(lhs.reshape(s.images * own * w, depth), two[dy])
            total = part if total is None else total + part
        results.append(total.reshape(s.images, own, w, s.out))
    for b in range(s.images):
        for e in range(own):
            for ph in range(2):
                raw = results[ph][b, e]
                dots += jnp.sum(raw * phases[b, e, ph].astype(F32), axis=0, keepdims=True)
                value = raw * inv_two + skip_part[b, e // 2] + bias
                pair[0, pl.ds(ph, w, 2), :] = value[:, :LANES]
                pair[1, pl.ds(ph, w, 2), :] = jnp.concatenate(
                    [value[:, LANES:], jnp.zeros((w, 2 * LANES - s.out), F32)], axis=1
                )
            out[b, e, :, :LANES] = pair[0].astype(BF16)
            out[b, e, :, LANES:] = pair[1][:, : s.out - LANES].astype(BF16)
    scale[...] = jnp.broadcast_to(jnp.sum(dots, axis=1, keepdims=True), scale.shape)

    count = s.images * own * w
    flips = [
        jnp.transpose(grad_low[:, :, ph].reshape(count, s.out)) for ph in range(2)
    ]
    for dy in range(3):
        total = None
        for ph in range(2):
            rhs = slots[:, dy : dy + own, :, ph * s.slot : ph * s.slot + depth]
            part = dot(flips[ph], rhs.reshape(count, depth))
            total = part if total is None else total + part
        for dx in range(3):
            at = (3 * dy + dx) * s.out
            grads[:, at : at + s.out] = total[:, dx * s.slot : dx * s.slot + s.out]
    count = s.images * s.rows * w
    flip = jnp.transpose(grad_skip[...].reshape(count, s.out))
    grads[:, 9 * s.out : 9 * s.out + s.chan] = dot(flip, image[...].reshape(count, s.chan))
    half = s.out // 2
    for ref, which in ((mine, core), (other, 1 - core)):
        at = pl.multiple_of(which * half, 8)
        for r in range(s.rows_n):
            start = r * s.n_two
            ref[r, :, : s.n_two] = grads[pl.ds(at, half), start : start + s.n_two]
            start = 9 * s.out + r * s.n_skip
            ref[r, :, s.n_two :] = grads[pl.ds(at, half), start : start + s.n_skip]


def hidden_grad_kernel(sizes, counts, got, dnorm, hidden, stats, spec, acts, slots, mine, other,
                       scale, bias_grad, low, grads):
    s = sizes
    _, _, core = position()
    w = s.width
    sums = jnp.sum(got[...], axis=0)
    count = live_total(counts, s) * (4 * w * w)
    mean, rstd = stats[0:1, : s.out], stats[1:2, : s.out]
    inv = spec[3:4, : s.out]
    total = sums[:, : s.out] / count
    cross = sums[:, s.slot : s.slot + s.out] / count
    bias_grad[...] = jnp.broadcast_to(sums[:, 2 * s.slot :], bias_grad.shape)
    slots[...] = jnp.zeros_like(slots)
    norm_scale = inv * rstd
    offset = mean * rstd

    def one(b, e, keep, own):
        par, k = e % 2, e // 2
        dots = jnp.zeros((8, s.out), F32)
        for ph in range(2):
            raw = hidden[b, e, ph]
            normed = raw * norm_scale - offset
            grad = keep * (rstd * (dnorm[b, e, ph] - total - normed * cross))
            if own:
                dots += jnp.sum((grad * raw).reshape(w // 8, 8, s.out), axis=0)
            value = grad * inv
            small = value.astype(BF16)
            at = (1 + ph) * s.slot
            slots[b, par, k, :, at : at + s.out] = small
            if own:
                low[1 - par, ph, b, (e - 1) // 2] = small
            if ph == 1:
                slots[b, par, k, :, : s.out] = shifted(value, -1).astype(BF16)
            else:
                slots[b, par, k, :, 3 * s.slot : 3 * s.slot + s.out] = shifted(value, 1).astype(
                    BF16
                )
        return dots

    scale[...] = jnp.zeros_like(scale)

    @pl.loop(0, s.images)
    def _(b):
        live = live_of(counts, b)
        one(b, 0, live * inside(-1, s, 2), False)
        dots = jnp.zeros((8, s.out), F32)
        for e in range(1, s.ext - 1):
            dots += one(b, e, live, True)
        one(b, s.ext - 1, live * inside(2 * s.rows, s, 2), False)
        scale[0:1, : s.out] += jnp.sum(dots, axis=0, keepdims=True)

    count = s.images * s.rows * w
    depth = 3 * s.chan
    for dy in range(3):
        total = None
        for phase in range(4):
            a, b = divmod(phase, 2)
            flip = jnp.transpose(low[a, b].reshape(count, s.out))
            start = 1 + (a + dy - 1) // 2
            rhs = acts[:, start : start + s.rows, :, b * s.chan : b * s.chan + depth]
            part = dot(flip, rhs.reshape(count, depth))
            total = part if total is None else total + part
        grads[:, dy * depth : (dy + 1) * depth] = total
    half = s.out // 2
    for ref, which in ((mine, core), (other, 1 - core)):
        at = pl.multiple_of(which * half, 8)
        for r in range(s.rows_n):
            start = r * s.n_one
            ref[r] = grads[pl.ds(at, half), start : start + s.n_one]


def input_grad_kernel(sizes, slots, weight, image, stats, proj, terms_two, scale_one, scale_two,
                      misc, dnorm, pay, back, terms, line):
    s = sizes
    w = s.width
    depth = 3 * s.slot
    back[...] = jnp.zeros_like(back)
    for t in range(9):
        dy, dx = divmod(t, 3)
        tap = weight[t * s.chan : (t + 1) * s.chan, :].astype(F32)
        at = (2 - dx) * s.slot
        back[dy, at : at + s.out, :] = jnp.transpose(tap).astype(BF16)
    total = None
    for a in range(2):
        for dy in range(3):
            par, k = (a + 2 - dy) % 2, (a + 2 - dy) // 2
            for ph in range(2):
                lhs = slots[:, par, k : k + s.rows, :, ph * s.slot : ph * s.slot + depth]
                part = dot(lhs.reshape(s.images * s.rows * w, depth), back[dy])
                total = part if total is None else total + part
    total = total.reshape(s.images, s.rows, w, s.chan)
    mean, rstd = stats[0:1, :], stats[1:2, :]
    all_sum = jnp.zeros((1, s.chan), F32)
    all_cross = jnp.zeros((1, s.chan), F32)
    for b in range(s.images):
        gain = 1.0 + proj[b : b + 1, : s.chan]
        shift = proj[b : b + 1, s.chan : 2 * s.chan]
        dsum = jnp.zeros((8, s.chan), F32)
        dgain = jnp.zeros((8, s.chan), F32)
        for i in range(s.rows):
            normed = (image[b, i].astype(F32) - mean) * rstd
            pre = gain * normed + shift
            sig = sigmoid(pre)
            dpre = total[b, i] * (sig * (1.0 + pre * (1.0 - sig)))
            dnorm[b, i] = gain * dpre
            dsum += jnp.sum(dpre.reshape(w // 8, 8, s.chan), axis=0)
            dgain += jnp.sum((dpre * normed).reshape(w // 8, 8, s.chan), axis=0)
        dsum = jnp.sum(dsum, axis=0, keepdims=True)
        dgain = jnp.sum(dgain, axis=0, keepdims=True)
        terms[b : b + 1, : s.chan] = dgain
        terms[b : b + 1, s.chan : 2 * s.chan] = dsum
        terms[b : b + 1, 2 * s.chan :] = terms_two[b : b + 1, : 2 * s.out]
        all_sum += gain * dsum
        all_cross += gain * dgain
    line[...] = jnp.zeros_like(line)
    line[0:1, : s.chan] = all_sum
    line[0:1, s.chan : 2 * s.chan] = all_cross
    at = s.at_scale
    line[0:1, at : at + 1] = jnp.sum(scale_one[0:1, : s.out], axis=1, keepdims=True)
    line[0:1, at + 1 : at + 2] = scale_two[0:1, 0:1]
    line[0:1, at + 2 : at + 3] = jnp.sum(misc[1:2, : s.out], axis=1, keepdims=True)
    for r in range(s.rows_n):
        for b in range(s.images):
            at = s.at_terms + b * s.cols
            line[0:1, at : at + s.cols] = terms[b : b + 1, r * s.cols : (r + 1) * s.cols]
        whole = line[...]
        for g in range(s.groups):
            pay[r * s.groups + g] = whole


def adamw(weight, first_old, second, gradient, learn_rate):
    first_new = BETA_ONE * first_old + (1.0 - BETA_ONE) * gradient
    second_new = BETA_TWO * second + (1.0 - BETA_TWO) * gradient * gradient
    first_hat = first_new / (1.0 - BETA_ONE**STEP)
    second_hat = second_new / (1.0 - BETA_TWO**STEP)
    weight_new = weight - learn_rate * (
        first_hat / (jnp.sqrt(second_hat) + ADAM_EPS) + DECAY_RATE * weight
    )
    return (weight_new, first_new, second_new)


def store_adamw(refs, olds, gradient, rate):
    for ref, value in zip(refs, adamw(*(old[...] for old in olds), gradient, rate)):
        ref[...] = value


def finish_kernel(sizes, counts, got, cond_got, bias_got, image, dnorm, grad_skip, skip_w, stats, proj,
                  cw, cm, cv, bw, bm, bv,
                  image_grad, cw_new, cm_new, cv_new, bw_new, bm_new, bv_new, scales, terms, conds):
    s = sizes
    w = s.width
    row_pos, _, _ = position()
    sums = jnp.sum(got[:, :, : s.at_terms], axis=0)
    scales[...] = jnp.broadcast_to(sums[:, s.at_scale :], scales.shape)
    count = live_total(counts, s) * (w * w)
    total = sums[:, : s.chan] / count
    cross = sums[:, s.chan : 2 * s.chan] / count
    mean, rstd = stats[0:1, :], stats[1:2, :]
    grad = dot(
        grad_skip[...].reshape(s.images * s.rows * w, s.out), skip_w[...], ((1,), (1,))
    ).reshape(s.images, s.rows, w, s.chan)
    for b in range(s.images):
        keep = live_of(counts, b) * rstd
        for i in range(s.rows):
            normed = (image[b, i].astype(F32) - mean) * rstd
            image_grad[b, i] = keep * (dnorm[b, i] - total - normed * cross) + grad[b, i]
    for g in range(s.groups):
        part = got[g, :, s.at_terms :]
        for r in range(1, s.rows_n):
            part = part + got[r * s.groups + g, :, s.at_terms :]
        for b in range(s.images):
            k = g * s.images + b
            terms[k : k + 1, :] = part[:, b * s.cols : (b + 1) * s.cols]
            at = s.at_cond + b * s.cond
            conds[k : k + 1, :] = cond_got[g, :, at : at + s.cond]
    grad = dot(terms[...], conds[...], ((0,), (0,)), precise)
    store_adamw((cw_new, cm_new, cv_new), (cw, cm, cv), grad, LEARN_RATES[3])
    grad = bias_got[0:1, : s.n_bias]
    for r in range(1, s.rows_n):
        grad = jnp.where(row_pos == r, bias_got[0:1, r * s.n_bias : (r + 1) * s.n_bias], grad)
    store_adamw((bw_new, bm_new, bv_new), (bw, bm, bv), grad, LEARN_RATES[4])


def weights_kernel(sizes, one_grad, two_grad, scales, spec, left_one, left_two, left_skip,
                   ow, om, ov, tw, tm, tv, sw, sm, sv,
                   ow_new, om_new, ov_new, tw_new, tm_new, tv_new, sw_new, sm_new, sv_new):
    s = sizes
    columns = jnp.transpose(spec[...])

    def factor(k):
        inv = spec[3 + k : 4 + k, 0:1]
        return scales[0:1, k : k + 1] * inv * inv * spec[8 + k : 9 + k, 0:1]

    grad = one_grad[...] - columns[: s.out, 0:1] * (left_one[...] * factor(0))
    store_adamw((ow_new, om_new, ov_new), (ow, om, ov), grad, LEARN_RATES[0])
    both = two_grad[...]
    grad = both[:, : s.n_two] - columns[: s.out, 1:2] * (left_two[...] * factor(1))
    store_adamw((tw_new, tm_new, tv_new), (tw, tm, tv), grad, LEARN_RATES[1])
    grad = jnp.transpose(both[:, s.n_two :])
    grad = grad - (left_skip[...] * factor(2)) * spec[2:3, : s.out]
    store_adamw((sw_new, sm_new, sv_new), (sw, sm, sv), grad, LEARN_RATES[2])


def share(chunks):
    return lax.all_to_all(chunks, ALL, 0, 0, tiled=True)


def core_swap(values):
    return lax.ppermute(values, "core", [(0, 1), (1, 0)])


def row_swaps(near, far):
    devices = lax.axis_size("rows")
    pairs = [(i, i ^ 1) for i in range(devices)]
    odd = [(i, i + 1) for i in range(1, devices - 1, 2)]
    odd = odd + [(j, i) for i, j in odd]
    return lax.ppermute(near, "rows", pairs), lax.ppermute(far, "rows", odd)


def scatter_sum(mine, other):
    rows_n, half, width = mine.shape
    n_x = lax.axis_size("x")
    held = mine + core_swap(other)
    got = lax.all_to_all(held.reshape(rows_n * n_x, half // n_x, width), ("rows", "x"), 0, 0, tiled=True)
    total = jnp.sum(got.reshape(rows_n * n_x, half // n_x, width), axis=0)
    return lax.all_gather(total, ("core", "x"), axis=0, tiled=True)


def body(
    image_in,
    condition,
    group_counts,
    out_cotangent,
    power_vectors,
    conv1_weight,
    conv2_weight,
    skip_weight,
    cond_weight,
    out_bias,
    conv1_first,
    conv2_first,
    skip_first,
    cond_first,
    bias_first,
    conv1_second,
    conv2_second,
    skip_second,
    cond_second,
    bias_second,
):
    rows_n = lax.axis_size("rows")
    groups_n = lax.axis_size("x") * lax.axis_size("core")
    masters = [conv1_weight, conv2_weight, skip_weight, cond_weight, out_bias]
    s = Sizes(
        image_in.shape, out_cotangent.shape, condition.shape, [m.shape for m in masters], rows_n, groups_n
    )
    bind = functools.partial
    scratch = pltpu.VMEM
    n, w = s.images, s.width
    depth = 3 * s.slot

    pay, half_one, half_two, near, far, left_one, left_two, left_skip = run(
        bind(prep_kernel, s),
        [
            shape((s.devices, 1, s.pay_one)),
            shape((rows_n, s.h_one, s.out), BF16),
            shape((rows_n, s.h_two + s.h_skip, s.out), BF16),
            shape((n, s.edge, LANES), BF16),
            shape((n, s.edge, LANES), BF16),
            shape((1, s.n_one)),
            shape((1, s.n_two)),
            shape((s.n_skip, 1)),
        ],
        [
            group_counts,
            image_in,
            out_cotangent,
            condition,
            power_vectors,
            power_vectors.T,
            conv1_weight.T,
            conv2_weight.T,
            skip_weight,
            cond_weight.T,
            out_bias[None],
        ],
        [scratch((1, s.pay_one), F32)],
    )
    near, far = row_swaps(near, far)
    mine_one = lax.all_to_all(half_one, "rows", 0, 0, tiled=True)
    got_one = share(pay)
    mine_two = lax.all_to_all(half_two, "rows", 0, 0, tiled=True)
    other_one = core_swap(mine_one)
    other_two = core_swap(mine_two)

    acts, proj, stats_one, spec = run(
        bind(act_kernel, s),
        [
            shape((n, s.rows + 2, w, 4 * s.chan), BF16),
            shape((n, rows_n * s.cols)),
            shape((2, s.chan)),
            shape((16, s.slot)),
        ],
        [group_counts, got_one, image_in, near, far],
    )
    hidden, weight_one, pay = run(
        bind(conv_one_kernel, s),
        [
            shape((n, s.ext, 2, w, s.out)),
            shape((9 * s.chan, s.out), BF16),
            shape((s.devices, 1, s.pay_two)),
        ],
        [group_counts, acts, mine_one, other_one, condition],
        [scratch((1, s.pay_two), F32), scratch((9 * s.chan, s.out), F32)],
        flops=2 * n * s.ext * 2 * w * 9 * s.chan * s.out,
    )
    got_two = share(pay)
    dact, phases, grad_low, grad_skip, skip_part, weight_two, weight_skip, misc = run(
        bind(cot_kernel, s),
        [
            shape((n, s.ext, 2, w, s.out)),
            shape((n, 2 * s.rows, 2, w, s.out), BF16),
            shape((n, 2 * s.rows, 2, w, s.out), BF16),
            shape((n, s.rows, w, s.out), BF16),
            shape((n, s.rows, w, s.out)),
            shape((3, depth, s.out), BF16),
            shape((s.chan, s.out), BF16),
            shape((8, s.slot)),
        ],
        [group_counts, out_cotangent, near, far, image_in, mine_two, other_two, spec],
        [
            scratch((n, 2 * s.rows + 4, w, 4 * s.slot), BF16),
            scratch((9 * s.out + s.chan, s.out), F32),
            scratch((2, 2 * w, LANES), F32),
            scratch((3, depth, s.out), BF16),
        ],
        flops=2 * n * s.ext * 2 * w * 9 * s.out * s.out,
    )
    slots_two, dnorm, stats_two, terms_two, pay = run(
        bind(norm_two_kernel, s),
        [
            shape((n, s.ext, w, 4 * s.slot), BF16),
            shape((n, s.ext, 2, w, s.out)),
            shape((2, s.slot)),
            shape((8, 2 * s.slot)),
            shape((s.devices, 1, s.pay_three)),
        ],
        [group_counts, got_two, hidden, dact, spec, proj, misc],
        [scratch((1, s.pay_three), F32)],
    )
    got_three = share(pay)
    out_image, mine, other, scale_two = run(
        bind(conv_two_kernel, s),
        [
            shape(out_cotangent.shape, BF16),
            shape((rows_n, s.out // 2, s.n_two + s.n_skip)),
            shape((rows_n, s.out // 2, s.n_two + s.n_skip)),
            shape((8, LANES)),
        ],
        [slots_two, weight_two, phases, grad_low, grad_skip, skip_part, image_in, spec],
        [scratch((2, 2 * w, LANES), F32), scratch((s.out, 9 * s.out + s.chan), F32)],
        scalars=0,
        flops=8 * n * s.rows * 2 * w * 9 * s.out * s.out,
    )
    two_grad = scatter_sum(mine, other)
    slots_one, mine, other, scale_one, bias_grad = run(
        bind(hidden_grad_kernel, s),
        [
            shape((n, 2, s.rows + 1, w, 4 * s.slot), BF16),
            shape((rows_n, s.out // 2, s.n_one)),
            shape((rows_n, s.out // 2, s.n_one)),
            shape((8, s.slot)),
            shape((8, s.slot)),
        ],
        [group_counts, got_three, dnorm, hidden, stats_two, spec, acts],
        [scratch((2, 2, n, s.rows, w, s.out), BF16), scratch((s.out, 9 * s.chan), F32)],
        flops=8 * n * s.rows * w * 9 * s.chan * s.out,
    )
    one_grad = scatter_sum(mine, other)
    dnorm_one, pay = run(
        bind(input_grad_kernel, s),
        [shape((n, s.rows, w, s.chan)), shape((s.devices, 1, s.pay_four))],
        [slots_one, weight_one, image_in, stats_one, proj, terms_two, scale_one, scale_two, misc],
        [
            scratch((3, depth, s.chan), BF16),
            scratch((8, rows_n * s.cols), F32),
            scratch((1, s.pay_four), F32),
        ],
        scalars=0,
        flops=8 * n * s.rows * w * 9 * s.chan * s.out,
    )
    got_four = share(pay)
    moments = [cond_weight, cond_first, cond_second]
    biases = [out_bias, bias_first, bias_second]
    image_grad, *rest, scales = run(
        bind(finish_kernel, s),
        [
            shape(image_in.shape),
            *[shape((s.cols, s.cond))] * 3,
            *[shape((1, s.n_bias))] * 3,
            shape((8, LANES)),
        ],
        [
            group_counts,
            got_four,
            got_two,
            bias_grad,
            image_in,
            dnorm_one,
            grad_skip,
            weight_skip,
            stats_one,
            proj,
            *[m.T for m in moments],
            *[b[None] for b in biases],
        ],
        [
            scratch((groups_n * n, s.cols), F32),
            scratch((groups_n * n, s.cond), F32),
        ],
    )
    cond_new = [c.T for c in rest[:3]]
    bias_new = [b[0] for b in rest[3:]]
    olds = [
        *[m.T for m in (conv1_weight, conv1_first, conv1_second)],
        *[m.T for m in (conv2_weight, conv2_first, conv2_second)],
        skip_weight,
        skip_first,
        skip_second,
    ]
    news = run(
        bind(weights_kernel, s),
        [shape(o.shape) for o in olds],
        [one_grad, two_grad, scales, spec, left_one, left_two, left_skip, *olds],
        scalars=0,
    )
    weights_new = [m.T for m in news[:6]] + list(news[6:])
    return (out_image, image_grad, *weights_new, *cond_new, *bias_new)


def solution(mesh):
    rows_n, imgs_n = mesh.devices.shape
    fine = Mesh(np.asarray(mesh.devices).reshape(rows_n, imgs_n // 2, 2), ALL)
    groups = ("x", "core")
    picture = P(groups, "rows", None, None)
    weight = P("rows", None)
    column = P(None, "rows")
    masters = (weight, weight, weight, column, P("rows"))
    return jax.shard_map(
        body,
        mesh=fine,
        in_specs=(picture, P(groups, None), P(), picture, P(), *masters, *masters, *masters),
        out_specs=(
            picture,
            picture,
            *(weight,) * 9,
            *(column,) * 3,
            *(P("rows"),) * 3,
        ),
        check_vma=False,
    )
```

```python
import functools

import jax
import jax.numpy as jnp
import numpy as np
from jax import lax
from jax.experimental import pallas as pl
from jax.experimental.pallas import tpu as pltpu
from jax.sharding import Mesh
from jax.sharding import PartitionSpec as P

STEP = 10
precise = lax.Precision.HIGHEST
NORM_EPS = 1e-05
BETA_ONE = 0.9
BETA_TWO = 0.999
ADAM_EPS = 1e-08
DECAY_RATE = 0.01
LEARN_RATES = (0.02, 0.02, 0.05, 0.03, 0.15)
ALL = ("rows", "x", "core")
F32, BF16 = jnp.float32, jnp.bfloat16
LANES = 128
VMEM_LIMIT = 60 * 2**20


def shape(dims, kind=F32):
    return jax.ShapeDtypeStruct(tuple(dims), kind)


def skipping(kernel, start, count):
    return lambda *refs: kernel(*refs[:start], *refs[start + count :])


def run(kernel, outs, args, scratch=(), scalars=1, flops=0, limit=VMEM_LIMIT, after=(), whole=()):
    spec = pl.BlockSpec(memory_space=pltpu.VMEM)
    specs = [pl.BlockSpec(memory_space=pltpu.SMEM)] * scalars + [spec] * (len(args) - scalars)
    specs += [pl.BlockSpec(memory_space=pl.ANY)] * (len(whole) + len(after))
    moved = sum(a.size * a.dtype.itemsize for a in args)
    args = [*args, *whole, *after]
    if after:
        kernel = skipping(kernel, len(args) - len(after), len(after))
    moved += sum(np.prod(o.shape) * np.dtype(o.dtype).itemsize for o in outs)
    return pl.pallas_call(
        kernel,
        out_shape=tuple(outs),
        in_specs=specs,
        out_specs=tuple(spec for _ in outs),
        scratch_shapes=scratch,
        cost_estimate=pl.CostEstimate(
            flops=int(flops), bytes_accessed=int(moved), transcendentals=0
        ),
        compiler_params=pltpu.CompilerParams(vmem_limit_bytes=limit),
    )(*args)


def round_up(value, step):
    return -(-value // step) * step


class Sizes:
    def __init__(self, image, cot, condition, masters, rows_n, n_x):
        self.images, self.rows, self.width, self.chan = image
        self.out = cot[3]
        self.slot = round_up(self.out, LANES)
        self.ext = 2 * self.rows + 2
        self.cond = condition[1]
        self.n_one, self.n_two, self.n_skip = masters[0][0], masters[1][0], masters[2][0]
        self.cols = masters[3][1]
        self.n_bias = masters[4][0]
        self.rows_n, self.groups = rows_n, 2 * n_x
        self.devices = rows_n * self.groups
        self.h_one = round_up(-(-self.n_one // 2), 8)
        self.h_two = round_up(-(-self.n_two // 2), 8)
        self.h_skip = round_up(-(-self.n_skip // 2), 8)
        self.pack_one = round_up(packed_rows(self.h_one), 16)
        self.pack_two = round_up(packed_rows(self.h_two + self.h_skip), 16)
        self.at_power = 2 * self.chan
        self.at_norm = self.at_power + 3 * self.out
        self.at_bias = self.at_norm + 8
        self.at_proj = round_up(self.at_bias + self.n_bias, LANES)
        self.pay_one = round_up(self.at_proj + self.images * self.cols, LANES)
        self.pay_two = round_up(2 * self.out, LANES)
        self.at_scale = 2 * self.chan
        self.at_gbias = self.at_scale + LANES
        self.at_terms = self.at_gbias + self.slot
        self.at_cond = self.at_terms + round_up(self.images * self.cols, LANES)
        self.pay_four = round_up(self.at_cond + self.images * self.cond, LANES)
        self.part = self.out // 2 // n_x
        self.n_x = n_x
        self.grad_one = grad_rows(self.part, self.n_one)
        self.grad_two = grad_rows(self.part, self.n_two)
        self.grad_skip = grad_rows(self.part, self.n_skip)


HALF = LANES // 2


def from_row(near, far, row):
    row_pos = lax.axis_index("rows")
    at = (row_pos // 2) ^ (row // 2)
    same = lax.rem(row_pos, 2) == row % 2
    return jnp.where(same, near[at].astype(F32), far[at].astype(F32))


def packed_rows(rows):
    return rows + round_up(-(-rows // 2), 8)


def pack(values):
    rows = values.shape[0]
    h = round_up(-(-rows // 2), 8)
    right = values[:, LANES:]
    return jnp.concatenate(
        [values[:, :LANES], jnp.concatenate([right[:h], right[rows - h :]], axis=1)], axis=0
    )


def unpack(values, rows):
    h = round_up(-(-rows // 2), 8)
    right = values[rows : rows + h]
    low = jnp.concatenate([right[:, :HALF], right[2 * h - rows :, HALF:]], axis=0)
    return jnp.concatenate([values[:rows], low], axis=1)


def grad_rows(part, width):
    tail = width % LANES
    rows = part * (width // LANES)
    if tail:
        rows += part // 2 if tail <= HALF and part % 16 == 0 else part
    return rows


def pack_grad(ref, at, lead, values):
    part, width = values.shape
    full = width // LANES
    for k in range(full):
        ref[lead, at + k * part : at + (k + 1) * part, :] = values[:, k * LANES : (k + 1) * LANES]
    at += full * part
    tail = width - full * LANES
    if tail and tail <= HALF and part % 16 == 0:
        h = part // 2
        ref[lead, at : at + h, :tail] = values[:h, full * LANES :]
        ref[lead, at : at + h, HALF : HALF + tail] = values[h:, full * LANES :]
    elif tail:
        ref[lead, at : at + part, :tail] = values[:, full * LANES :]


def unpack_grad(values, at, part, width):
    full = width // LANES
    pieces = [values[at + k * part : at + (k + 1) * part] for k in range(full)]
    at += full * part
    tail = width - full * LANES
    if tail and tail <= HALF and part % 16 == 0:
        h = part // 2
        both = values[at : at + h]
        pieces.append(
            jnp.concatenate([both[:, :tail], both[:, HALF : HALF + tail]], axis=0)
        )
    elif tail:
        pieces.append(values[at : at + part, :tail])
    return pieces[0] if len(pieces) == 1 else jnp.concatenate(pieces, axis=1)


def position():
    return lax.axis_index("rows"), lax.axis_index("x"), lax.axis_index("core")


def group_position():
    return lax.axis_index("x") * lax.axis_size("core") + lax.axis_index("core")


def live_of(counts, image):
    return jnp.where(image < counts[group_position()], 1.0, 0.0).astype(F32)


def live_total(counts, sizes):
    total = counts[0]
    for g in range(1, sizes.groups):
        total = total + counts[g]
    return total.astype(F32)


def inside(row, sizes, scale):
    at = lax.axis_index("rows") * (scale * sizes.rows) + row
    return jnp.where((at >= 0) & (at < scale * sizes.rows * sizes.rows_n), 1.0, 0.0).astype(F32)


def sigmoid(values):
    return 1.0 / (1.0 + jnp.exp(-values))


def shifted(values, step):
    width = values.shape[0]
    rolled = pltpu.roll(values, (-step) % width, 0)
    where = lax.broadcasted_iota(jnp.int32, values.shape, 0)
    edge = 0 if step < 0 else width - 1
    return jnp.where(where == edge, 0.0, rolled)


def dot(a, b, dims=((1,), (0,)), precision=None):
    return lax.dot_general(a, b, (dims, ((), ())), preferred_element_type=F32, precision=precision)


def prep_kernel(sizes, counts, image, cond, vec, one_t, two_t, skip, cond_t, bias,
                pay, half_one, half_two, near, far, left_one, left_two,
                left_skip, line):
    s = sizes
    row_pos, _, core = position()
    even = lax.rem(row_pos, 2) == 0
    last, w = s.rows - 1, s.width

    line[...] = jnp.zeros_like(line)
    vec_t = jnp.transpose(jnp.concatenate([vec[...], jnp.zeros((5, s.out), F32)], axis=0))

    def power(k, low):
        column = jnp.sum(low * vec[k : k + 1, :], axis=1, keepdims=True)
        row = jnp.sum(low * column, axis=0, keepdims=True)
        at = s.at_power + k * s.out
        line[0:1, at : at + s.out] = row
        at = s.at_norm + k
        line[0:1, at : at + 1] = jnp.sum(column * column, axis=0, keepdims=True)
        return column

    low_t = one_t[...].astype(BF16).astype(F32)
    left_one[...] = jnp.sum(low_t * vec_t[:, 0:1], axis=0, keepdims=True)
    low = jnp.transpose(low_t)
    power(0, low)
    n, h = s.n_one, s.h_one
    packed_one = pack(jnp.where(core == 0, low[:h], low[n - h :]))
    low_t = two_t[...].astype(BF16).astype(F32)
    left_two[...] = jnp.sum(low_t * vec_t[:, 1:2], axis=0, keepdims=True)
    low = jnp.transpose(low_t)
    power(1, low)
    n, h = s.n_two, s.h_two
    half_a = jnp.where(core == 0, low[:h], low[n - h :])
    low = skip[...].astype(BF16).astype(F32)
    left_skip[...] = power(2, low)
    n, h = s.n_skip, s.h_skip
    half_b = jnp.where(core == 0, low[:h], low[n - h :])
    packed = pack(jnp.concatenate([half_a, half_b], axis=0))
    if s.pack_two > packed.shape[0]:
        packed = jnp.concatenate(
            [packed, jnp.zeros((s.pack_two - packed.shape[0], LANES), F32)], axis=0
        )
    packed = packed.astype(BF16)
    half_two[...] = packed
    line[0:1, s.at_bias : s.at_bias + s.n_bias] = bias[...].astype(BF16).astype(F32)
    proj = dot(cond[...], cond_t[...].astype(BF16), ((1,), (1,)))
    for b in range(s.images):
        at = s.at_proj + b * s.cols
        line[0:1, at : at + s.cols] = proj[b : b + 1]
    if s.pack_one > packed_one.shape[0]:
        packed_one = jnp.concatenate(
            [packed_one, jnp.zeros((s.pack_one - packed_one.shape[0], LANES), F32)], axis=0
        )
    half_one[...] = packed_one.astype(BF16)

    def edges(ref, row):
        for t in range(3):
            ref[:, t * w : (t + 1) * w, :] = image[:, row, :, t * LANES : (t + 1) * LANES]

    @pl.when(even)
    def _():
        edges(near, last)
        edges(far, 0)

    @pl.when(jnp.logical_not(even))
    def _():
        edges(near, 0)
        edges(far, last)

    sums = jnp.zeros((8, s.chan), F32)
    squares = jnp.zeros((8, s.chan), F32)
    for b in range(s.images):
        part = jnp.zeros((8, s.chan), F32)
        part_sq = jnp.zeros((8, s.chan), F32)
        for i in range(s.rows):
            x = image[b, i].astype(F32).reshape(w // 8, 8, s.chan)
            part += jnp.sum(x, axis=0)
            part_sq += jnp.sum(x * x, axis=0)
        sums += part * live_of(counts, b)
        squares += part_sq * live_of(counts, b)
    line[0:1, : s.chan] = jnp.sum(sums, axis=0, keepdims=True)
    line[0:1, s.chan : 2 * s.chan] = jnp.sum(squares, axis=0, keepdims=True)
    whole = line[...]
    for d in range(s.devices):
        pay[d] = whole


def stack_kernel(sizes, two, *refs):
    s = sizes
    *blocks, near, two_out = refs
    for m, block in enumerate(blocks):
        near[m] = block[...]
    two_out[...] = two[...]


def act_kernel(sizes, counts, got, image, near, far, cot, slots, proj, stats, spec,
               near_cot, far_cot, first_rows, last_rows, sems):
    s = sizes
    row_pos, _, _ = position()
    even = lax.rem(row_pos, 2) == 0
    copies = [
        pltpu.make_async_copy(cot.at[:, pl.ds(0, 2)], first_rows, sems.at[0]),
        pltpu.make_async_copy(cot.at[:, pl.ds(2 * s.rows - 2, 2)], last_rows, sems.at[1]),
    ]
    for copy in copies:
        copy.start()
    group = group_position()
    sums = jnp.sum(got[:, :, : 2 * s.chan], axis=0)
    count = live_total(counts, s) * (s.width * s.width)
    mean = sums[:, : s.chan] / count
    rstd = lax.rsqrt(sums[:, s.chan :] / count - mean * mean + NORM_EPS)
    stats[0:1, :] = mean
    stats[1:2, :] = rstd

    spec[...] = jnp.zeros_like(spec)
    total = None
    for r in range(s.rows_n):
        piece = got[r * s.groups + group, :, s.at_power :]
        part = piece[:, : s.at_proj - s.at_power]
        total = part if total is None else total + part
        at = s.at_bias - s.at_power
        spec[6:7, r * s.n_bias : (r + 1) * s.n_bias] = piece[:, at : at + s.n_bias]
        for b in range(s.images):
            at = s.at_proj - s.at_power + b * s.cols
            proj[b : b + 1, r * s.cols : (r + 1) * s.cols] = piece[:, at : at + s.cols]
    for k in range(3):
        at = s.at_norm - s.at_power + k
        inv_norm = lax.rsqrt(total[:, at : at + 1])
        row = total[:, k * s.out : (k + 1) * s.out] * inv_norm
        inv_sigma = lax.rsqrt(jnp.sum(row * row, axis=1, keepdims=True))
        spec[k : k + 1, : s.out] = row * inv_sigma
        spec[3 + k : 4 + k, :] = jnp.broadcast_to(inv_sigma, (1, s.slot))
        spec[8 + k : 9 + k, :] = jnp.broadcast_to(inv_norm, (1, s.slot))

    w = s.width

    def one(b, e, x, keep):
        gain = 1.0 + proj[pl.ds(b, 1), : s.chan]
        shift = proj[pl.ds(b, 1), s.chan : 2 * s.chan]
        pre = gain * ((x - mean) * rstd) + shift
        act = pre * sigmoid(pre)
        if keep is not None:
            act = act * keep
        low = act.astype(BF16)
        slots[b, e, :, s.chan : 2 * s.chan] = low
        slots[b, e, :, 2 * s.chan : 3 * s.chan] = low
        slots[b, e, :, : s.chan] = shifted(act, -1).astype(BF16)
        slots[b, e, :, 3 * s.chan :] = shifted(act, 1).astype(BF16)

    def edge(ref, b):
        return jnp.concatenate(
            [ref[b, t * w : (t + 1) * w, :].astype(F32) for t in range(3)], axis=1
        )

    @pl.loop(0, s.images)
    def _(b):
        a, c = edge(near, b), edge(far, b)
        one(b, 0, jnp.where(even, c, a), inside(-1, s, 1))
        for i in range(s.rows):
            one(b, i + 1, image[b, i].astype(F32), None)
        one(b, s.rows + 1, jnp.where(even, a, c), inside(s.rows, s, 1))

    for copy in copies:
        copy.wait()

    def cot_edges(ref, rows):
        for b in range(s.images):
            for k in range(2):
                ref[b, 2 * w * k : 2 * w * (k + 1), :] = rows[b, k, :, :LANES]
            right = [rows[b, k, :, LANES:].astype(F32) for k in range(2)]
            ref[b, 4 * w :, :] = jnp.concatenate(right, axis=1).astype(BF16)

    @pl.when(even)
    def _():
        cot_edges(near_cot, last_rows)
        cot_edges(far_cot, first_rows)

    @pl.when(jnp.logical_not(even))
    def _():
        cot_edges(near_cot, first_rows)
        cot_edges(far_cot, last_rows)


def conv_one_kernel(sizes, counts, slots, mine_near, mine_far, other_near, other_far, hidden, weight, pay, line, wide):
    s = sizes
    _, _, core = position()
    first = core == 0
    for r in range(s.rows_n):
        a = unpack(from_row(mine_near, mine_far, r), s.h_one)
        b = unpack(from_row(other_near, other_far, r), s.h_one)
        at = r * s.n_one
        wide[at : at + s.h_one, :] = jnp.where(first, a, b)
        at += s.n_one - s.h_one
        wide[at : at + s.h_one, :] = jnp.where(first, b, a)
    for t in range(9):
        weight[t * s.chan : (t + 1) * s.chan] = wide[t * s.chan : (t + 1) * s.chan, :].astype(BF16)
    depth = 3 * s.chan
    rows = s.rows + 1
    sums = jnp.zeros((8, s.out), F32)
    squares = jnp.zeros((8, s.out), F32)
    for phase in range(4):
        a, b = divmod(phase, 2)
        total = None
        for dy in range(3):
            start = (a + dy - 1) // 2 + 1 - a
            lhs = slots[:, start : start + rows, :, b * s.chan : b * s.chan + depth]
            part = dot(
                lhs.reshape(s.images * rows * s.width, depth),
                weight[dy * depth : (dy + 1) * depth, :],
            )
            total = part if total is None else total + part
        total = total.reshape(s.images, rows, s.width, s.out)
        for i in range(s.images):
            part = jnp.zeros((8, s.out), F32)
            part_sq = jnp.zeros((8, s.out), F32)
            for k in range(rows):
                e = 2 * k + 1 - a
                value = total[i, k]
                hidden[i, e, b] = value
                if 0 < e < s.ext - 1:
                    x = value.reshape(s.width // 8, 8, s.out)
                    part += jnp.sum(x, axis=0)
                    part_sq += jnp.sum(x * x, axis=0)
            sums += part * live_of(counts, i)
            squares += part_sq * live_of(counts, i)
    line[...] = jnp.zeros_like(line)
    line[0:1, : s.out] = jnp.sum(sums, axis=0, keepdims=True)
    line[0:1, s.out : 2 * s.out] = jnp.sum(squares, axis=0, keepdims=True)
    whole = line[...]
    for d in range(s.devices):
        pay[d] = whole


def cot_kernel(sizes, counts, cot, near, far, image, mine_near, mine_far, other_near, other_far, spec, dact, phases, grad_low,
               grad_skip, skip_part, two, skip_w, misc, slots, wide, pair, flip):
    s = sizes
    row_pos, _, core = position()
    even = lax.rem(row_pos, 2) == 0
    first = core == 0
    w = s.width
    for r in range(s.rows_n):
        a = unpack(from_row(mine_near, mine_far, r), s.h_two + s.h_skip)
        b = unpack(from_row(other_near, other_far, r), s.h_two + s.h_skip)
        lo, hi = jnp.where(first, a, b), jnp.where(first, b, a)
        at = r * s.n_two
        wide[at : at + s.h_two, :] = lo[: s.h_two]
        at += s.n_two - s.h_two
        wide[at : at + s.h_two, :] = hi[: s.h_two]
        at = 9 * s.out + r * s.n_skip
        wide[at : at + s.h_skip, :] = lo[s.h_two :]
        at += s.n_skip - s.h_skip
        wide[at : at + s.h_skip, :] = hi[s.h_two :]
    two[...] = jnp.zeros_like(two)
    flip[...] = jnp.zeros_like(flip)
    for t in range(9):
        dy, dx = divmod(t, 3)
        tap = wide[t * s.out : (t + 1) * s.out, :]
        two[dy, dx * s.slot : dx * s.slot + s.out, :] = tap.astype(BF16)
        back = jnp.transpose(tap).astype(BF16)
        flip[2 - dy, (2 - dx) * s.slot : (2 - dx) * s.slot + s.out, :] = back
    skip_w[...] = wide[9 * s.out : 9 * s.out + s.chan, :].astype(BF16)

    slots[...] = jnp.zeros_like(slots)
    inv_two = spec[4:5, : s.out]
    inv_skip = spec[5:6, : s.out]

    def split(b, q, row, own):
        pair[0] = row[:, :LANES]
        pair[1, :, : s.out - LANES] = row[:, LANES:]
        both = []
        for ph in range(2):
            value = jnp.concatenate(
                [pair[0, pl.ds(ph, w, 2), :], pair[1, pl.ds(ph, w, 2), :][:, : s.out - LANES]],
                axis=1,
            )
            low = (value * inv_two).astype(BF16)
            both.append(value)
            if own is not None:
                phases[b, own, ph] = value.astype(BF16)
                grad_low[b, own, ph] = low
            at = (1 + ph) * s.slot
            slots[b, q, :, at : at + s.out] = low
            if ph == 1:
                slots[b, q, :, : s.out] = shifted(low.astype(F32), -1).astype(BF16)
            else:
                slots[b, q, :, 3 * s.slot : 3 * s.slot + s.out] = shifted(
                    low.astype(F32), 1
                ).astype(BF16)
        return both[0] + both[1]

    def edge_row(ref, b, k):
        right = ref[b, 4 * w :, :].astype(F32)
        return jnp.concatenate(
            [
                ref[b, 2 * w * k : 2 * w * (k + 1), :].astype(F32),
                right[:, k * HALF : k * HALF + s.out - LANES],
            ],
            axis=1,
        )

    misc[...] = jnp.zeros_like(misc)

    @pl.loop(0, s.images)
    def _(b):
        live = live_of(counts, b)
        above = inside(-1, s, 1) * live
        below = inside(s.rows, s, 1) * live
        for k in range(2):
            a, c = edge_row(near, b, k), edge_row(far, b, k)
            split(b, k, jnp.where(even, c, a) * above, None)
            split(b, 2 * s.rows + 2 + k, jnp.where(even, a, c) * below, None)
        bias = jnp.zeros((1, s.out), F32)
        skip_sum = jnp.zeros((1, s.out), F32)
        for i in range(s.rows):
            pooled = split(b, 2 * i + 2, cot[b, 2 * i].astype(F32) * live, 2 * i)
            pooled += split(b, 2 * i + 3, cot[b, 2 * i + 1].astype(F32) * live, 2 * i + 1)
            grad_skip[b, i] = (pooled * inv_skip).astype(BF16)
            bias += jnp.sum(pooled, axis=0, keepdims=True)
            raw = dot(image[b, i], skip_w[...])
            skip_part[b, i] = raw * inv_skip
            skip_sum += jnp.sum(pooled * raw, axis=0, keepdims=True)
        misc[0:1, : s.out] += bias
        misc[1:2, : s.out] += skip_sum

    depth = 3 * s.slot
    for ph in range(2):
        total = None
        for dy in range(3):
            lhs = slots[:, dy : dy + s.ext, :, ph * s.slot : ph * s.slot + depth]
            part = dot(lhs.reshape(s.images * s.ext * w, depth), flip[dy])
            total = part if total is None else total + part
        dact[:, :, ph] = total.reshape(s.images, s.ext, w, s.out)


def norm_two_kernel(sizes, counts, got, hidden, dact, spec, proj, slots, dnorm, stats,
                    terms, pay, line):
    s = sizes
    w = s.width
    inv = spec[3:4, : s.out]
    sums = jnp.sum(got[...], axis=0)
    count = live_total(counts, s) * (4 * w * w)
    mean = sums[:, : s.out] * inv / count
    square = sums[:, s.out : 2 * s.out] * inv * inv / count
    rstd = lax.rsqrt(square - mean * mean + NORM_EPS)
    stats[0:1, : s.out] = mean
    stats[1:2, : s.out] = rstd
    scale = inv * rstd
    offset = mean * rstd
    slots[...] = jnp.zeros_like(slots)
    base = 2 * s.chan

    def one(b, e, keep):
        gain = 1.0 + proj[pl.ds(b, 1), base : base + s.out]
        shift = proj[pl.ds(b, 1), base + s.out : base + 2 * s.out]
        dsum = jnp.zeros((8, s.out), F32)
        dgain = jnp.zeros((8, s.out), F32)
        for ph in range(2):
            normed = hidden[b, e, ph] * scale - offset
            pre = gain * normed + shift
            sig = sigmoid(pre)
            act = pre * sig
            if keep is not None:
                act = act * keep
            at = (1 + ph) * s.slot
            slots[b, e, :, at : at + s.out] = act.astype(BF16)
            if ph == 1:
                slots[b, e, :, : s.out] = shifted(act, -1).astype(BF16)
            else:
                slots[b, e, :, 3 * s.slot : 3 * s.slot + s.out] = shifted(act, 1).astype(BF16)
            dpre = dact[b, e, ph] * (sig * (1.0 + pre * (1.0 - sig)))
            dnorm[b, e, ph] = gain * dpre
            if keep is None:
                dsum += jnp.sum(dpre.reshape(w // 8, 8, s.out), axis=0)
                dgain += jnp.sum((dpre * normed).reshape(w // 8, 8, s.out), axis=0)
        return dsum, dgain

    terms[...] = jnp.zeros_like(terms)

    @pl.loop(0, s.images)
    def _(b):
        one(b, 0, inside(-1, s, 2))
        dsum = jnp.zeros((8, s.out), F32)
        dgain = jnp.zeros((8, s.out), F32)
        for e in range(1, s.ext - 1):
            a, c = one(b, e, None)
            dsum += a
            dgain += c
        one(b, s.ext - 1, inside(2 * s.rows, s, 2))
        terms[pl.ds(b, 1), : s.out] = jnp.sum(dgain, axis=0, keepdims=True)
        terms[pl.ds(b, 1), s.out : 2 * s.out] = jnp.sum(dsum, axis=0, keepdims=True)

    total = jnp.zeros((1, s.out), F32)
    cross = jnp.zeros((1, s.out), F32)
    for b in range(s.images):
        gain = 1.0 + proj[b : b + 1, base : base + s.out]
        cross += gain * terms[b : b + 1, : s.out]
        total += gain * terms[b : b + 1, s.out : 2 * s.out]
    line[...] = jnp.zeros_like(line)
    line[0:1, : s.out] = total
    line[0:1, s.out : 2 * s.out] = cross
    whole = line[...]
    for d in range(s.devices):
        pay[d] = whole


def conv_two_kernel(sizes, slots, two, phases, skip_part, spec, out, scale, pair):
    s = sizes
    w = s.width
    depth = 3 * s.slot
    own = 2 * s.rows
    inv_two = spec[4:5, : s.out]
    bias = spec[6:7, : s.out]
    dots = jnp.zeros((1, s.out), F32)
    results = []
    for ph in range(2):
        total = None
        for dy in range(3):
            lhs = slots[:, dy : dy + own, :, ph * s.slot : ph * s.slot + depth]
            part = dot(lhs.reshape(s.images * own * w, depth), two[dy])
            total = part if total is None else total + part
        results.append(total.reshape(s.images, own, w, s.out))
    for b in range(s.images):
        for e in range(own):
            for ph in range(2):
                raw = results[ph][b, e]
                dots += jnp.sum(raw * phases[b, e, ph].astype(F32), axis=0, keepdims=True)
                value = raw * inv_two + skip_part[b, e // 2] + bias
                pair[0, pl.ds(ph, w, 2), :] = value[:, :LANES]
                pair[1, pl.ds(ph, w, 2), :] = jnp.concatenate(
                    [value[:, LANES:], jnp.zeros((w, 2 * LANES - s.out), F32)], axis=1
                )
            out[b, e, :, :LANES] = pair[0].astype(BF16)
            out[b, e, :, LANES:] = pair[1][:, : s.out - LANES].astype(BF16)
    scale[...] = jnp.broadcast_to(jnp.sum(dots, axis=1, keepdims=True), scale.shape)


def grads_two(s, slots, grad_low, grad_skip, image, grads):
    w = s.width
    own = 2 * s.rows
    depth = 3 * s.slot
    count = s.images * own * w
    flips = [jnp.transpose(grad_low[:, :, ph].reshape(count, s.out)) for ph in range(2)]
    for dy in range(3):
        total = None
        for ph in range(2):
            rhs = slots[:, dy : dy + own, :, ph * s.slot : ph * s.slot + depth]
            part = dot(flips[ph], rhs.reshape(count, depth))
            total = part if total is None else total + part
        for dx in range(3):
            at = (3 * dy + dx) * s.out
            grads[:, at : at + s.out] = total[:, dx * s.slot : dx * s.slot + s.out]
    count = s.images * s.rows * w
    flip = jnp.transpose(grad_skip[...].reshape(count, s.out))
    grads[:, 9 * s.out : 9 * s.out + s.chan] = dot(flip, image[...].reshape(count, s.chan))


def hidden_grad_kernel(sizes, counts, got, dnorm, hidden, stats, spec, acts, slots_two, grad_low,
                       grad_skip, image, slots, mine, other, scale, low, grads, grads_b):
    s = sizes
    _, _, core = position()
    w = s.width
    sums = jnp.sum(got[...], axis=0)
    count = live_total(counts, s) * (4 * w * w)
    mean, rstd = stats[0:1, : s.out], stats[1:2, : s.out]
    inv = spec[3:4, : s.out]
    total = sums[:, : s.out] / count
    cross = sums[:, s.out : 2 * s.out] / count
    slots[...] = jnp.zeros_like(slots)
    norm_scale = inv * rstd
    offset = mean * rstd

    def one(b, e, keep, own):
        par, k = e % 2, e // 2
        dots = jnp.zeros((8, s.out), F32)
        for ph in range(2):
            raw = hidden[b, e, ph]
            normed = raw * norm_scale - offset
            grad = keep * (rstd * (dnorm[b, e, ph] - total - normed * cross))
            if own:
                dots += jnp.sum((grad * raw).reshape(w // 8, 8, s.out), axis=0)
            value = grad * inv
            small = value.astype(BF16)
            at = (1 + ph) * s.slot
            slots[b, par, k, :, at : at + s.out] = small
            if own:
                low[1 - par, ph, b, (e - 1) // 2] = small
            if ph == 1:
                slots[b, par, k, :, : s.out] = shifted(value, -1).astype(BF16)
            else:
                slots[b, par, k, :, 3 * s.slot : 3 * s.slot + s.out] = shifted(value, 1).astype(
                    BF16
                )
        return dots

    scale[...] = jnp.zeros_like(scale)

    @pl.loop(0, s.images)
    def _(b):
        live = live_of(counts, b)
        one(b, 0, live * inside(-1, s, 2), False)
        dots = jnp.zeros((8, s.out), F32)
        for e in range(1, s.ext - 1):
            dots += one(b, e, live, True)
        one(b, s.ext - 1, live * inside(2 * s.rows, s, 2), False)
        scale[0:1, : s.out] += jnp.sum(dots, axis=0, keepdims=True)

    count = s.images * s.rows * w
    depth = 3 * s.chan
    for dy in range(3):
        total = None
        for phase in range(4):
            a, b = divmod(phase, 2)
            flip = jnp.transpose(low[a, b].reshape(count, s.out))
            start = 1 + (a + dy - 1) // 2
            rhs = acts[:, start : start + s.rows, :, b * s.chan : b * s.chan + depth]
            part = dot(flip, rhs.reshape(count, depth))
            total = part if total is None else total + part
        grads[:, dy * depth : (dy + 1) * depth] = total
    grads_two(s, slots_two, grad_low, grad_skip, image, grads_b)
    for ref, which in ((mine, core), (other, 1 - core)):
        for x in range(s.n_x):
            at = pl.multiple_of((which * s.n_x + x) * s.part, 8)
            here = pl.ds(at, s.part)
            for r in range(s.rows_n):
                lead = r * s.n_x + x
                start = r * s.n_one
                pack_grad(ref, 0, lead, grads[here, start : start + s.n_one])
                start = r * s.n_two
                pack_grad(ref, s.grad_one, lead, grads_b[here, start : start + s.n_two])
                start = 9 * s.out + r * s.n_skip
                pack_grad(
                    ref, s.grad_one + s.grad_two, lead, grads_b[here, start : start + s.n_skip]
                )


def input_grad_kernel(sizes, slots, weight, image, stats, proj, terms_two, scale_one, scale_two,
                      misc, cond, dnorm, pay, back, terms, line):
    s = sizes
    w = s.width
    depth = 3 * s.slot
    back[...] = jnp.zeros_like(back)
    for t in range(9):
        dy, dx = divmod(t, 3)
        tap = weight[t * s.chan : (t + 1) * s.chan, :].astype(F32)
        at = (2 - dx) * s.slot
        back[dy, at : at + s.out, :] = jnp.transpose(tap).astype(BF16)
    total = None
    for a in range(2):
        for dy in range(3):
            par, k = (a + 2 - dy) % 2, (a + 2 - dy) // 2
            for ph in range(2):
                lhs = slots[:, par, k : k + s.rows, :, ph * s.slot : ph * s.slot + depth]
                part = dot(lhs.reshape(s.images * s.rows * w, depth), back[dy])
                total = part if total is None else total + part
    total = total.reshape(s.images, s.rows, w, s.chan)
    mean, rstd = stats[0:1, :], stats[1:2, :]
    all_sum = jnp.zeros((1, s.chan), F32)
    all_cross = jnp.zeros((1, s.chan), F32)
    for b in range(s.images):
        gain = 1.0 + proj[b : b + 1, : s.chan]
        shift = proj[b : b + 1, s.chan : 2 * s.chan]
        dsum = jnp.zeros((8, s.chan), F32)
        dgain = jnp.zeros((8, s.chan), F32)
        for i in range(s.rows):
            normed = (image[b, i].astype(F32) - mean) * rstd
            pre = gain * normed + shift
            sig = sigmoid(pre)
            dpre = total[b, i] * (sig * (1.0 + pre * (1.0 - sig)))
            dnorm[b, i] = gain * dpre
            dsum += jnp.sum(dpre.reshape(w // 8, 8, s.chan), axis=0)
            dgain += jnp.sum((dpre * normed).reshape(w // 8, 8, s.chan), axis=0)
        dsum = jnp.sum(dsum, axis=0, keepdims=True)
        dgain = jnp.sum(dgain, axis=0, keepdims=True)
        terms[b : b + 1, : s.chan] = dgain
        terms[b : b + 1, s.chan : 2 * s.chan] = dsum
        terms[b : b + 1, 2 * s.chan :] = terms_two[b : b + 1, : 2 * s.out]
        all_sum += gain * dsum
        all_cross += gain * dgain
    line[...] = jnp.zeros_like(line)
    line[0:1, : s.chan] = all_sum
    line[0:1, s.chan : 2 * s.chan] = all_cross
    at = s.at_scale
    line[0:1, at : at + 1] = jnp.sum(scale_one[0:1, : s.out], axis=1, keepdims=True)
    line[0:1, at + 1 : at + 2] = scale_two[0:1, 0:1]
    line[0:1, at + 2 : at + 3] = jnp.sum(misc[1:2, : s.out], axis=1, keepdims=True)
    at = s.at_gbias
    line[0:1, at : at + s.out] = misc[0:1, : s.out]
    for b in range(s.images):
        at = s.at_cond + b * s.cond
        line[0:1, at : at + s.cond] = cond[b : b + 1, :].astype(F32)
    for r in range(s.rows_n):
        for b in range(s.images):
            at = s.at_terms + b * s.cols
            line[0:1, at : at + s.cols] = terms[b : b + 1, r * s.cols : (r + 1) * s.cols]
        whole = line[...]
        for g in range(s.groups):
            pay[r * s.groups + g] = whole


def adamw(weight, first_old, second, gradient, learn_rate):
    first_new = BETA_ONE * first_old + (1.0 - BETA_ONE) * gradient
    second_new = BETA_TWO * second + (1.0 - BETA_TWO) * gradient * gradient
    first_hat = first_new / (1.0 - BETA_ONE**STEP)
    second_hat = second_new / (1.0 - BETA_TWO**STEP)
    weight_new = weight - learn_rate * (
        first_hat / (jnp.sqrt(second_hat) + ADAM_EPS) + DECAY_RATE * weight
    )
    return (weight_new, first_new, second_new)


def store_adamw(refs, olds, gradient, rate):
    for ref, value in zip(refs, adamw(*(old[...] for old in olds), gradient, rate)):
        ref[...] = value


def finish_kernel(sizes, counts, got, image, dnorm, grad_skip, skip_w, stats, proj,
                  cw, cm, cv, bw, bm, bv,
                  image_grad, cw_new, cm_new, cv_new, bw_new, bm_new, bv_new, scales, terms, conds):
    s = sizes
    w = s.width
    row_pos, _, _ = position()
    sums = jnp.sum(got[:, :, : s.at_terms], axis=0)
    scales[...] = jnp.broadcast_to(sums[:, s.at_scale : s.at_gbias], scales.shape)
    count = live_total(counts, s) * (w * w)
    total = sums[:, : s.chan] / count
    cross = sums[:, s.chan : 2 * s.chan] / count
    mean, rstd = stats[0:1, :], stats[1:2, :]
    grad = dot(
        grad_skip[...].reshape(s.images * s.rows * w, s.out), skip_w[...], ((1,), (1,))
    ).reshape(s.images, s.rows, w, s.chan)
    for b in range(s.images):
        keep = live_of(counts, b) * rstd
        for i in range(s.rows):
            normed = (image[b, i].astype(F32) - mean) * rstd
            image_grad[b, i] = keep * (dnorm[b, i] - total - normed * cross) + grad[b, i]
    for g in range(s.groups):
        part = got[g, :, s.at_terms : s.at_cond]
        for r in range(1, s.rows_n):
            part = part + got[r * s.groups + g, :, s.at_terms : s.at_cond]
        for b in range(s.images):
            k = g * s.images + b
            terms[k : k + 1, :] = part[:, b * s.cols : (b + 1) * s.cols]
            at = s.at_cond + b * s.cond
            conds[k : k + 1, :] = got[g, :, at : at + s.cond]
    grad = dot(terms[...], conds[...], ((0,), (0,)), precise)
    store_adamw((cw_new, cm_new, cv_new), (cw, cm, cv), grad, LEARN_RATES[3])
    grad = sums[:, s.at_gbias : s.at_gbias + s.n_bias]
    for r in range(1, s.rows_n):
        at = s.at_gbias + r * s.n_bias
        grad = jnp.where(row_pos == r, sums[:, at : at + s.n_bias], grad)
    store_adamw((bw_new, bm_new, bv_new), (bw, bm, bv), grad, LEARN_RATES[4])


def weights_kernel(sizes, own, beside, beyond, across, scales, spec, left_one, left_two, left_skip,
                   ow, om, ov, tw, tm, tv, sw, sm, sv,
                   ow_new, om_new, ov_new, tw_new, tm_new, tv_new, sw_new, sm_new, sv_new, one_grad, two_grad, skip_grad):
    s = sizes
    _, x_pos, core = position()
    columns = jnp.transpose(spec[...])

    def factor(k):
        inv = spec[3 + k : 4 + k, 0:1]
        return scales[0:1, k : k + 1] * inv * inv * spec[8 + k : 9 + k, 0:1]

    def place(parts, which):
        for x, part in enumerate(parts):
            at = pl.multiple_of((which * s.n_x + x) * s.part, 8)
            here = pl.ds(at, s.part)
            one_grad[here, :] = unpack_grad(part, 0, s.part, s.n_one)
            two_grad[here, :] = unpack_grad(part, s.grad_one, s.part, s.n_two)
            skip_grad[here, :] = unpack_grad(part, s.grad_one + s.grad_two, s.part, s.n_skip)

    def ordered(mine, other):
        if s.n_x != 2:
            return [mine[x] for x in range(s.n_x)]
        a, b = mine[0], other[0]
        return [jnp.where(x_pos == 0, a, b), jnp.where(x_pos == 0, b, a)]

    place(ordered(own, beside), core)
    place(ordered(beyond, across), 1 - core)

    grad = one_grad[...] - columns[: s.out, 0:1] * (left_one[...] * factor(0))
    store_adamw((ow_new, om_new, ov_new), (ow, om, ov), grad, LEARN_RATES[0])
    grad = two_grad[...] - columns[: s.out, 1:2] * (left_two[...] * factor(1))
    store_adamw((tw_new, tm_new, tv_new), (tw, tm, tv), grad, LEARN_RATES[1])
    grad = jnp.transpose(skip_grad[...])
    grad = grad - (left_skip[...] * factor(2)) * spec[2:3, : s.out]
    store_adamw((sw_new, sm_new, sv_new), (sw, sm, sv), grad, LEARN_RATES[2])


def share(chunks):
    return lax.all_to_all(chunks, ALL, 0, 0, tiled=True)


def core_swap(values):
    return lax.ppermute(values, "core", [(0, 1), (1, 0)])


def row_swaps(near, far):
    devices = lax.axis_size("rows")
    pairs = [(i, i ^ 1) for i in range(devices)]
    odd = [(i, i + 1) for i in range(1, devices - 1, 2)]
    odd = odd + [(j, i) for i, j in odd]
    return lax.ppermute(near, "rows", pairs), lax.ppermute(far, "rows", odd)


def row_swap(values, step):
    devices = lax.axis_size("rows")
    return lax.ppermute(values, "rows", [(i, i ^ step) for i in range(devices)])


def x_swap(values):
    return lax.ppermute(values, "x", [(0, 1), (1, 0)])


def gather_upper(block):
    return [block] + [row_swap(block, 2 * m) for m in range(1, lax.axis_size("rows") // 2)]


def first_sum_kernel(mine, got, send_a, keep_a, send_b, keep_b):
    _, x, _ = position()
    low = lax.rem(lax.axis_index("rows"), 2)
    half = send_a.shape[0]
    for i in range(half):
        for k in range(2):
            send_a[i, k] = mine[i, k, 1 - x] + got[i, k, 1 - x]
            keep_a[i, k] = mine[i, k, x] + got[i, k, x]
            send_b[i, k] = mine[half + i, 1 - low, k] + got[half + i, 1 - low, k]
            keep_b[i, k] = mine[half + i, low, k] + got[half + i, low, k]


def second_sum_kernel(keep_a, got_a, keep_b, got_b, send_a, held_a, send_b, held_b):
    _, x, _ = position()
    low = lax.rem(lax.axis_index("rows"), 2)
    for i in range(keep_a.shape[0]):
        send_a[i] = keep_a[i, 1 - low] + got_a[i, 1 - low]
        held_a[i] = keep_a[i, low] + got_a[i, low]
        send_b[i] = keep_b[i, 1 - x] + got_b[i, 1 - x]
        held_b[i] = keep_b[i, x] + got_b[i, x]


def third_sum_kernel(held_a, got_a, held_b, got_b, *outs):
    high = lax.axis_index("rows") // 2
    half = held_a.shape[0]
    for m, out in enumerate(outs):
        at = high ^ m

        @pl.when(at < half)
        def _():
            out[0] = held_a[jnp.minimum(at, half - 1)] + got_a[jnp.minimum(at, half - 1)]

        @pl.when(at >= half)
        def _():
            at_b = jnp.maximum(at - half, 0)
            out[0] = held_b[at_b] + got_b[at_b]


def sum_kernel(*refs):
    *parts, out = refs
    total = parts[0][...]
    for part in parts[1:]:
        total = total + part[...]
    out[...] = total


class StagedSum:
    small = 8 * 2**20

    def __init__(self, mine, other):
        self.high = lax.axis_size("rows") // 2
        self.tail = mine.shape[1:]
        mine = mine.reshape(self.high, 2, 2, *self.tail)
        got = core_swap(other).reshape(self.high, 2, 2, *self.tail)
        send_a, keep_a, send_b, keep_b = run(
            first_sum_kernel,
            [shape((self.high // 2, 2, *self.tail))] * 4,
            [mine, got],
            scalars=0,
            limit=self.small,
        )
        self.held = [keep_a, x_swap(send_a), keep_b, row_swap(send_b, 1)]

    def second(self, after):
        send_a, held_a, send_b, held_b = run(
            second_sum_kernel,
            [shape((self.high // 2, *self.tail))] * 4,
            self.held,
            scalars=0,
            limit=self.small,
            after=after,
        )
        self.held = [held_a, row_swap(send_a, 1), held_b, x_swap(send_b)]

    def third(self, after):
        parts = run(
            third_sum_kernel,
            [shape((1, *self.tail))] * self.high,
            self.held,
            scalars=0,
            limit=self.small,
            after=after,
        )
        self.held = [parts[0]] + [row_swap(parts[m], 2 * m) for m in range(1, self.high)]

    def last(self, after):
        (total,) = run(
            sum_kernel,
            [shape((1, *self.tail))],
            self.held,
            scalars=0,
            limit=self.small,
            after=after,
        )
        return total


class PlainSum:
    def __init__(self, mine, other):
        self.held = lax.all_to_all(mine + core_swap(other), ("rows", "x"), 0, 0, tiled=True)

    def second(self, after):
        pass

    def third(self, after):
        pass

    def last(self, after):
        return jnp.sum(self.held, axis=0, keepdims=True)


def spread(total):
    if lax.axis_size("x") == 2:
        beside = x_swap(total)
        return total, beside, core_swap(total), core_swap(beside)
    total = lax.all_gather(total, "x", axis=0, tiled=True)
    beyond = core_swap(total)
    return total, total, beyond, beyond


def body(
    image_in,
    condition,
    group_counts,
    out_cotangent,
    power_vectors,
    conv1_weight,
    conv2_weight,
    skip_weight,
    cond_weight,
    out_bias,
    conv1_first,
    conv2_first,
    skip_first,
    cond_first,
    bias_first,
    conv1_second,
    conv2_second,
    skip_second,
    cond_second,
    bias_second,
):
    rows_n = lax.axis_size("rows")
    n_x = lax.axis_size("x")
    groups_n = 2 * n_x
    masters = [conv1_weight, conv2_weight, skip_weight, cond_weight, out_bias]
    s = Sizes(
        image_in.shape, out_cotangent.shape, condition.shape, [m.shape for m in masters], rows_n, n_x
    )
    bind = functools.partial
    scratch = pltpu.VMEM
    n, w = s.images, s.width
    depth = 3 * s.slot

    pay, half_one, half_two, near, far, left_one, left_two, left_skip = run(
        bind(prep_kernel, s),
        [
            shape((s.devices, 1, s.pay_one)),
            shape((s.pack_one, LANES), BF16),
            shape((s.pack_two, LANES), BF16),
            shape((n, 3 * w, LANES), BF16),
            shape((n, 3 * w, LANES), BF16),
            shape((1, s.n_one)),
            shape((1, s.n_two)),
            shape((s.n_skip, 1)),
        ],
        [
            group_counts,
            image_in,
            condition,
            power_vectors,
            conv1_weight.T,
            conv2_weight.T,
            skip_weight,
            cond_weight.T,
            out_bias[None],
        ],
        [scratch((1, s.pay_one), F32)],
    )
    blocks = gather_upper(half_one)
    got_one = share(pay)
    near, far = row_swaps(near, far)
    acts, proj, stats_one, spec, near_cot, far_cot = run(
        bind(act_kernel, s),
        [
            shape((n, s.rows + 2, w, 4 * s.chan), BF16),
            shape((n, rows_n * s.cols)),
            shape((2, s.chan)),
            shape((16, s.slot)),
            *[shape((n, 6 * w, LANES), BF16)] * 2,
        ],
        [group_counts, got_one, image_in, near, far],
        [
            *[scratch((n, 2, 2 * w, s.out), BF16)] * 2,
            pltpu.SemaphoreType.DMA((2,)),
        ],
        whole=[out_cotangent],
    )
    high = rows_n // 2
    near_one, half_two = run(
        bind(stack_kernel, s),
        [shape((high, s.pack_one, LANES), BF16), shape(half_two.shape, BF16)],
        [half_two, *blocks],
        scalars=0,
        after=[acts],
    )
    far_one = row_swap(near_one, 1)
    far_one, near_two = lax.optimization_barrier((far_one, jnp.stack(gather_upper(half_two))))
    blocks_one = near_one, far_one, core_swap(near_one), core_swap(far_one)

    far_two = row_swap(near_two, 1)
    near_cot, far_cot = row_swaps(near_cot, far_cot)
    hidden, weight_one, pay = run(
        bind(conv_one_kernel, s),
        [
            shape((n, s.ext, 2, w, s.out)),
            shape((9 * s.chan, s.out), BF16),
            shape((s.devices, 1, s.pay_two)),
        ],
        [group_counts, acts, *blocks_one],
        [scratch((1, s.pay_two), F32), scratch((9 * s.chan, s.out), F32)],
        flops=2 * n * s.ext * 2 * w * 9 * s.chan * s.out,
    )
    far_two, pay = lax.optimization_barrier((far_two, pay))
    blocks_two = near_two, far_two, core_swap(near_two), core_swap(far_two)
    got_two = share(pay)
    dact, phases, grad_low, grad_skip, skip_part, weight_two, weight_skip, misc = run(
        bind(cot_kernel, s),
        [
            shape((n, s.ext, 2, w, s.out)),
            shape((n, 2 * s.rows, 2, w, s.out), BF16),
            shape((n, 2 * s.rows, 2, w, s.out), BF16),
            shape((n, s.rows, w, s.out), BF16),
            shape((n, s.rows, w, s.out)),
            shape((3, depth, s.out), BF16),
            shape((s.chan, s.out), BF16),
            shape((8, s.slot)),
        ],
        [group_counts, out_cotangent, near_cot, far_cot, image_in, *blocks_two, spec],
        [
            scratch((n, 2 * s.rows + 4, w, 4 * s.slot), BF16),
            scratch((9 * s.out + s.chan, s.out), F32),
            scratch((2, 2 * w, LANES), F32),
            scratch((3, depth, s.out), BF16),
        ],
        flops=2 * n * s.ext * 2 * w * 9 * s.out * s.out,
    )
    slots_two, dnorm, stats_two, terms_two, pay = run(
        bind(norm_two_kernel, s),
        [
            shape((n, s.ext, w, 4 * s.slot), BF16),
            shape((n, s.ext, 2, w, s.out)),
            shape((2, s.slot)),
            shape((8, 2 * s.slot)),
            shape((s.devices, 1, s.pay_two)),
        ],
        [group_counts, got_two, hidden, dact, spec, proj],
        [scratch((1, s.pay_two), F32)],
    )
    got_three = share(pay)
    slots_one, mine, other, scale_one = run(
        bind(hidden_grad_kernel, s),
        [
            shape((n, 2, s.rows + 1, w, 4 * s.slot), BF16),
            *[shape((s.rows_n * n_x, s.grad_one + s.grad_two + s.grad_skip, LANES))] * 2,
            shape((8, s.slot)),
        ],
        [
            group_counts,
            got_three,
            dnorm,
            hidden,
            stats_two,
            spec,
            acts,
            slots_two,
            grad_low,
            grad_skip,
            image_in,
        ],
        [
            scratch((2, 2, n, s.rows, w, s.out), BF16),
            scratch((s.out, 9 * s.chan), F32),
            scratch((s.out, 9 * s.out + s.chan), F32),
        ],
        flops=8 * n * s.rows * w * 9 * s.chan * s.out,
    )
    sums = (StagedSum if n_x == 2 else PlainSum)(mine, other)
    out_image, scale_two = run(
        bind(conv_two_kernel, s),
        [shape(out_cotangent.shape, BF16), shape((8, LANES))],
        [slots_two, weight_two, phases, skip_part, spec],
        [scratch((2, 2 * w, LANES), F32)],
        scalars=0,
        after=[scale_one],
        flops=8 * n * s.rows * 2 * w * 9 * s.out * s.out,
    )
    dnorm_one, pay = run(
        bind(input_grad_kernel, s),
        [shape((n, s.rows, w, s.chan)), shape((s.devices, 1, s.pay_four))],
        [slots_one, weight_one, image_in, stats_one, proj, terms_two, scale_one, scale_two, misc, condition],
        [
            scratch((3, depth, s.chan), BF16),
            scratch((8, rows_n * s.cols), F32),
            scratch((1, s.pay_four), F32),
        ],
        scalars=0,
        flops=8 * n * s.rows * w * 9 * s.chan * s.out,
    )
    sums.second([pay])
    got_four = share(pay)
    sums.third([got_four])
    moments = [cond_weight, cond_first, cond_second]
    biases = [out_bias, bias_first, bias_second]
    image_grad, *rest, scales = run(
        bind(finish_kernel, s),
        [
            shape(image_in.shape),
            *[shape((s.cols, s.cond))] * 3,
            *[shape((1, s.n_bias))] * 3,
            shape((8, LANES)),
        ],
        [
            group_counts,
            got_four,
            image_in,
            dnorm_one,
            grad_skip,
            weight_skip,
            stats_one,
            proj,
            *[m.T for m in moments],
            *[b[None] for b in biases],
        ],
        [
            scratch((groups_n * n, s.cols), F32),
            scratch((groups_n * n, s.cond), F32),
        ],
    )
    parts = spread(sums.last([scales]))
    cond_new = [c.T for c in rest[:3]]
    bias_new = [b[0] for b in rest[3:]]
    olds = [
        *[m.T for m in (conv1_weight, conv1_first, conv1_second)],
        *[m.T for m in (conv2_weight, conv2_first, conv2_second)],
        skip_weight,
        skip_first,
        skip_second,
    ]
    news = run(
        bind(weights_kernel, s),
        [shape(o.shape) for o in olds],
        [*parts, scales, spec, left_one, left_two, left_skip, *olds],
        [scratch((s.out, k), F32) for k in (s.n_one, s.n_two, s.n_skip)],
        scalars=0,
    )
    weights_new = [m.T for m in news[:6]] + list(news[6:])
    return (out_image, image_grad, *weights_new, *cond_new, *bias_new)


def solution(mesh):
    rows_n, imgs_n = mesh.devices.shape
    fine = Mesh(np.asarray(mesh.devices).reshape(rows_n, imgs_n // 2, 2), ALL)
    groups = ("x", "core")
    picture = P(groups, "rows", None, None)
    weight = P("rows", None)
    column = P(None, "rows")
    masters = (weight, weight, weight, column, P("rows"))
    return jax.shard_map(
        body,
        mesh=fine,
        in_specs=(picture, P(groups, None), P(), picture, P(), *masters, *masters, *masters),
        out_specs=(
            picture,
            picture,
            *(weight,) * 9,
            *(column,) * 3,
            *(P("rows"),) * 3,
        ),
        check_vma=False,
    )
```

```python
import functools

import jax
import jax.numpy as jnp
import numpy as np
from jax import lax
from jax.experimental import pallas as pl
from jax.experimental.pallas import tpu as pltpu
from jax.sharding import Mesh
from jax.sharding import PartitionSpec as P

STEP = 10
precise = lax.Precision.HIGHEST
NORM_EPS = 1e-05
BETA_ONE = 0.9
BETA_TWO = 0.999
ADAM_EPS = 1e-08
DECAY_RATE = 0.01
LEARN_RATES = (0.02, 0.02, 0.05, 0.03, 0.15)
ALL = ("rows", "x", "core")
F32, BF16 = jnp.float32, jnp.bfloat16
LANES = 128
VMEM_LIMIT = 56 * 2**20


def shape(dims, kind=F32):
    return jax.ShapeDtypeStruct(tuple(dims), kind)


def run(kernel, outs, args, scratch=(), scalars=1, flops=0, limit=VMEM_LIMIT, whole=(), results=()):
    spec = pl.BlockSpec(memory_space=pltpu.VMEM)
    specs = [pl.BlockSpec(memory_space=pltpu.SMEM)] * scalars + [spec] * (len(args) - scalars)
    specs += [pl.BlockSpec(memory_space=pl.ANY)] * len(whole)
    moved = sum(a.size * a.dtype.itemsize for a in args)
    args = [*args, *whole]
    scratch = [pltpu.VMEM(a.shape, a.dtype) for a in (*whole, *results)] + list(scratch)
    out_specs = [spec] * len(outs) + [pl.BlockSpec(memory_space=pl.ANY)] * len(results)
    outs = [*outs, *results]
    moved += sum(np.prod(o.shape) * np.dtype(o.dtype).itemsize for o in outs)
    return pl.pallas_call(
        kernel,
        out_shape=tuple(outs),
        in_specs=specs,
        out_specs=tuple(out_specs),
        scratch_shapes=scratch,
        cost_estimate=pl.CostEstimate(
            flops=int(flops), bytes_accessed=int(moved), transcendentals=0
        ),
        compiler_params=pltpu.CompilerParams(vmem_limit_bytes=limit),
    )(*args)


def round_up(value, step):
    return -(-value // step) * step


class Sizes:
    def __init__(self, image, cot, condition, masters, rows_n, n_x):
        self.images, self.rows, self.width, self.chan = image
        self.out = cot[3]
        self.slot = round_up(self.out, LANES)
        self.ext = 2 * self.rows + 2
        self.cond = condition[1]
        self.n_one, self.n_two, self.n_skip = masters[0][0], masters[1][0], masters[2][0]
        self.cols = masters[3][1]
        self.n_bias = masters[4][0]
        self.rows_n, self.groups = rows_n, 2 * n_x
        self.devices = rows_n * self.groups
        self.h_one = round_up(-(-self.n_one // 2), 8)
        self.h_two = round_up(-(-self.n_two // 2), 8)
        self.h_skip = round_up(-(-self.n_skip // 2), 8)
        self.pack_one = round_up(packed_rows(self.h_one), 16)
        self.pack_two = round_up(packed_rows(self.h_two + self.h_skip), 16)
        self.at_power = 2 * self.chan
        self.at_norm = self.at_power + 3 * self.out
        self.at_bias = self.at_norm + 8
        self.at_proj = round_up(self.at_bias + self.n_bias, LANES)
        self.pay_one = round_up(self.at_proj + self.images * self.cols, LANES)
        self.pay_two = round_up(2 * self.out, LANES)
        self.at_scale = 2 * self.chan
        self.at_gbias = self.at_scale + HALF
        self.at_terms = self.at_gbias + self.out
        self.pay_four = round_up(self.at_terms + self.images * self.cols, LANES)
        self.part = self.out // 2 // n_x
        self.n_x = n_x
        self.wide = self.n_one + self.n_two + self.n_skip
        self.pitch = round_up(self.wide, LANES)
        self.grad_rows = grad_rows(self.part, self.wide)


HALF = LANES // 2


def from_row(near, far, row):
    row_pos = lax.axis_index("rows")
    at = (row_pos // 2) ^ (row // 2)
    same = lax.rem(row_pos, 2) == row % 2
    return jnp.where(same, near[at].astype(F32), far[at].astype(F32))


def packed_rows(rows):
    return rows + round_up(-(-rows // 2), 8)


def pack(values):
    rows = values.shape[0]
    h = round_up(-(-rows // 2), 8)
    right = values[:, LANES:]
    return jnp.concatenate(
        [values[:, :LANES], jnp.concatenate([right[:h], right[rows - h :]], axis=1)], axis=0
    )


def unpack(values, rows):
    h = round_up(-(-rows // 2), 8)
    right = values[rows : rows + h]
    low = jnp.concatenate([right[:, :HALF], right[2 * h - rows :, HALF:]], axis=0)
    return jnp.concatenate([values[:rows], low], axis=1)


def grad_rows(part, width):
    tail = width % LANES
    rows = part * (width // LANES)
    if tail:
        rows += part // 2 if tail <= HALF and part % 16 == 0 else part
    return rows


def pack_grad(ref, lead, grads, here, begin, width):
    part = here.size
    full = width // LANES
    for k in range(full):
        at = begin + k * LANES
        ref[lead, k * part : (k + 1) * part, :] = grads[here, at : at + LANES]
    tail = width - full * LANES
    if not tail:
        return
    at = full * part
    rest = grads[here, begin + full * LANES : begin + (full + 1) * LANES]
    if tail <= HALF and part % 16 == 0:
        h = part // 2
        ref[lead, at : at + h, :] = jnp.concatenate([rest[:h, :HALF], rest[h:, :HALF]], axis=1)
    else:
        ref[lead, at : at + part, :] = rest


def unpack_grad(values, at, part, width):
    full = width // LANES
    pieces = [values[at + k * part : at + (k + 1) * part] for k in range(full)]
    at += full * part
    tail = width - full * LANES
    if tail and tail <= HALF and part % 16 == 0:
        h = part // 2
        both = values[at : at + h]
        pieces.append(
            jnp.concatenate([both[:, :tail], both[:, HALF : HALF + tail]], axis=0)
        )
    elif tail:
        pieces.append(values[at : at + part, :tail])
    return pieces[0] if len(pieces) == 1 else jnp.concatenate(pieces, axis=1)


def position():
    return lax.axis_index("rows"), lax.axis_index("x"), lax.axis_index("core")


def group_position():
    return lax.axis_index("x") * lax.axis_size("core") + lax.axis_index("core")


def live_of(counts, image):
    return jnp.where(image < counts[group_position()], 1.0, 0.0).astype(F32)


def live_total(counts, sizes):
    total = counts[0]
    for g in range(1, sizes.groups):
        total = total + counts[g]
    return total.astype(F32)


def inside(row, sizes, scale):
    at = lax.axis_index("rows") * (scale * sizes.rows) + row
    return jnp.where((at >= 0) & (at < scale * sizes.rows * sizes.rows_n), 1.0, 0.0).astype(F32)


def start(source, target, sem):
    copy = pltpu.make_async_copy(source, target, sem)
    copy.start()
    return copy


def sigmoid(values):
    return 1.0 / (1.0 + jnp.exp(-values))


def shifted(values, step):
    width = values.shape[0]
    rolled = pltpu.roll(values, (-step) % width, 0)
    where = lax.broadcasted_iota(jnp.int32, values.shape, 0)
    edge = 0 if step < 0 else width - 1
    return jnp.where(where == edge, 0.0, rolled)


def dot(a, b, dims=((1,), (0,)), precision=None):
    return lax.dot_general(a, b, (dims, ((), ())), preferred_element_type=F32, precision=precision)


def prep_kernel(sizes, counts, image, cond, vec, one_t, two_t, skip, cond_t, bias,
                pay, half_one, half_two, near, far, left_one, left_two,
                left_skip, line):
    s = sizes
    row_pos, _, core = position()
    even = lax.rem(row_pos, 2) == 0
    last, w = s.rows - 1, s.width

    line[...] = jnp.zeros_like(line)
    vec_t = jnp.transpose(jnp.concatenate([vec[...], jnp.zeros((5, s.out), F32)], axis=0))

    def power(k, low):
        column = jnp.sum(low * vec[k : k + 1, :], axis=1, keepdims=True)
        row = jnp.sum(low * column, axis=0, keepdims=True)
        at = s.at_power + k * s.out
        line[0:1, at : at + s.out] = row
        at = s.at_norm + k
        line[0:1, at : at + 1] = jnp.sum(column * column, axis=0, keepdims=True)
        return column

    low_t = one_t[...].astype(BF16).astype(F32)
    left_one[...] = jnp.sum(low_t * vec_t[:, 0:1], axis=0, keepdims=True)
    low = jnp.transpose(low_t)
    power(0, low)
    n, h = s.n_one, s.h_one
    packed_one = pack(jnp.where(core == 0, low[:h], low[n - h :]))
    low_t = two_t[...].astype(BF16).astype(F32)
    left_two[...] = jnp.sum(low_t * vec_t[:, 1:2], axis=0, keepdims=True)
    low = jnp.transpose(low_t)
    power(1, low)
    n, h = s.n_two, s.h_two
    half_a = jnp.where(core == 0, low[:h], low[n - h :])
    low = skip[...].astype(BF16).astype(F32)
    left_skip[...] = power(2, low)
    n, h = s.n_skip, s.h_skip
    half_b = jnp.where(core == 0, low[:h], low[n - h :])
    packed = pack(jnp.concatenate([half_a, half_b], axis=0))
    if s.pack_two > packed.shape[0]:
        packed = jnp.concatenate(
            [packed, jnp.zeros((s.pack_two - packed.shape[0], LANES), F32)], axis=0
        )
    packed = packed.astype(BF16)
    half_two[...] = packed
    line[0:1, s.at_bias : s.at_bias + s.n_bias] = bias[...].astype(BF16).astype(F32)
    proj = dot(cond[...], cond_t[...].astype(BF16), ((1,), (1,)))
    for b in range(s.images):
        at = s.at_proj + b * s.cols
        line[0:1, at : at + s.cols] = proj[b : b + 1]
    if s.pack_one > packed_one.shape[0]:
        packed_one = jnp.concatenate(
            [packed_one, jnp.zeros((s.pack_one - packed_one.shape[0], LANES), F32)], axis=0
        )
    half_one[...] = packed_one.astype(BF16)

    def edges(ref, row):
        for t in range(3):
            ref[:, t * w : (t + 1) * w, :] = image[:, row, :, t * LANES : (t + 1) * LANES]

    @pl.when(even)
    def _():
        edges(near, last)
        edges(far, 0)

    @pl.when(jnp.logical_not(even))
    def _():
        edges(near, 0)
        edges(far, last)

    sums = jnp.zeros((8, s.chan), F32)
    squares = jnp.zeros((8, s.chan), F32)
    for b in range(s.images):
        part = jnp.zeros((8, s.chan), F32)
        part_sq = jnp.zeros((8, s.chan), F32)
        for i in range(s.rows):
            x = image[b, i].astype(F32).reshape(w // 8, 8, s.chan)
            part += jnp.sum(x, axis=0)
            part_sq += jnp.sum(x * x, axis=0)
        sums += part * live_of(counts, b)
        squares += part_sq * live_of(counts, b)
    line[0:1, : s.chan] = jnp.sum(sums, axis=0, keepdims=True)
    line[0:1, s.chan : 2 * s.chan] = jnp.sum(squares, axis=0, keepdims=True)
    whole = line[...]
    for d in range(s.devices):
        pay[d] = whole


def act_kernel(sizes, counts, got, image, near, far, cot, slots, proj, stats, spec,
               near_cot, far_cot, rows, sems):
    s = sizes
    row_pos, _, _ = position()
    even = lax.rem(row_pos, 2) == 0
    copies = [
        start(cot.at[:, pl.ds(at, 2)], rows.at[:, pl.ds(at, 2)], sems.at[k])
        for k, at in enumerate(sorted({0, 2 * s.rows - 2}))
    ]
    group = group_position()
    sums = jnp.sum(got[:, :, : 2 * s.chan], axis=0)
    count = live_total(counts, s) * (s.width * s.width)
    mean = sums[:, : s.chan] / count
    rstd = lax.rsqrt(sums[:, s.chan :] / count - mean * mean + NORM_EPS)
    stats[0:1, :] = mean
    stats[1:2, :] = rstd

    spec[...] = jnp.zeros_like(spec)
    total = None
    for r in range(s.rows_n):
        piece = got[r * s.groups + group, :, s.at_power :]
        part = piece[:, : s.at_proj - s.at_power]
        total = part if total is None else total + part
        at = s.at_bias - s.at_power
        spec[6:7, r * s.n_bias : (r + 1) * s.n_bias] = piece[:, at : at + s.n_bias]
        for b in range(s.images):
            at = s.at_proj - s.at_power + b * s.cols
            proj[b : b + 1, r * s.cols : (r + 1) * s.cols] = piece[:, at : at + s.cols]
    for k in range(3):
        at = s.at_norm - s.at_power + k
        inv_norm = lax.rsqrt(total[:, at : at + 1])
        row = total[:, k * s.out : (k + 1) * s.out] * inv_norm
        inv_sigma = lax.rsqrt(jnp.sum(row * row, axis=1, keepdims=True))
        spec[k : k + 1, : s.out] = row * inv_sigma
        spec[3 + k : 4 + k, :] = jnp.broadcast_to(inv_sigma, (1, s.slot))
        spec[8 + k : 9 + k, :] = jnp.broadcast_to(inv_norm, (1, s.slot))

    w = s.width

    def one(b, e, x, keep):
        gain = 1.0 + proj[pl.ds(b, 1), : s.chan]
        shift = proj[pl.ds(b, 1), s.chan : 2 * s.chan]
        pre = gain * ((x - mean) * rstd) + shift
        act = pre * sigmoid(pre)
        if keep is not None:
            act = act * keep
        low = act.astype(BF16)
        slots[b, e, :, s.chan : 2 * s.chan] = low
        slots[b, e, :, 2 * s.chan : 3 * s.chan] = low
        slots[b, e, :, : s.chan] = shifted(act, -1).astype(BF16)
        slots[b, e, :, 3 * s.chan :] = shifted(act, 1).astype(BF16)

    def edge(ref, b):
        return jnp.concatenate(
            [ref[b, t * w : (t + 1) * w, :].astype(F32) for t in range(3)], axis=1
        )

    @pl.loop(0, s.images)
    def _(b):
        a, c = edge(near, b), edge(far, b)
        one(b, 0, jnp.where(even, c, a), inside(-1, s, 1))
        for i in range(s.rows):
            one(b, i + 1, image[b, i].astype(F32), None)
        one(b, s.rows + 1, jnp.where(even, a, c), inside(s.rows, s, 1))

    for copy in copies:
        copy.wait()

    def cot_edges(ref, row):
        for b in range(s.images):
            for k in range(2):
                ref[b, 2 * w * k : 2 * w * (k + 1), :] = rows[b, row + k, :, :LANES]
            right = [rows[b, row + k, :, LANES:].astype(F32) for k in range(2)]
            ref[b, 4 * w :, :] = jnp.concatenate(right, axis=1).astype(BF16)

    @pl.when(even)
    def _():
        cot_edges(near_cot, 2 * s.rows - 2)
        cot_edges(far_cot, 0)

    @pl.when(jnp.logical_not(even))
    def _():
        cot_edges(near_cot, 0)
        cot_edges(far_cot, 2 * s.rows - 2)


def conv_one_kernel(sizes, counts, slots, mine_near, mine_far, other_near, other_far, hidden, weight, pay, line, wide):
    s = sizes
    _, _, core = position()
    first = core == 0
    for r in range(s.rows_n):
        a = unpack(from_row(mine_near, mine_far, r), s.h_one)
        b = unpack(from_row(other_near, other_far, r), s.h_one)
        at = r * s.n_one
        wide[at : at + s.h_one, :] = jnp.where(first, a, b)
        at += s.n_one - s.h_one
        wide[at : at + s.h_one, :] = jnp.where(first, b, a)
    for t in range(9):
        weight[t * s.chan : (t + 1) * s.chan] = wide[t * s.chan : (t + 1) * s.chan, :].astype(BF16)
    depth = 3 * s.chan
    rows = s.rows + 1
    sums = jnp.zeros((8, s.out), F32)
    squares = jnp.zeros((8, s.out), F32)
    for phase in range(4):
        a, b = divmod(phase, 2)
        total = None
        for dy in range(3):
            at = (a + dy - 1) // 2 + 1 - a
            lhs = slots[:, at : at + rows, :, b * s.chan : b * s.chan + depth]
            part = dot(
                lhs.reshape(s.images * rows * s.width, depth),
                weight[dy * depth : (dy + 1) * depth, :],
            )
            total = part if total is None else total + part
        total = total.reshape(s.images, rows, s.width, s.out)
        for i in range(s.images):
            part = jnp.zeros((8, s.out), F32)
            part_sq = jnp.zeros((8, s.out), F32)
            for k in range(rows):
                e = 2 * k + 1 - a
                value = total[i, k]
                hidden[i, e, b] = value
                if 0 < e < s.ext - 1:
                    x = value.reshape(s.width // 8, 8, s.out)
                    part += jnp.sum(x, axis=0)
                    part_sq += jnp.sum(x * x, axis=0)
            sums += part * live_of(counts, i)
            squares += part_sq * live_of(counts, i)
    line[...] = jnp.zeros_like(line)
    line[0:1, : s.out] = jnp.sum(sums, axis=0, keepdims=True)
    line[0:1, s.out : 2 * s.out] = jnp.sum(squares, axis=0, keepdims=True)
    whole = line[...]
    for d in range(s.devices):
        pay[d] = whole


def cot_kernel(sizes, counts, cot, near, far, image, mine_near, mine_far, other_near, other_far, spec, dact, phases, grad_low,
               grad_skip, skip_part, two, skip_w, misc, slots, wide, pair, flip):
    s = sizes
    row_pos, _, core = position()
    even = lax.rem(row_pos, 2) == 0
    first = core == 0
    w = s.width
    for r in range(s.rows_n):
        a = unpack(from_row(mine_near, mine_far, r), s.h_two + s.h_skip)
        b = unpack(from_row(other_near, other_far, r), s.h_two + s.h_skip)
        lo, hi = jnp.where(first, a, b), jnp.where(first, b, a)
        at = r * s.n_two
        wide[at : at + s.h_two, :] = lo[: s.h_two]
        at += s.n_two - s.h_two
        wide[at : at + s.h_two, :] = hi[: s.h_two]
        at = 9 * s.out + r * s.n_skip
        wide[at : at + s.h_skip, :] = lo[s.h_two :]
        at += s.n_skip - s.h_skip
        wide[at : at + s.h_skip, :] = hi[s.h_two :]
    two[...] = jnp.zeros_like(two)
    flip[...] = jnp.zeros_like(flip)
    for t in range(9):
        dy, dx = divmod(t, 3)
        tap = wide[t * s.out : (t + 1) * s.out, :]
        two[dy, dx * s.slot : dx * s.slot + s.out, :] = tap.astype(BF16)
        back = jnp.transpose(tap).astype(BF16)
        flip[2 - dy, (2 - dx) * s.slot : (2 - dx) * s.slot + s.out, :] = back
    skip_w[...] = wide[9 * s.out : 9 * s.out + s.chan, :].astype(BF16)

    slots[...] = jnp.zeros_like(slots)
    inv_two = spec[4:5, : s.out]
    inv_skip = spec[5:6, : s.out]

    def split(b, q, row, own):
        pair[0] = row[:, :LANES]
        pair[1, :, : s.out - LANES] = row[:, LANES:]
        both = []
        for ph in range(2):
            value = jnp.concatenate(
                [pair[0, pl.ds(ph, w, 2), :], pair[1, pl.ds(ph, w, 2), :][:, : s.out - LANES]],
                axis=1,
            )
            low = (value * inv_two).astype(BF16)
            both.append(value)
            if own is not None:
                phases[b, own, ph] = value.astype(BF16)
                grad_low[b, own, ph] = low
            at = (1 + ph) * s.slot
            slots[b, q, :, at : at + s.out] = low
            if ph == 1:
                slots[b, q, :, : s.out] = shifted(low.astype(F32), -1).astype(BF16)
            else:
                slots[b, q, :, 3 * s.slot : 3 * s.slot + s.out] = shifted(
                    low.astype(F32), 1
                ).astype(BF16)
        return both[0] + both[1]

    def edge_row(ref, b, k):
        right = ref[b, 4 * w :, :].astype(F32)
        return jnp.concatenate(
            [
                ref[b, 2 * w * k : 2 * w * (k + 1), :].astype(F32),
                right[:, k * HALF : k * HALF + s.out - LANES],
            ],
            axis=1,
        )

    misc[...] = jnp.zeros_like(misc)

    @pl.loop(0, s.images)
    def _(b):
        live = live_of(counts, b)
        above = inside(-1, s, 1) * live
        below = inside(s.rows, s, 1) * live
        for k in range(2):
            a, c = edge_row(near, b, k), edge_row(far, b, k)
            split(b, k, jnp.where(even, c, a) * above, None)
            split(b, 2 * s.rows + 2 + k, jnp.where(even, a, c) * below, None)
        bias = jnp.zeros((1, s.out), F32)
        skip_sum = jnp.zeros((1, s.out), F32)
        for i in range(s.rows):
            pooled = split(b, 2 * i + 2, cot[b, 2 * i].astype(F32) * live, 2 * i)
            pooled += split(b, 2 * i + 3, cot[b, 2 * i + 1].astype(F32) * live, 2 * i + 1)
            grad_skip[b, i] = (pooled * inv_skip).astype(BF16)
            bias += jnp.sum(pooled, axis=0, keepdims=True)
            raw = dot(image[b, i], skip_w[...])
            skip_part[b, i] = raw * inv_skip
            skip_sum += jnp.sum(pooled * raw, axis=0, keepdims=True)
        misc[0:1, : s.out] += bias
        misc[1:2, : s.out] += skip_sum

    depth = 3 * s.slot
    for ph in range(2):
        total = None
        for dy in range(3):
            lhs = slots[:, dy : dy + s.ext, :, ph * s.slot : ph * s.slot + depth]
            part = dot(lhs.reshape(s.images * s.ext * w, depth), flip[dy])
            total = part if total is None else total + part
        dact[:, :, ph] = total.reshape(s.images, s.ext, w, s.out)


def norm_two_kernel(sizes, counts, got, spec, proj, hidden_from, dact_from, stats, terms, pay,
                    slots_to, dnorm_to, hidden, dact, slots, dnorm, line, sems):
    s = sizes
    w = s.width
    for b in range(s.images):
        start(hidden_from.at[b], hidden.at[b], sems.at[0, b])
        start(dact_from.at[b], dact.at[b], sems.at[1, b])
    inv = spec[3:4, : s.out]
    sums = jnp.sum(got[...], axis=0)
    count = live_total(counts, s) * (4 * w * w)
    mean = sums[:, : s.out] * inv / count
    square = sums[:, s.out : 2 * s.out] * inv * inv / count
    rstd = lax.rsqrt(square - mean * mean + NORM_EPS)
    stats[0:1, : s.out] = mean
    stats[1:2, : s.out] = rstd
    scale = inv * rstd
    offset = mean * rstd
    slots[...] = jnp.zeros_like(slots)
    base = 2 * s.chan

    def one(b, e, keep):
        gain = 1.0 + proj[pl.ds(b, 1), base : base + s.out]
        shift = proj[pl.ds(b, 1), base + s.out : base + 2 * s.out]
        dsum = jnp.zeros((8, s.out), F32)
        dgain = jnp.zeros((8, s.out), F32)
        for ph in range(2):
            normed = hidden[b, e, ph] * scale - offset
            pre = gain * normed + shift
            sig = sigmoid(pre)
            act = pre * sig
            if keep is not None:
                act = act * keep
            at = (1 + ph) * s.slot
            slots[b, e, :, at : at + s.out] = act.astype(BF16)
            if ph == 1:
                slots[b, e, :, : s.out] = shifted(act, -1).astype(BF16)
            else:
                slots[b, e, :, 3 * s.slot : 3 * s.slot + s.out] = shifted(act, 1).astype(BF16)
            dpre = dact[b, e, ph] * (sig * (1.0 + pre * (1.0 - sig)))
            dnorm[b, e, ph] = gain * dpre
            if keep is None:
                dsum += jnp.sum(dpre.reshape(w // 8, 8, s.out), axis=0)
                dgain += jnp.sum((dpre * normed).reshape(w // 8, 8, s.out), axis=0)
        return dsum, dgain

    terms[...] = jnp.zeros_like(terms)

    def sent(b):
        return [
            pltpu.make_async_copy(slots.at[b], slots_to.at[b], sems.at[2, b]),
            pltpu.make_async_copy(dnorm.at[b], dnorm_to.at[b], sems.at[3, b]),
        ]

    @pl.loop(0, s.images)
    def _(b):
        pltpu.make_async_copy(hidden_from.at[b], hidden.at[b], sems.at[0, b]).wait()
        pltpu.make_async_copy(dact_from.at[b], dact.at[b], sems.at[1, b]).wait()
        one(b, 0, inside(-1, s, 2))
        dsum = jnp.zeros((8, s.out), F32)
        dgain = jnp.zeros((8, s.out), F32)
        for e in range(1, s.ext - 1):
            a, c = one(b, e, None)
            dsum += a
            dgain += c
        one(b, s.ext - 1, inside(2 * s.rows, s, 2))
        terms[pl.ds(b, 1), : s.out] = jnp.sum(dgain, axis=0, keepdims=True)
        terms[pl.ds(b, 1), s.out : 2 * s.out] = jnp.sum(dsum, axis=0, keepdims=True)
        for copy in sent(b):
            copy.start()

    total = jnp.zeros((1, s.out), F32)
    cross = jnp.zeros((1, s.out), F32)
    for b in range(s.images):
        gain = 1.0 + proj[b : b + 1, base : base + s.out]
        cross += gain * terms[b : b + 1, : s.out]
        total += gain * terms[b : b + 1, s.out : 2 * s.out]
    line[...] = jnp.zeros_like(line)
    line[0:1, : s.out] = total
    line[0:1, s.out : 2 * s.out] = cross
    whole = line[...]
    for d in range(s.devices):
        pay[d] = whole
    for b in range(s.images):
        for copy in sent(b):
            copy.wait()


def conv_two_kernel(sizes, slots, two, phases, skip_part, spec, out, scale, pair):
    s = sizes
    w = s.width
    depth = 3 * s.slot
    own = 2 * s.rows
    inv_two = spec[4:5, : s.out]
    bias = spec[6:7, : s.out]
    dots = jnp.zeros((1, s.out), F32)
    results = []
    for ph in range(2):
        total = None
        for dy in range(3):
            lhs = slots[:, dy : dy + own, :, ph * s.slot : ph * s.slot + depth]
            part = dot(lhs.reshape(s.images * own * w, depth), two[dy])
            total = part if total is None else total + part
        results.append(total.reshape(s.images, own, w, s.out))
    for b in range(s.images):
        for e in range(own):
            for ph in range(2):
                raw = results[ph][b, e]
                dots += jnp.sum(raw * phases[b, e, ph].astype(F32), axis=0, keepdims=True)
                value = raw * inv_two + skip_part[b, e // 2] + bias
                pair[0, pl.ds(ph, w, 2), :] = value[:, :LANES]
                pair[1, pl.ds(ph, w, 2), :] = jnp.concatenate(
                    [value[:, LANES:], jnp.zeros((w, 2 * LANES - s.out), F32)], axis=1
                )
            out[b, e, :, :LANES] = pair[0].astype(BF16)
            out[b, e, :, LANES:] = pair[1][:, : s.out - LANES].astype(BF16)
    scale[...] = jnp.broadcast_to(jnp.sum(dots, axis=1, keepdims=True), scale.shape)


def place(s, grads, values, first, shard, offset):
    end = first + values.shape[1]
    for r in range(first // shard, (end - 1) // shard + 1):
        low, high = max(first, r * shard), min(end, (r + 1) * shard)
        at = r * s.pitch + offset + low - r * shard
        grads[:, at : at + high - low] = values[:, low - first : high - first]


def grads_two(s, slots, grad_low, grad_skip, image, grads):
    w = s.width
    own = 2 * s.rows
    depth = 3 * s.slot
    count = s.images * own * w
    flips = [jnp.transpose(grad_low[:, :, ph].reshape(count, s.out)) for ph in range(2)]
    for dy in range(3):
        total = None
        for ph in range(2):
            rhs = slots[:, dy : dy + own, :, ph * s.slot : ph * s.slot + depth]
            part = dot(flips[ph], rhs.reshape(count, depth))
            total = part if total is None else total + part
        for dx in range(3):
            tap = total[:, dx * s.slot : dx * s.slot + s.out]
            place(s, grads, tap, (3 * dy + dx) * s.out, s.n_two, s.n_one)
    count = s.images * s.rows * w
    flip = jnp.transpose(grad_skip[...].reshape(count, s.out))
    place(s, grads, dot(flip, image[...].reshape(count, s.chan)), 0, s.n_skip, s.n_one + s.n_two)


def hidden_grad_kernel(sizes, counts, got, stats, spec, grad_skip, image,
                       dnorm_from, hidden_from, acts_from, slots_two_from, grad_low_from,
                       scale, other_to, mine_to, slots_to,
                       dnorm, hidden, acts, slots_two, grad_low, other, mine, slots,
                       low, grads, sems):
    s = sizes
    _, _, core = position()
    w = s.width
    for b in range(s.images):
        start(hidden_from.at[b], hidden.at[b], sems.at[0, b])
        start(dnorm_from.at[b], dnorm.at[b], sems.at[1, b])
    fetch_acts = start(acts_from, acts, sems.at[3, 0])
    fetch_two = [
        start(slots_two_from, slots_two, sems.at[3, 1]),
        start(grad_low_from, grad_low, sems.at[3, 2]),
    ]
    sums = jnp.sum(got[...], axis=0)
    count = live_total(counts, s) * (4 * w * w)
    mean, rstd = stats[0:1, : s.out], stats[1:2, : s.out]
    inv = spec[3:4, : s.out]
    total = sums[:, : s.out] / count
    cross = sums[:, s.out : 2 * s.out] / count
    slots[...] = jnp.zeros_like(slots)
    norm_scale = inv * rstd
    offset = mean * rstd

    def one(b, e, keep, own):
        par, k = e % 2, e // 2
        dots = jnp.zeros((8, s.out), F32)
        for ph in range(2):
            raw = hidden[b, e, ph]
            normed = raw * norm_scale - offset
            grad = keep * (rstd * (dnorm[b, e, ph] - total - normed * cross))
            if own:
                dots += jnp.sum((grad * raw).reshape(w // 8, 8, s.out), axis=0)
            value = grad * inv
            small = value.astype(BF16)
            at = (1 + ph) * s.slot
            slots[b, par, k, :, at : at + s.out] = small
            if own:
                low[1 - par, ph, b, (e - 1) // 2] = small
            if ph == 1:
                slots[b, par, k, :, : s.out] = shifted(value, -1).astype(BF16)
            else:
                slots[b, par, k, :, 3 * s.slot : 3 * s.slot + s.out] = shifted(value, 1).astype(
                    BF16
                )
        return dots

    scale[...] = jnp.zeros_like(scale)

    def sent(b):
        return pltpu.make_async_copy(slots.at[b], slots_to.at[b], sems.at[2, b])

    @pl.loop(0, s.images)
    def _(b):
        pltpu.make_async_copy(hidden_from.at[b], hidden.at[b], sems.at[0, b]).wait()
        pltpu.make_async_copy(dnorm_from.at[b], dnorm.at[b], sems.at[1, b]).wait()
        live = live_of(counts, b)
        one(b, 0, live * inside(-1, s, 2), False)
        dots = jnp.zeros((8, s.out), F32)
        for e in range(1, s.ext - 1):
            dots += one(b, e, live, True)
        one(b, s.ext - 1, live * inside(2 * s.rows, s, 2), False)
        scale[0:1, : s.out] += jnp.sum(dots, axis=0, keepdims=True)
        sent(b).start()

    fetch_acts.wait()
    count = s.images * s.rows * w
    depth = 3 * s.chan
    for dy in range(3):
        total = None
        for phase in range(4):
            a, b = divmod(phase, 2)
            flip = jnp.transpose(low[a, b].reshape(count, s.out))
            first = 1 + (a + dy - 1) // 2
            rhs = acts[:, first : first + s.rows, :, b * s.chan : b * s.chan + depth]
            part = dot(flip, rhs.reshape(count, depth))
            total = part if total is None else total + part
        place(s, grads, total, dy * depth, s.n_one, 0)
    for copy in fetch_two:
        copy.wait()
    grads_two(s, slots_two, grad_low, grad_skip, image, grads)
    copies = []
    for ref, to, which in ((other, other_to, 1 - core), (mine, mine_to, core)):
        for x in range(s.n_x):
            at = pl.multiple_of((which * s.n_x + x) * s.part, 8)
            here = pl.ds(at, s.part)
            for r in range(s.rows_n):
                pack_grad(ref, r * s.n_x + x, grads, here, r * s.pitch, s.wide)
        copies.append(start(ref, to, sems.at[4, len(copies)]))
    for b in range(s.images):
        copies.append(sent(b))
    for copy in copies:
        copy.wait()


def input_grad_kernel(sizes, slots, weight, image, stats, proj, terms_two, scale_one, scale_two,
                      misc, dnorm, pay, back, terms, line):
    s = sizes
    w = s.width
    depth = 3 * s.slot
    back[...] = jnp.zeros_like(back)
    for t in range(9):
        dy, dx = divmod(t, 3)
        tap = weight[t * s.chan : (t + 1) * s.chan, :].astype(F32)
        at = (2 - dx) * s.slot
        back[dy, at : at + s.out, :] = jnp.transpose(tap).astype(BF16)
    total = None
    for a in range(2):
        for dy in range(3):
            par, k = (a + 2 - dy) % 2, (a + 2 - dy) // 2
            for ph in range(2):
                lhs = slots[:, par, k : k + s.rows, :, ph * s.slot : ph * s.slot + depth]
                part = dot(lhs.reshape(s.images * s.rows * w, depth), back[dy])
                total = part if total is None else total + part
    total = total.reshape(s.images, s.rows, w, s.chan)
    mean, rstd = stats[0:1, :], stats[1:2, :]
    all_sum = jnp.zeros((1, s.chan), F32)
    all_cross = jnp.zeros((1, s.chan), F32)
    for b in range(s.images):
        gain = 1.0 + proj[b : b + 1, : s.chan]
        shift = proj[b : b + 1, s.chan : 2 * s.chan]
        dsum = jnp.zeros((8, s.chan), F32)
        dgain = jnp.zeros((8, s.chan), F32)
        for i in range(s.rows):
            normed = (image[b, i].astype(F32) - mean) * rstd
            pre = gain * normed + shift
            sig = sigmoid(pre)
            dpre = total[b, i] * (sig * (1.0 + pre * (1.0 - sig)))
            dnorm[b, i] = gain * dpre
            dsum += jnp.sum(dpre.reshape(w // 8, 8, s.chan), axis=0)
            dgain += jnp.sum((dpre * normed).reshape(w // 8, 8, s.chan), axis=0)
        dsum = jnp.sum(dsum, axis=0, keepdims=True)
        dgain = jnp.sum(dgain, axis=0, keepdims=True)
        terms[b : b + 1, : s.chan] = dgain
        terms[b : b + 1, s.chan : 2 * s.chan] = dsum
        terms[b : b + 1, 2 * s.chan :] = terms_two[b : b + 1, : 2 * s.out]
        all_sum += gain * dsum
        all_cross += gain * dgain
    line[...] = jnp.zeros_like(line)
    line[0:1, : s.chan] = all_sum
    line[0:1, s.chan : 2 * s.chan] = all_cross
    at = s.at_scale
    line[0:1, at : at + 1] = jnp.sum(scale_one[0:1, : s.out], axis=1, keepdims=True)
    line[0:1, at + 1 : at + 2] = scale_two[0:1, 0:1]
    line[0:1, at + 2 : at + 3] = jnp.sum(misc[1:2, : s.out], axis=1, keepdims=True)
    at = s.at_gbias
    line[0:1, at : at + s.out] = misc[0:1, : s.out]
    for r in range(s.rows_n):
        for b in range(s.images):
            at = s.at_terms + b * s.cols
            line[0:1, at : at + s.cols] = terms[b : b + 1, r * s.cols : (r + 1) * s.cols]
        whole = line[...]
        for g in range(s.groups):
            pay[r * s.groups + g] = whole


def adamw(weight, first_old, second, gradient, learn_rate):
    first_new = BETA_ONE * first_old + (1.0 - BETA_ONE) * gradient
    second_new = BETA_TWO * second + (1.0 - BETA_TWO) * gradient * gradient
    first_hat = first_new / (1.0 - BETA_ONE**STEP)
    second_hat = second_new / (1.0 - BETA_TWO**STEP)
    weight_new = weight - learn_rate * (
        first_hat / (jnp.sqrt(second_hat) + ADAM_EPS) + DECAY_RATE * weight
    )
    return (weight_new, first_new, second_new)


def store_adamw(refs, olds, gradient, rate):
    for ref, value in zip(refs, adamw(*(old[...] for old in olds), gradient, rate)):
        ref[...] = value


def finish_kernel(sizes, counts, got, cond_all, image, dnorm, grad_skip, skip_w, stats, proj,
                  cw, cm, cv, bw, bm, bv,
                  image_grad, cw_new, cm_new, cv_new, bw_new, bm_new, bv_new, scales, terms, conds):
    s = sizes
    w = s.width
    row_pos, _, _ = position()
    sums = jnp.sum(got[:, :, : s.at_terms], axis=0)
    scales[...] = jnp.broadcast_to(sums[:, s.at_scale : s.at_scale + LANES], scales.shape)
    count = live_total(counts, s) * (w * w)
    total = sums[:, : s.chan] / count
    cross = sums[:, s.chan : 2 * s.chan] / count
    mean, rstd = stats[0:1, :], stats[1:2, :]
    grad = dot(
        grad_skip[...].reshape(s.images * s.rows * w, s.out), skip_w[...], ((1,), (1,))
    ).reshape(s.images, s.rows, w, s.chan)
    for b in range(s.images):
        keep = live_of(counts, b) * rstd
        for i in range(s.rows):
            normed = (image[b, i].astype(F32) - mean) * rstd
            image_grad[b, i] = keep * (dnorm[b, i] - total - normed * cross) + grad[b, i]
    for g in range(s.groups):
        part = got[g, :, s.at_terms :]
        for r in range(1, s.rows_n):
            part = part + got[r * s.groups + g, :, s.at_terms :]
        for b in range(s.images):
            k = g * s.images + b
            terms[k : k + 1, :] = part[:, b * s.cols : (b + 1) * s.cols]
            conds[k : k + 1, :] = cond_all[g, b : b + 1, :].astype(F32)
    grad = dot(terms[...], conds[...], ((0,), (0,)), precise)
    store_adamw((cw_new, cm_new, cv_new), (cw, cm, cv), grad, LEARN_RATES[3])
    grad = sums[:, s.at_gbias : s.at_gbias + s.n_bias]
    for r in range(1, s.rows_n):
        at = s.at_gbias + r * s.n_bias
        grad = jnp.where(row_pos == r, sums[:, at : at + s.n_bias], grad)
    store_adamw((bw_new, bm_new, bv_new), (bw, bm, bv), grad, LEARN_RATES[4])


def weights_kernel(sizes, own, beside, beyond, across, scales, spec, left_one, left_two, left_skip,
                   ow, om, ov, tw, tm, tv, sw, sm, sv,
                   ow_new, om_new, ov_new, tw_new, tm_new, tv_new, sw_new, sm_new, sv_new, grads):
    s = sizes
    _, x_pos, core = position()
    columns = jnp.transpose(spec[...])

    def factor(k):
        inv = spec[3 + k : 4 + k, 0:1]
        return scales[0:1, k : k + 1] * inv * inv * spec[8 + k : 9 + k, 0:1]

    def place(parts, which):
        for x, part in enumerate(parts):
            at = pl.multiple_of((which * s.n_x + x) * s.part, 8)
            here = pl.ds(at, s.part)
            grads[here, : s.wide] = unpack_grad(part, 0, s.part, s.wide)

    def ordered(mine, other):
        if s.n_x != 2:
            return [mine[x] for x in range(s.n_x)]
        a, b = mine[0], other[0]
        return [jnp.where(x_pos == 0, a, b), jnp.where(x_pos == 0, b, a)]

    place(ordered(own, beside), core)
    place(ordered(beyond, across), 1 - core)

    grad = grads[:, : s.n_one] - columns[: s.out, 0:1] * (left_one[...] * factor(0))
    store_adamw((ow_new, om_new, ov_new), (ow, om, ov), grad, LEARN_RATES[0])
    grad = grads[:, s.n_one : s.n_one + s.n_two] - columns[: s.out, 1:2] * (left_two[...] * factor(1))
    store_adamw((tw_new, tm_new, tv_new), (tw, tm, tv), grad, LEARN_RATES[1])
    grad = jnp.transpose(grads[:, s.n_one + s.n_two : s.wide])
    grad = grad - (left_skip[...] * factor(2)) * spec[2:3, : s.out]
    store_adamw((sw_new, sm_new, sv_new), (sw, sm, sv), grad, LEARN_RATES[2])


def share(chunks):
    return lax.all_to_all(chunks, ALL, 0, 0, tiled=True)


def core_swap(values):
    return lax.ppermute(values, "core", [(0, 1), (1, 0)])


def row_swaps(near, far):
    devices = lax.axis_size("rows")
    pairs = [(i, i ^ 1) for i in range(devices)]
    odd = [(i, i + 1) for i in range(1, devices - 1, 2)]
    odd = odd + [(j, i) for i, j in odd]
    return lax.ppermute(near, "rows", pairs), lax.ppermute(far, "rows", odd)


def row_swap(values, step):
    devices = lax.axis_size("rows")
    return lax.ppermute(values, "rows", [(i, i ^ step) for i in range(devices)])


def x_swap(values):
    return lax.ppermute(values, "x", [(0, 1), (1, 0)])


def gather_upper(block):
    return [block] + [row_swap(block, 2 * m) for m in range(1, lax.axis_size("rows") // 2)]


def gather_groups(values):
    if lax.axis_size("x") != 2:
        return lax.all_gather(values, ("x", "core"), axis=0)
    x, core = lax.axis_index("x"), lax.axis_index("core")
    pair = jnp.stack([values, core_swap(values)])
    pair = jnp.where(core == 0, pair, pair[::-1])
    both = jnp.stack([pair, x_swap(pair)])
    both = jnp.where(x == 0, both, both[::-1])
    return both.reshape(4, *values.shape)


def first_sum_kernel(mine, got, send_a, keep_a, send_b, keep_b):
    _, x, _ = position()
    low = lax.rem(lax.axis_index("rows"), 2)
    half = send_a.shape[0]
    for i in range(half):
        for k in range(2):
            send_a[i, k] = mine[i, k, 1 - x] + got[i, k, 1 - x]
            keep_a[i, k] = mine[i, k, x] + got[i, k, x]
            send_b[i, k] = mine[half + i, 1 - low, k] + got[half + i, 1 - low, k]
            keep_b[i, k] = mine[half + i, low, k] + got[half + i, low, k]


def second_sum_kernel(keep_a, got_a, keep_b, got_b, send_a, held_a, send_b, held_b):
    _, x, _ = position()
    low = lax.rem(lax.axis_index("rows"), 2)
    for i in range(keep_a.shape[0]):
        send_a[i] = keep_a[i, 1 - low] + got_a[i, 1 - low]
        held_a[i] = keep_a[i, low] + got_a[i, low]
        send_b[i] = keep_b[i, 1 - x] + got_b[i, 1 - x]
        held_b[i] = keep_b[i, x] + got_b[i, x]


def third_sum_kernel(held_a, got_a, held_b, got_b, *outs):
    high = lax.axis_index("rows") // 2
    half = held_a.shape[0]
    for m, out in enumerate(outs):
        at = high ^ m

        @pl.when(at < half)
        def _():
            out[0] = held_a[jnp.minimum(at, half - 1)] + got_a[jnp.minimum(at, half - 1)]

        @pl.when(at >= half)
        def _():
            at_b = jnp.maximum(at - half, 0)
            out[0] = held_b[at_b] + got_b[at_b]


def sum_kernel(*refs):
    *parts, out = refs
    total = parts[0][...]
    for part in parts[1:]:
        total = total + part[...]
    out[...] = total


def tied(values, after):
    return list(lax.optimization_barrier((tuple(values), tuple(after)))[0])


class StagedSum:
    small = 8 * 2**20

    def __init__(self, mine, other, after):
        self.high = lax.axis_size("rows") // 2
        self.tail = mine.shape[1:]
        mine = mine.reshape(self.high, 2, 2, *self.tail)
        got = core_swap(other).reshape(self.high, 2, 2, *self.tail)
        send_a, keep_a, send_b, keep_b = run(
            first_sum_kernel,
            [shape((self.high // 2, 2, *self.tail))] * 4,
            tied([mine, got], after),
            scalars=0,
            limit=self.small,
        )
        self.held = [keep_a, x_swap(send_a), keep_b, row_swap(send_b, 1)]

    def second(self, after):
        send_a, held_a, send_b, held_b = run(
            second_sum_kernel,
            [shape((self.high // 2, *self.tail))] * 4,
            tied(self.held, after),
            scalars=0,
            limit=self.small,
        )
        self.held = [held_a, row_swap(send_a, 1), held_b, x_swap(send_b)]

    def third(self, after):
        parts = run(
            third_sum_kernel,
            [shape((1, *self.tail))] * self.high,
            tied(self.held, after),
            scalars=0,
            limit=self.small,
        )
        self.held = [parts[0]] + [row_swap(parts[m], 2 * m) for m in range(1, self.high)]

    def last(self, after):
        (total,) = run(
            sum_kernel,
            [shape((1, *self.tail))],
            tied(self.held, after),
            scalars=0,
            limit=self.small,
        )
        return total


class PlainSum:
    def __init__(self, mine, other, after):
        self.held = lax.all_to_all(mine + core_swap(other), ("rows", "x"), 0, 0, tiled=True)

    def second(self, after):
        pass

    def third(self, after):
        pass

    def last(self, after):
        return jnp.sum(self.held, axis=0, keepdims=True)


def spread(total):
    if lax.axis_size("x") == 2:
        beside = x_swap(total)
        return total, beside, core_swap(total), core_swap(beside)
    total = lax.all_gather(total, "x", axis=0, tiled=True)
    beyond = core_swap(total)
    return total, total, beyond, beyond


def body(
    image_in,
    condition,
    group_counts,
    out_cotangent,
    power_vectors,
    conv1_weight,
    conv2_weight,
    skip_weight,
    cond_weight,
    out_bias,
    conv1_first,
    conv2_first,
    skip_first,
    cond_first,
    bias_first,
    conv1_second,
    conv2_second,
    skip_second,
    cond_second,
    bias_second,
):
    rows_n = lax.axis_size("rows")
    n_x = lax.axis_size("x")
    groups_n = 2 * n_x
    masters = [conv1_weight, conv2_weight, skip_weight, cond_weight, out_bias]
    s = Sizes(
        image_in.shape, out_cotangent.shape, condition.shape, [m.shape for m in masters], rows_n, n_x
    )
    bind = functools.partial
    scratch = pltpu.VMEM
    n, w = s.images, s.width
    depth = 3 * s.slot

    pay, half_one, half_two, near, far, left_one, left_two, left_skip = run(
        bind(prep_kernel, s),
        [
            shape((s.devices, 1, s.pay_one)),
            shape((s.pack_one, LANES), BF16),
            shape((s.pack_two, LANES), BF16),
            shape((n, 3 * w, LANES), BF16),
            shape((n, 3 * w, LANES), BF16),
            shape((1, s.n_one)),
            shape((1, s.n_two)),
            shape((s.n_skip, 1)),
        ],
        [
            group_counts,
            image_in,
            condition,
            power_vectors,
            conv1_weight.T,
            conv2_weight.T,
            skip_weight,
            cond_weight.T,
            out_bias[None],
        ],
        [scratch((1, s.pay_one), F32)],
        limit=60 * 2**20,
    )
    blocks = gather_upper(half_one)
    near, far = row_swaps(near, far)
    (pay,) = tied([pay], [near, far])
    got_one = share(pay)
    acts, proj, stats_one, spec, near_cot, far_cot = run(
        bind(act_kernel, s),
        [
            shape((n, s.rows + 2, w, 4 * s.chan), BF16),
            shape((n, rows_n * s.cols)),
            shape((2, s.chan)),
            shape((16, s.slot)),
            *[shape((n, 6 * w, LANES), BF16)] * 2,
        ],
        [group_counts, got_one, image_in, near, far],
        [pltpu.SemaphoreType.DMA((2,))],
        whole=[out_cotangent],
    )
    near_one = jnp.stack(blocks)
    (half_two,) = tied([half_two], [near_one])
    far_one = row_swap(near_one, 1)
    near_two = jnp.stack(gather_upper(half_two))
    far_one, near_two, acts = lax.optimization_barrier((far_one, near_two, acts))
    blocks_one = near_one, far_one, core_swap(near_one), core_swap(far_one)

    far_two = row_swap(near_two, 1)
    near_cot, far_cot = row_swaps(near_cot, far_cot)
    hidden, weight_one, pay = run(
        bind(conv_one_kernel, s),
        [
            shape((n, s.ext, 2, w, s.out)),
            shape((9 * s.chan, s.out), BF16),
            shape((s.devices, 1, s.pay_two)),
        ],
        [group_counts, acts, *blocks_one],
        [scratch((1, s.pay_two), F32), scratch((9 * s.chan, s.out), F32)],
        flops=2 * n * s.ext * 2 * w * 9 * s.chan * s.out,
    )
    far_two, near_cot, far_cot, pay = lax.optimization_barrier((far_two, near_cot, far_cot, pay))
    blocks_two = near_two, far_two, core_swap(near_two), core_swap(far_two)
    got_two = share(pay)
    dact, phases, grad_low, grad_skip, skip_part, weight_two, weight_skip, misc = run(
        bind(cot_kernel, s),
        [
            shape((n, s.ext, 2, w, s.out)),
            shape((n, 2 * s.rows, 2, w, s.out), BF16),
            shape((n, 2 * s.rows, 2, w, s.out), BF16),
            shape((n, s.rows, w, s.out), BF16),
            shape((n, s.rows, w, s.out)),
            shape((3, depth, s.out), BF16),
            shape((s.chan, s.out), BF16),
            shape((8, s.slot)),
        ],
        [group_counts, out_cotangent, near_cot, far_cot, image_in, *blocks_two, spec],
        [
            scratch((n, 2 * s.rows + 4, w, 4 * s.slot), BF16),
            scratch((9 * s.out + s.chan, s.out), F32),
            scratch((2, 2 * w, LANES), F32),
            scratch((3, depth, s.out), BF16),
        ],
        flops=2 * n * s.ext * 2 * w * 9 * s.out * s.out,
    )
    stats_two, terms_two, pay, slots_two, dnorm = run(
        bind(norm_two_kernel, s),
        [shape((2, s.slot)), shape((8, 2 * s.slot)), shape((s.devices, 1, s.pay_two))],
        [group_counts, got_two, spec, proj],
        [scratch((1, s.pay_two), F32), pltpu.SemaphoreType.DMA((4, n))],
        whole=[hidden, dact],
        results=[shape((n, s.ext, w, 4 * s.slot), BF16), shape((n, s.ext, 2, w, s.out))],
    )
    got_three = share(pay)
    sent = shape((s.rows_n * n_x, s.grad_rows, LANES))
    scale_one, other, mine, slots_one = run(
        bind(hidden_grad_kernel, s),
        [shape((8, s.slot))],
        [group_counts, got_three, stats_two, spec, grad_skip, image_in],
        [
            scratch((2, 2, n, s.rows, w, s.out), BF16),
            scratch((s.out, rows_n * s.pitch), F32),
            pltpu.SemaphoreType.DMA((5, max(n, 3))),
        ],
        flops=8 * n * s.rows * w * 9 * s.chan * s.out,
        whole=[dnorm, hidden, acts, slots_two, grad_low],
        results=[sent, sent, shape((n, 2, s.rows + 1, w, 4 * s.slot), BF16)],
        limit=48 * 2**20,
    )
    out_image, scale_two = run(
        bind(conv_two_kernel, s),
        [shape(out_cotangent.shape, BF16), shape((8, LANES))],
        tied([slots_two, weight_two, phases, skip_part, spec], [scale_one]),
        [scratch((2, 2 * w, LANES), F32)],
        scalars=0,
        flops=8 * n * s.rows * 2 * w * 9 * s.out * s.out,
        limit=48 * 2**20,
    )
    sums = (StagedSum if n_x == 2 else PlainSum)(mine, other, [scale_two])
    dnorm_one, pay = run(
        bind(input_grad_kernel, s),
        [shape((n, s.rows, w, s.chan)), shape((s.devices, 1, s.pay_four))],
        [slots_one, weight_one, image_in, stats_one, proj, terms_two, scale_one, scale_two, misc],
        [
            scratch((3, depth, s.chan), BF16),
            scratch((8, rows_n * s.cols), F32),
            scratch((1, s.pay_four), F32),
        ],
        scalars=0,
        flops=8 * n * s.rows * w * 9 * s.chan * s.out,
    )
    sums.second([pay])
    late_condition, pay = lax.optimization_barrier((condition, pay))
    cond_all = gather_groups(late_condition)
    got_four = share(pay)
    sums.third([got_four])
    moments = [cond_weight, cond_first, cond_second]
    biases = [out_bias, bias_first, bias_second]
    image_grad, *rest, scales = run(
        bind(finish_kernel, s),
        [
            shape(image_in.shape),
            *[shape((s.cols, s.cond))] * 3,
            *[shape((1, s.n_bias))] * 3,
            shape((8, LANES)),
        ],
        [
            group_counts,
            got_four,
            cond_all,
            image_in,
            dnorm_one,
            grad_skip,
            weight_skip,
            stats_one,
            proj,
            *[m.T for m in moments],
            *[b[None] for b in biases],
        ],
        [
            scratch((groups_n * n, s.cols), F32),
            scratch((groups_n * n, s.cond), F32),
        ],
        limit=60 * 2**20,
    )
    parts = spread(sums.last([scales]))
    cond_new = [c.T for c in rest[:3]]
    bias_new = [b[0] for b in rest[3:]]
    olds = [
        *[m.T for m in (conv1_weight, conv1_first, conv1_second)],
        *[m.T for m in (conv2_weight, conv2_first, conv2_second)],
        skip_weight,
        skip_first,
        skip_second,
    ]
    news = run(
        bind(weights_kernel, s),
        [shape(o.shape) for o in olds],
        [*parts, scales, spec, left_one, left_two, left_skip, *olds],
        [scratch((s.out, s.pitch), F32)],
        limit=24 * 2**20,
        scalars=0,
    )
    weights_new = [m.T for m in news[:6]] + list(news[6:])
    return (out_image, image_grad, *weights_new, *cond_new, *bias_new)


def solution(mesh):
    rows_n, imgs_n = mesh.devices.shape
    fine = Mesh(np.asarray(mesh.devices).reshape(rows_n, imgs_n // 2, 2), ALL)
    groups = ("x", "core")
    picture = P(groups, "rows", None, None)
    weight = P("rows", None)
    column = P(None, "rows")
    masters = (weight, weight, weight, column, P("rows"))
    return jax.shard_map(
        body,
        mesh=fine,
        in_specs=(picture, P(groups, None), P(), picture, P(), *masters, *masters, *masters),
        out_specs=(
            picture,
            picture,
            *(weight,) * 9,
            *(column,) * 3,
            *(P("rows"),) * 3,
        ),
        check_vma=False,
    )
```

```python
import functools

import jax
import jax.numpy as jnp
import numpy as np
from jax import lax
from jax.experimental import pallas as pl
from jax.experimental.pallas import tpu as pltpu
from jax.sharding import Mesh
from jax.sharding import PartitionSpec as P

STEP = 10
precise = lax.Precision.HIGHEST
NORM_EPS = 1e-05
BETA_ONE = 0.9
BETA_TWO = 0.999
ADAM_EPS = 1e-08
DECAY_RATE = 0.01
LEARN_RATES = (0.02, 0.02, 0.05, 0.03, 0.15)
ALL = ("rows", "x", "core")
F32, BF16 = jnp.float32, jnp.bfloat16
LANES = 128
VMEM_LIMIT = 56 * 2**20


def shape(dims, kind=F32):
    return jax.ShapeDtypeStruct(tuple(dims), kind)


def run(kernel, outs, args, scratch=(), scalars=1, flops=0, limit=VMEM_LIMIT, whole=(), results=(), idle=False):
    spec = pl.BlockSpec(memory_space=pltpu.VMEM)
    specs = [pl.BlockSpec(memory_space=pltpu.SMEM)] * scalars + [spec] * (len(args) - scalars)
    specs += [pl.BlockSpec(memory_space=pl.ANY)] * len(whole)
    moved = sum(a.size * a.dtype.itemsize for a in args)
    moved += sum(np.prod(o.shape) * np.dtype(o.dtype).itemsize for o in outs)
    args = [*args, *whole]
    if idle:
        moved = 0
    scratch = [pltpu.VMEM(a.shape, a.dtype) for a in (*whole, *results)] + list(scratch)
    out_specs = [spec] * len(outs) + [pl.BlockSpec(memory_space=pl.ANY)] * len(results)
    outs = [*outs, *results]
    return pl.pallas_call(
        kernel,
        out_shape=tuple(outs),
        in_specs=specs,
        out_specs=tuple(out_specs),
        scratch_shapes=scratch,
        cost_estimate=pl.CostEstimate(
            flops=int(flops), bytes_accessed=int(moved), transcendentals=0
        ),
        compiler_params=pltpu.CompilerParams(vmem_limit_bytes=limit),
    )(*args)


def round_up(value, step):
    return -(-value // step) * step


class Sizes:
    def __init__(self, image, cot, condition, masters, rows_n, n_x):
        self.images, self.rows, self.width, self.chan = image
        self.out = cot[3]
        self.slot = round_up(self.out, LANES)
        self.ext = 2 * self.rows + 2
        self.cond = condition[1]
        self.n_one, self.n_two, self.n_skip = masters[0][0], masters[1][0], masters[2][0]
        self.cols = masters[3][1]
        self.n_bias = masters[4][0]
        self.rows_n, self.groups = rows_n, 2 * n_x
        self.devices = rows_n * self.groups
        self.h_one = round_up(-(-self.n_one // 2), 8)
        self.h_two = round_up(-(-self.n_two // 2), 8)
        self.h_skip = round_up(-(-self.n_skip // 2), 8)
        self.pack_one = round_up(packed_rows(self.h_one), 16)
        self.pack_two = round_up(packed_rows(self.h_two + self.h_skip), 16)
        self.at_power = 2 * self.chan
        self.at_norm = self.at_power + 3 * self.out
        self.at_bias = self.at_norm + 8
        self.at_proj = round_up(self.at_bias + self.n_bias, LANES)
        self.pay_one = round_up(self.at_proj + self.images * self.cols, LANES)
        self.pay_two = round_up(2 * self.out, LANES)
        self.at_scale = 2 * self.chan
        self.at_gbias = self.at_scale + HALF
        self.at_terms = self.at_gbias + self.out
        self.pay_four = round_up(self.at_terms + self.images * self.cols, LANES)
        self.part = self.out // 2 // n_x
        self.n_x = n_x
        self.wide = self.n_one + self.n_two + self.n_skip
        self.pitch = round_up(self.wide, LANES)
        self.grad_rows = grad_rows(self.part, self.wide)


HALF = LANES // 2


def from_row(near, far, row):
    row_pos = lax.axis_index("rows")
    at = (row_pos // 2) ^ (row // 2)
    same = lax.rem(row_pos, 2) == row % 2
    return jnp.where(same, near[at].astype(F32), far[at].astype(F32))


def packed_rows(rows):
    return rows + round_up(-(-rows // 2), 8)


def pack(values):
    rows = values.shape[0]
    h = round_up(-(-rows // 2), 8)
    right = values[:, LANES:]
    return jnp.concatenate(
        [values[:, :LANES], jnp.concatenate([right[:h], right[rows - h :]], axis=1)], axis=0
    )


def unpack(values, rows):
    h = round_up(-(-rows // 2), 8)
    right = values[rows : rows + h]
    low = jnp.concatenate([right[:, :HALF], right[2 * h - rows :, HALF:]], axis=0)
    return jnp.concatenate([values[:rows], low], axis=1)


def grad_rows(part, width):
    tail = width % LANES
    rows = part * (width // LANES)
    if tail:
        rows += part // 2 if tail <= HALF and part % 16 == 0 else part
    return rows


def pack_grad(ref, lead, grads, here, begin, width):
    part = here.size
    full = width // LANES
    for k in range(full):
        at = begin + k * LANES
        ref[lead, k * part : (k + 1) * part, :] = grads[here, at : at + LANES]
    tail = width - full * LANES
    if not tail:
        return
    at = full * part
    rest = grads[here, begin + full * LANES : begin + (full + 1) * LANES]
    if tail <= HALF and part % 16 == 0:
        h = part // 2
        ref[lead, at : at + h, :] = jnp.concatenate([rest[:h, :HALF], rest[h:, :HALF]], axis=1)
    else:
        ref[lead, at : at + part, :] = rest


def unpack_grad(values, at, part, width):
    full = width // LANES
    pieces = [values[at + k * part : at + (k + 1) * part] for k in range(full)]
    at += full * part
    tail = width - full * LANES
    if tail and tail <= HALF and part % 16 == 0:
        h = part // 2
        both = values[at : at + h]
        pieces.append(
            jnp.concatenate([both[:, :tail], both[:, HALF : HALF + tail]], axis=0)
        )
    elif tail:
        pieces.append(values[at : at + part, :tail])
    return pieces[0] if len(pieces) == 1 else jnp.concatenate(pieces, axis=1)


def position():
    return lax.axis_index("rows"), lax.axis_index("x"), lax.axis_index("core")


def group_position():
    return lax.axis_index("x") * lax.axis_size("core") + lax.axis_index("core")


def live_of(counts, image):
    return jnp.where(image < counts[group_position()], 1.0, 0.0).astype(F32)


def live_total(counts, sizes):
    total = counts[0]
    for g in range(1, sizes.groups):
        total = total + counts[g]
    return total.astype(F32)


def inside(row, sizes, scale):
    at = lax.axis_index("rows") * (scale * sizes.rows) + row
    return jnp.where((at >= 0) & (at < scale * sizes.rows * sizes.rows_n), 1.0, 0.0).astype(F32)


def start(source, target, sem):
    copy = pltpu.make_async_copy(source, target, sem)
    copy.start()
    return copy


def sigmoid(values):
    return 1.0 / (1.0 + jnp.exp(-values))


def shifted(values, step):
    width = values.shape[0]
    rolled = pltpu.roll(values, (-step) % width, 0)
    where = lax.broadcasted_iota(jnp.int32, values.shape, 0)
    edge = 0 if step < 0 else width - 1
    return jnp.where(where == edge, 0.0, rolled)


def padded(values, size):
    rest = size - values.shape[1]
    if not rest:
        return values
    return jnp.concatenate([values, jnp.zeros((values.shape[0], rest), values.dtype)], axis=1)


def fill(ref, where, phase, value, slot):
    value = padded(value, slot)
    at = (1 + phase) * slot
    ref[(*where, slice(None), slice(at, at + slot))] = value.astype(BF16)
    step, at = (-1, 0) if phase else (1, 3 * slot)
    ref[(*where, slice(None), slice(at, at + slot))] = shifted(value, step).astype(BF16)


def dot(a, b, dims=((1,), (0,)), precision=None):
    return lax.dot_general(a, b, (dims, ((), ())), preferred_element_type=F32, precision=precision)


def prep_kernel(sizes, counts, image, cond, vec, one_t, two_t, skip, cond_t, bias,
                pay, half_one, half_two, near, far, left_one, left_two,
                left_skip, line):
    s = sizes
    row_pos, _, core = position()
    even = lax.rem(row_pos, 2) == 0
    last, w = s.rows - 1, s.width

    line[...] = jnp.zeros_like(line)
    vec_t = jnp.transpose(jnp.concatenate([vec[...], jnp.zeros((5, s.out), F32)], axis=0))

    def power(k, low):
        column = jnp.sum(low * vec[k : k + 1, :], axis=1, keepdims=True)
        row = jnp.sum(low * column, axis=0, keepdims=True)
        at = s.at_power + k * s.out
        line[0:1, at : at + s.out] = row
        at = s.at_norm + k
        line[0:1, at : at + 1] = jnp.sum(column * column, axis=0, keepdims=True)
        return column

    low_t = one_t[...].astype(BF16).astype(F32)
    left_one[...] = jnp.sum(low_t * vec_t[:, 0:1], axis=0, keepdims=True)
    low = jnp.transpose(low_t)
    power(0, low)
    n, h = s.n_one, s.h_one
    packed_one = pack(jnp.where(core == 0, low[:h], low[n - h :]))
    low_t = two_t[...].astype(BF16).astype(F32)
    left_two[...] = jnp.sum(low_t * vec_t[:, 1:2], axis=0, keepdims=True)
    low = jnp.transpose(low_t)
    power(1, low)
    n, h = s.n_two, s.h_two
    half_a = jnp.where(core == 0, low[:h], low[n - h :])
    low = skip[...].astype(BF16).astype(F32)
    left_skip[...] = power(2, low)
    n, h = s.n_skip, s.h_skip
    half_b = jnp.where(core == 0, low[:h], low[n - h :])
    packed = pack(jnp.concatenate([half_a, half_b], axis=0))
    if s.pack_two > packed.shape[0]:
        packed = jnp.concatenate(
            [packed, jnp.zeros((s.pack_two - packed.shape[0], LANES), F32)], axis=0
        )
    packed = packed.astype(BF16)
    half_two[...] = packed
    line[0:1, s.at_bias : s.at_bias + s.n_bias] = bias[...].astype(BF16).astype(F32)
    proj = dot(cond[...], cond_t[...].astype(BF16), ((1,), (1,)))
    for b in range(s.images):
        at = s.at_proj + b * s.cols
        line[0:1, at : at + s.cols] = proj[b : b + 1]
    if s.pack_one > packed_one.shape[0]:
        packed_one = jnp.concatenate(
            [packed_one, jnp.zeros((s.pack_one - packed_one.shape[0], LANES), F32)], axis=0
        )
    half_one[...] = packed_one.astype(BF16)

    def edges(ref, row):
        for t in range(3):
            ref[:, t * w : (t + 1) * w, :] = image[:, row, :, t * LANES : (t + 1) * LANES]

    @pl.when(even)
    def _():
        edges(near, last)
        edges(far, 0)

    @pl.when(jnp.logical_not(even))
    def _():
        edges(near, 0)
        edges(far, last)

    sums = jnp.zeros((8, s.chan), F32)
    squares = jnp.zeros((8, s.chan), F32)
    for b in range(s.images):
        part = jnp.zeros((8, s.chan), F32)
        part_sq = jnp.zeros((8, s.chan), F32)
        for i in range(s.rows):
            x = image[b, i].astype(F32).reshape(w // 8, 8, s.chan)
            part += jnp.sum(x, axis=0)
            part_sq += jnp.sum(x * x, axis=0)
        sums += part * live_of(counts, b)
        squares += part_sq * live_of(counts, b)
    line[0:1, : s.chan] = jnp.sum(sums, axis=0, keepdims=True)
    line[0:1, s.chan : 2 * s.chan] = jnp.sum(squares, axis=0, keepdims=True)
    whole = line[...]
    for d in range(s.devices):
        pay[d] = whole


def act_kernel(sizes, counts, got, image, near, far, cot, slots, proj, stats, spec,
               near_cot, far_cot, rows, sems):
    s = sizes
    row_pos, _, _ = position()
    even = lax.rem(row_pos, 2) == 0
    copies = [
        start(cot.at[:, pl.ds(at, 2)], rows.at[:, pl.ds(at, 2)], sems.at[k])
        for k, at in enumerate(sorted({0, 2 * s.rows - 2}))
    ]
    group = group_position()
    sums = jnp.sum(got[:, :, : 2 * s.chan], axis=0)
    count = live_total(counts, s) * (s.width * s.width)
    mean = sums[:, : s.chan] / count
    rstd = lax.rsqrt(sums[:, s.chan :] / count - mean * mean + NORM_EPS)
    stats[0:1, :] = mean
    stats[1:2, :] = rstd

    spec[...] = jnp.zeros_like(spec)
    total = None
    for r in range(s.rows_n):
        piece = got[r * s.groups + group, :, s.at_power :]
        part = piece[:, : s.at_proj - s.at_power]
        total = part if total is None else total + part
        at = s.at_bias - s.at_power
        spec[6:7, r * s.n_bias : (r + 1) * s.n_bias] = piece[:, at : at + s.n_bias]
        for b in range(s.images):
            at = s.at_proj - s.at_power + b * s.cols
            proj[b : b + 1, r * s.cols : (r + 1) * s.cols] = piece[:, at : at + s.cols]
    for k in range(3):
        at = s.at_norm - s.at_power + k
        inv_norm = lax.rsqrt(total[:, at : at + 1])
        row = total[:, k * s.out : (k + 1) * s.out] * inv_norm
        inv_sigma = lax.rsqrt(jnp.sum(row * row, axis=1, keepdims=True))
        spec[k : k + 1, : s.out] = row * inv_sigma
        spec[3 + k : 4 + k, :] = jnp.broadcast_to(inv_sigma, (1, s.slot))
        spec[8 + k : 9 + k, :] = jnp.broadcast_to(inv_norm, (1, s.slot))

    w = s.width

    def one(b, e, x, keep):
        gain = 1.0 + proj[pl.ds(b, 1), : s.chan]
        shift = proj[pl.ds(b, 1), s.chan : 2 * s.chan]
        pre = gain * ((x - mean) * rstd) + shift
        act = pre * sigmoid(pre)
        if keep is not None:
            act = act * keep
        low = act.astype(BF16)
        slots[b, e, :, s.chan : 2 * s.chan] = low
        slots[b, e, :, 2 * s.chan : 3 * s.chan] = low
        slots[b, e, :, : s.chan] = shifted(act, -1).astype(BF16)
        slots[b, e, :, 3 * s.chan :] = shifted(act, 1).astype(BF16)

    def edge(ref, b):
        return jnp.concatenate(
            [ref[b, t * w : (t + 1) * w, :].astype(F32) for t in range(3)], axis=1
        )

    @pl.loop(0, s.images)
    def _(b):
        a, c = edge(near, b), edge(far, b)
        one(b, 0, jnp.where(even, c, a), inside(-1, s, 1))
        for i in range(s.rows):
            one(b, i + 1, image[b, i].astype(F32), None)
        one(b, s.rows + 1, jnp.where(even, a, c), inside(s.rows, s, 1))

    for copy in copies:
        copy.wait()

    def cot_edges(ref, row):
        for b in range(s.images):
            for k in range(2):
                ref[b, 2 * w * k : 2 * w * (k + 1), :] = rows[b, row + k, :, :LANES]
            right = [rows[b, row + k, :, LANES:].astype(F32) for k in range(2)]
            ref[b, 4 * w :, :] = jnp.concatenate(right, axis=1).astype(BF16)

    @pl.when(even)
    def _():
        cot_edges(near_cot, 2 * s.rows - 2)
        cot_edges(far_cot, 0)

    @pl.when(jnp.logical_not(even))
    def _():
        cot_edges(near_cot, 0)
        cot_edges(far_cot, 2 * s.rows - 2)


def conv_one_kernel(sizes, counts, slots, mine_near, mine_far, other_near, other_far, hidden, weight, pay, line, wide):
    s = sizes
    _, _, core = position()
    first = core == 0
    for r in range(s.rows_n):
        a = unpack(from_row(mine_near, mine_far, r), s.h_one)
        b = unpack(from_row(other_near, other_far, r), s.h_one)
        at = r * s.n_one
        wide[at : at + s.h_one, :] = jnp.where(first, a, b)
        at += s.n_one - s.h_one
        wide[at : at + s.h_one, :] = jnp.where(first, b, a)
    for t in range(9):
        weight[t * s.chan : (t + 1) * s.chan] = wide[t * s.chan : (t + 1) * s.chan, :].astype(BF16)
    depth = 3 * s.chan
    rows = s.rows + 1
    sums = jnp.zeros((8, s.out), F32)
    squares = jnp.zeros((8, s.out), F32)
    for phase in range(4):
        a, b = divmod(phase, 2)
        total = None
        for dy in range(3):
            at = (a + dy - 1) // 2 + 1 - a
            lhs = slots[:, at : at + rows, :, b * s.chan : b * s.chan + depth]
            part = dot(
                lhs.reshape(s.images * rows * s.width, depth),
                weight[dy * depth : (dy + 1) * depth, :],
            )
            total = part if total is None else total + part
        total = total.reshape(s.images, rows, s.width, s.out)
        for i in range(s.images):
            part = jnp.zeros((8, s.out), F32)
            part_sq = jnp.zeros((8, s.out), F32)
            for k in range(rows):
                e = 2 * k + 1 - a
                value = total[i, k]
                hidden[i, e, b] = value
                if 0 < e < s.ext - 1:
                    x = value.reshape(s.width // 8, 8, s.out)
                    part += jnp.sum(x, axis=0)
                    part_sq += jnp.sum(x * x, axis=0)
            sums += part * live_of(counts, i)
            squares += part_sq * live_of(counts, i)
    line[...] = jnp.zeros_like(line)
    line[0:1, : s.out] = jnp.sum(sums, axis=0, keepdims=True)
    line[0:1, s.out : 2 * s.out] = jnp.sum(squares, axis=0, keepdims=True)
    whole = line[...]
    for d in range(s.devices):
        pay[d] = whole


def cot_kernel(sizes, counts, cot, near, far, image, mine_near, mine_far, other_near, other_far, spec, dact, phases, grad_low,
               grad_skip, skip_part, two, skip_w, misc, slots, wide, pair, flip):
    s = sizes
    row_pos, _, core = position()
    even = lax.rem(row_pos, 2) == 0
    first = core == 0
    w = s.width
    for r in range(s.rows_n):
        a = unpack(from_row(mine_near, mine_far, r), s.h_two + s.h_skip)
        b = unpack(from_row(other_near, other_far, r), s.h_two + s.h_skip)
        lo, hi = jnp.where(first, a, b), jnp.where(first, b, a)
        at = r * s.n_two
        wide[at : at + s.h_two, :] = lo[: s.h_two]
        at += s.n_two - s.h_two
        wide[at : at + s.h_two, :] = hi[: s.h_two]
        at = 9 * s.out + r * s.n_skip
        wide[at : at + s.h_skip, :] = lo[s.h_two :]
        at += s.n_skip - s.h_skip
        wide[at : at + s.h_skip, :] = hi[s.h_two :]
    two[...] = jnp.zeros_like(two)
    flip[...] = jnp.zeros_like(flip)
    for t in range(9):
        dy, dx = divmod(t, 3)
        tap = wide[t * s.out : (t + 1) * s.out, :]
        two[dy, dx * s.slot : dx * s.slot + s.out, :] = tap.astype(BF16)
        back = jnp.transpose(tap).astype(BF16)
        flip[2 - dy, (2 - dx) * s.slot : (2 - dx) * s.slot + s.out, :] = back
    skip_w[...] = wide[9 * s.out : 9 * s.out + s.chan, :].astype(BF16)

    inv_two = spec[4:5, : s.out]
    inv_skip = spec[5:6, : s.out]

    def split(b, q, row, own):
        pair[0] = row[:, :LANES]
        pair[1, :, : s.out - LANES] = row[:, LANES:]
        both = []
        for ph in range(2):
            value = jnp.concatenate(
                [pair[0, pl.ds(ph, w, 2), :], pair[1, pl.ds(ph, w, 2), :][:, : s.out - LANES]],
                axis=1,
            )
            low = (value * inv_two).astype(BF16)
            both.append(value)
            if own is not None:
                phases[b, own, ph] = value.astype(BF16)
                grad_low[b, own, ph] = low
            fill(slots, (b, q), ph, low.astype(F32), s.slot)
        return both[0] + both[1]

    def edge_row(ref, b, k):
        right = ref[b, 4 * w :, :].astype(F32)
        return jnp.concatenate(
            [
                ref[b, 2 * w * k : 2 * w * (k + 1), :].astype(F32),
                right[:, k * HALF : k * HALF + s.out - LANES],
            ],
            axis=1,
        )

    misc[...] = jnp.zeros_like(misc)

    @pl.loop(0, s.images)
    def _(b):
        live = live_of(counts, b)
        above = inside(-1, s, 1) * live
        below = inside(s.rows, s, 1) * live
        for k in range(2):
            a, c = edge_row(near, b, k), edge_row(far, b, k)
            split(b, k, jnp.where(even, c, a) * above, None)
            split(b, 2 * s.rows + 2 + k, jnp.where(even, a, c) * below, None)
        bias = jnp.zeros((1, s.out), F32)
        skip_sum = jnp.zeros((1, s.out), F32)
        for i in range(s.rows):
            pooled = split(b, 2 * i + 2, cot[b, 2 * i].astype(F32) * live, 2 * i)
            pooled += split(b, 2 * i + 3, cot[b, 2 * i + 1].astype(F32) * live, 2 * i + 1)
            grad_skip[b, i] = (pooled * inv_skip).astype(BF16)
            bias += jnp.sum(pooled, axis=0, keepdims=True)
            raw = dot(image[b, i], skip_w[...])
            skip_part[b, i] = raw * inv_skip
            skip_sum += jnp.sum(pooled * raw, axis=0, keepdims=True)
        misc[0:1, : s.out] += bias
        misc[1:2, : s.out] += skip_sum

    depth = 3 * s.slot
    for ph in range(2):
        total = None
        for dy in range(3):
            lhs = slots[:, dy : dy + s.ext, :, ph * s.slot : ph * s.slot + depth]
            part = dot(lhs.reshape(s.images * s.ext * w, depth), flip[dy])
            total = part if total is None else total + part
        dact[:, :, ph] = total.reshape(s.images, s.ext, w, s.out)


def norm_two_kernel(sizes, counts, got, spec, proj, hidden_from, dact_from, stats, terms, pay,
                    slots_to, dnorm_to, hidden, dact, slots, dnorm, line, sems):
    s = sizes
    w = s.width
    for b in range(s.images):
        start(hidden_from.at[b], hidden.at[b], sems.at[0, b])
        start(dact_from.at[b], dact.at[b], sems.at[1, b])
    inv = spec[3:4, : s.out]
    sums = jnp.sum(got[...], axis=0)
    count = live_total(counts, s) * (4 * w * w)
    mean = sums[:, : s.out] * inv / count
    square = sums[:, s.out : 2 * s.out] * inv * inv / count
    rstd = lax.rsqrt(square - mean * mean + NORM_EPS)
    stats[0:1, : s.out] = mean
    stats[1:2, : s.out] = rstd
    scale = inv * rstd
    offset = mean * rstd
    base = 2 * s.chan

    def one(b, e, keep):
        gain = 1.0 + proj[pl.ds(b, 1), base : base + s.out]
        shift = proj[pl.ds(b, 1), base + s.out : base + 2 * s.out]
        dsum = jnp.zeros((8, s.out), F32)
        dgain = jnp.zeros((8, s.out), F32)
        for ph in range(2):
            normed = hidden[b, e, ph] * scale - offset
            pre = gain * normed + shift
            sig = sigmoid(pre)
            act = pre * sig
            if keep is not None:
                act = act * keep
            fill(slots, (b, e), ph, act, s.slot)
            dpre = dact[b, e, ph] * (sig * (1.0 + pre * (1.0 - sig)))
            dnorm[b, e, ph] = gain * dpre
            if keep is None:
                dsum += jnp.sum(dpre.reshape(w // 8, 8, s.out), axis=0)
                dgain += jnp.sum((dpre * normed).reshape(w // 8, 8, s.out), axis=0)
        return dsum, dgain

    terms[...] = jnp.zeros_like(terms)

    def sent(b):
        return [
            pltpu.make_async_copy(slots.at[b], slots_to.at[b], sems.at[2, b]),
            pltpu.make_async_copy(dnorm.at[b], dnorm_to.at[b], sems.at[3, b]),
        ]

    @pl.loop(0, s.images)
    def _(b):
        pltpu.make_async_copy(hidden_from.at[b], hidden.at[b], sems.at[0, b]).wait()
        pltpu.make_async_copy(dact_from.at[b], dact.at[b], sems.at[1, b]).wait()
        one(b, 0, inside(-1, s, 2))
        dsum = jnp.zeros((8, s.out), F32)
        dgain = jnp.zeros((8, s.out), F32)
        for e in range(1, s.ext - 1):
            a, c = one(b, e, None)
            dsum += a
            dgain += c
        one(b, s.ext - 1, inside(2 * s.rows, s, 2))
        terms[pl.ds(b, 1), : s.out] = jnp.sum(dgain, axis=0, keepdims=True)
        terms[pl.ds(b, 1), s.out : 2 * s.out] = jnp.sum(dsum, axis=0, keepdims=True)
        for copy in sent(b):
            copy.start()

    total = jnp.zeros((1, s.out), F32)
    cross = jnp.zeros((1, s.out), F32)
    for b in range(s.images):
        gain = 1.0 + proj[b : b + 1, base : base + s.out]
        cross += gain * terms[b : b + 1, : s.out]
        total += gain * terms[b : b + 1, s.out : 2 * s.out]
    line[...] = jnp.zeros_like(line)
    line[0:1, : s.out] = total
    line[0:1, s.out : 2 * s.out] = cross
    whole = line[...]
    for d in range(s.devices):
        pay[d] = whole
    for b in range(s.images):
        for copy in sent(b):
            copy.wait()


def conv_two_kernel(sizes, slots, two, phases, skip_part, spec, out, scale, pair):
    s = sizes
    w = s.width
    depth = 3 * s.slot
    own = 2 * s.rows
    inv_two = spec[4:5, : s.out]
    bias = spec[6:7, : s.out]
    dots = jnp.zeros((1, s.out), F32)
    results = []
    for ph in range(2):
        total = None
        for dy in range(3):
            lhs = slots[:, dy : dy + own, :, ph * s.slot : ph * s.slot + depth]
            part = dot(lhs.reshape(s.images * own * w, depth), two[dy])
            total = part if total is None else total + part
        results.append(total.reshape(s.images, own, w, s.out))
    for b in range(s.images):
        for e in range(own):
            for ph in range(2):
                raw = results[ph][b, e]
                dots += jnp.sum(raw * phases[b, e, ph].astype(F32), axis=0, keepdims=True)
                value = raw * inv_two + skip_part[b, e // 2] + bias
                pair[0, pl.ds(ph, w, 2), :] = value[:, :LANES]
                pair[1, pl.ds(ph, w, 2), :] = jnp.concatenate(
                    [value[:, LANES:], jnp.zeros((w, 2 * LANES - s.out), F32)], axis=1
                )
            out[b, e, :, :LANES] = pair[0].astype(BF16)
            out[b, e, :, LANES:] = pair[1][:, : s.out - LANES].astype(BF16)
    scale[...] = jnp.broadcast_to(jnp.sum(dots, axis=1, keepdims=True), scale.shape)


def place(s, grads, values, first, shard, offset):
    end = first + values.shape[1]
    for r in range(first // shard, (end - 1) // shard + 1):
        low, high = max(first, r * shard), min(end, (r + 1) * shard)
        at = r * s.pitch + offset + low - r * shard
        grads[:, at : at + high - low] = values[:, low - first : high - first]


def grads_two(s, slots, grad_low, grad_skip, image, grads):
    w = s.width
    own = 2 * s.rows
    depth = 3 * s.slot
    count = s.images * own * w
    flips = [jnp.transpose(grad_low[:, :, ph].reshape(count, s.out)) for ph in range(2)]
    for dy in range(3):
        total = None
        for ph in range(2):
            rhs = slots[:, dy : dy + own, :, ph * s.slot : ph * s.slot + depth]
            part = dot(flips[ph], rhs.reshape(count, depth))
            total = part if total is None else total + part
        for dx in range(3):
            tap = total[:, dx * s.slot : dx * s.slot + s.out]
            place(s, grads, tap, (3 * dy + dx) * s.out, s.n_two, s.n_one)
    count = s.images * s.rows * w
    flip = jnp.transpose(grad_skip[...].reshape(count, s.out))
    place(s, grads, dot(flip, image[...].reshape(count, s.chan)), 0, s.n_skip, s.n_one + s.n_two)


def hidden_grad_kernel(sizes, counts, got, stats, spec, grad_skip, image,
                       dnorm_from, hidden_from, acts_from, slots_two_from, grad_low_from,
                       scale, other_to, mine_to, slots_to,
                       dnorm, hidden, acts, slots_two, grad_low, other, mine, slots,
                       low, grads, sems):
    s = sizes
    _, _, core = position()
    w = s.width
    for b in range(s.images):
        start(hidden_from.at[b], hidden.at[b], sems.at[0, b])
        start(dnorm_from.at[b], dnorm.at[b], sems.at[1, b])
    fetch_acts = start(acts_from, acts, sems.at[3, 0])
    fetch_two = [
        start(slots_two_from, slots_two, sems.at[3, 1]),
        start(grad_low_from, grad_low, sems.at[3, 2]),
    ]
    sums = jnp.sum(got[...], axis=0)
    count = live_total(counts, s) * (4 * w * w)
    mean, rstd = stats[0:1, : s.out], stats[1:2, : s.out]
    inv = spec[3:4, : s.out]
    total = sums[:, : s.out] / count
    cross = sums[:, s.out : 2 * s.out] / count
    norm_scale = inv * rstd
    offset = mean * rstd

    def one(b, e, keep, own):
        par, k = e % 2, e // 2
        dots = jnp.zeros((8, s.out), F32)
        for ph in range(2):
            raw = hidden[b, e, ph]
            normed = raw * norm_scale - offset
            grad = keep * (rstd * (dnorm[b, e, ph] - total - normed * cross))
            if own:
                dots += jnp.sum((grad * raw).reshape(w // 8, 8, s.out), axis=0)
            value = grad * inv
            fill(slots, (b, par, k), ph, value, s.slot)
            if own:
                low[1 - par, ph, b, (e - 1) // 2] = value.astype(BF16)
        return dots

    scale[...] = jnp.zeros_like(scale)

    def sent(b):
        return pltpu.make_async_copy(slots.at[b], slots_to.at[b], sems.at[2, b])

    @pl.loop(0, s.images)
    def _(b):
        pltpu.make_async_copy(hidden_from.at[b], hidden.at[b], sems.at[0, b]).wait()
        pltpu.make_async_copy(dnorm_from.at[b], dnorm.at[b], sems.at[1, b]).wait()
        live = live_of(counts, b)
        one(b, 0, live * inside(-1, s, 2), False)
        dots = jnp.zeros((8, s.out), F32)
        for e in range(1, s.ext - 1):
            dots += one(b, e, live, True)
        one(b, s.ext - 1, live * inside(2 * s.rows, s, 2), False)
        scale[0:1, : s.out] += jnp.sum(dots, axis=0, keepdims=True)
        sent(b).start()

    fetch_acts.wait()
    count = s.images * s.rows * w
    depth = 3 * s.chan
    for dy in range(3):
        total = None
        for phase in range(4):
            a, b = divmod(phase, 2)
            flip = jnp.transpose(low[a, b].reshape(count, s.out))
            first = 1 + (a + dy - 1) // 2
            rhs = acts[:, first : first + s.rows, :, b * s.chan : b * s.chan + depth]
            part = dot(flip, rhs.reshape(count, depth))
            total = part if total is None else total + part
        place(s, grads, total, dy * depth, s.n_one, 0)
    for copy in fetch_two:
        copy.wait()
    grads_two(s, slots_two, grad_low, grad_skip, image, grads)
    copies = []
    for ref, to, which in ((other, other_to, 1 - core), (mine, mine_to, core)):
        for x in range(s.n_x):
            at = pl.multiple_of((which * s.n_x + x) * s.part, 8)
            here = pl.ds(at, s.part)
            for r in range(s.rows_n):
                pack_grad(ref, r * s.n_x + x, grads, here, r * s.pitch, s.wide)
        copies.append(start(ref, to, sems.at[4, len(copies)]))
    for b in range(s.images):
        copies.append(sent(b))
    for copy in copies:
        copy.wait()


def input_grad_kernel(sizes, slots, weight, image, stats, proj, terms_two, scale_one, scale_two,
                      misc, dnorm, pay, back, terms, line):
    s = sizes
    w = s.width
    depth = 3 * s.slot
    back[...] = jnp.zeros_like(back)
    for t in range(9):
        dy, dx = divmod(t, 3)
        tap = weight[t * s.chan : (t + 1) * s.chan, :].astype(F32)
        at = (2 - dx) * s.slot
        back[dy, at : at + s.out, :] = jnp.transpose(tap).astype(BF16)
    total = None
    for a in range(2):
        for dy in range(3):
            par, k = (a + 2 - dy) % 2, (a + 2 - dy) // 2
            for ph in range(2):
                lhs = slots[:, par, k : k + s.rows, :, ph * s.slot : ph * s.slot + depth]
                part = dot(lhs.reshape(s.images * s.rows * w, depth), back[dy])
                total = part if total is None else total + part
    total = total.reshape(s.images, s.rows, w, s.chan)
    mean, rstd = stats[0:1, :], stats[1:2, :]
    all_sum = jnp.zeros((1, s.chan), F32)
    all_cross = jnp.zeros((1, s.chan), F32)
    for b in range(s.images):
        gain = 1.0 + proj[b : b + 1, : s.chan]
        shift = proj[b : b + 1, s.chan : 2 * s.chan]
        dsum = jnp.zeros((8, s.chan), F32)
        dgain = jnp.zeros((8, s.chan), F32)
        for i in range(s.rows):
            normed = (image[b, i].astype(F32) - mean) * rstd
            pre = gain * normed + shift
            sig = sigmoid(pre)
            dpre = total[b, i] * (sig * (1.0 + pre * (1.0 - sig)))
            dnorm[b, i] = gain * dpre
            dsum += jnp.sum(dpre.reshape(w // 8, 8, s.chan), axis=0)
            dgain += jnp.sum((dpre * normed).reshape(w // 8, 8, s.chan), axis=0)
        dsum = jnp.sum(dsum, axis=0, keepdims=True)
        dgain = jnp.sum(dgain, axis=0, keepdims=True)
        terms[b : b + 1, : s.chan] = dgain
        terms[b : b + 1, s.chan : 2 * s.chan] = dsum
        terms[b : b + 1, 2 * s.chan :] = terms_two[b : b + 1, : 2 * s.out]
        all_sum += gain * dsum
        all_cross += gain * dgain
    line[...] = jnp.zeros_like(line)
    line[0:1, : s.chan] = all_sum
    line[0:1, s.chan : 2 * s.chan] = all_cross
    at = s.at_scale
    line[0:1, at : at + 1] = jnp.sum(scale_one[0:1, : s.out], axis=1, keepdims=True)
    line[0:1, at + 1 : at + 2] = scale_two[0:1, 0:1]
    line[0:1, at + 2 : at + 3] = jnp.sum(misc[1:2, : s.out], axis=1, keepdims=True)
    at = s.at_gbias
    line[0:1, at : at + s.out] = misc[0:1, : s.out]
    for r in range(s.rows_n):
        for b in range(s.images):
            at = s.at_terms + b * s.cols
            line[0:1, at : at + s.cols] = terms[b : b + 1, r * s.cols : (r + 1) * s.cols]
        whole = line[...]
        for g in range(s.groups):
            pay[r * s.groups + g] = whole


def adamw(weight, first_old, second, gradient, learn_rate):
    first_new = BETA_ONE * first_old + (1.0 - BETA_ONE) * gradient
    second_new = BETA_TWO * second + (1.0 - BETA_TWO) * gradient * gradient
    first_hat = first_new / (1.0 - BETA_ONE**STEP)
    second_hat = second_new / (1.0 - BETA_TWO**STEP)
    weight_new = weight - learn_rate * (
        first_hat / (jnp.sqrt(second_hat) + ADAM_EPS) + DECAY_RATE * weight
    )
    return (weight_new, first_new, second_new)


def store_adamw(refs, olds, gradient, rate):
    for ref, value in zip(refs, adamw(*(old[...] for old in olds), gradient, rate)):
        ref[...] = value


def finish_kernel(sizes, counts, got, cond_all, image, dnorm, grad_skip, skip_w, stats, proj,
                  cw, cm, cv, bw, bm, bv,
                  image_grad, cw_new, cm_new, cv_new, bw_new, bm_new, bv_new, scales, terms, conds):
    s = sizes
    w = s.width
    row_pos, _, _ = position()
    sums = jnp.sum(got[:, :, : s.at_terms], axis=0)
    scales[...] = jnp.broadcast_to(sums[:, s.at_scale : s.at_scale + LANES], scales.shape)
    count = live_total(counts, s) * (w * w)
    total = sums[:, : s.chan] / count
    cross = sums[:, s.chan : 2 * s.chan] / count
    mean, rstd = stats[0:1, :], stats[1:2, :]
    grad = dot(
        grad_skip[...].reshape(s.images * s.rows * w, s.out), skip_w[...], ((1,), (1,))
    ).reshape(s.images, s.rows, w, s.chan)
    for b in range(s.images):
        keep = live_of(counts, b) * rstd
        for i in range(s.rows):
            normed = (image[b, i].astype(F32) - mean) * rstd
            image_grad[b, i] = keep * (dnorm[b, i] - total - normed * cross) + grad[b, i]
    for g in range(s.groups):
        part = got[g, :, s.at_terms :]
        for r in range(1, s.rows_n):
            part = part + got[r * s.groups + g, :, s.at_terms :]
        for b in range(s.images):
            k = g * s.images + b
            terms[k : k + 1, :] = part[:, b * s.cols : (b + 1) * s.cols]
            conds[k : k + 1, :] = cond_all[g, b : b + 1, :].astype(F32)
    grad = dot(terms[...], conds[...], ((0,), (0,)), precise)
    store_adamw((cw_new, cm_new, cv_new), (cw, cm, cv), grad, LEARN_RATES[3])
    grad = sums[:, s.at_gbias : s.at_gbias + s.n_bias]
    for r in range(1, s.rows_n):
        at = s.at_gbias + r * s.n_bias
        grad = jnp.where(row_pos == r, sums[:, at : at + s.n_bias], grad)
    store_adamw((bw_new, bm_new, bv_new), (bw, bm, bv), grad, LEARN_RATES[4])


def weights_kernel(sizes, own, beside, beyond, across, scales, spec, left_one, left_two, left_skip,
                   ow, om, ov, tw, tm, tv, sw, sm, sv,
                   ow_new, om_new, ov_new, tw_new, tm_new, tv_new, sw_new, sm_new, sv_new, grads):
    s = sizes
    _, x_pos, core = position()
    columns = jnp.transpose(spec[...])

    def factor(k):
        inv = spec[3 + k : 4 + k, 0:1]
        return scales[0:1, k : k + 1] * inv * inv * spec[8 + k : 9 + k, 0:1]

    def place(parts, which):
        for x, part in enumerate(parts):
            at = pl.multiple_of((which * s.n_x + x) * s.part, 8)
            here = pl.ds(at, s.part)
            grads[here, : s.wide] = unpack_grad(part, 0, s.part, s.wide)

    def ordered(mine, other):
        if s.n_x != 2:
            return [mine[x] for x in range(s.n_x)]
        a, b = mine[0], other[0]
        return [jnp.where(x_pos == 0, a, b), jnp.where(x_pos == 0, b, a)]

    place(ordered(own, beside), core)
    place(ordered(beyond, across), 1 - core)

    grad = grads[:, : s.n_one] - columns[: s.out, 0:1] * (left_one[...] * factor(0))
    store_adamw((ow_new, om_new, ov_new), (ow, om, ov), grad, LEARN_RATES[0])
    grad = grads[:, s.n_one : s.n_one + s.n_two] - columns[: s.out, 1:2] * (left_two[...] * factor(1))
    store_adamw((tw_new, tm_new, tv_new), (tw, tm, tv), grad, LEARN_RATES[1])
    grad = jnp.transpose(grads[:, s.n_one + s.n_two : s.wide])
    grad = grad - (left_skip[...] * factor(2)) * spec[2:3, : s.out]
    store_adamw((sw_new, sm_new, sv_new), (sw, sm, sv), grad, LEARN_RATES[2])


def share(chunks):
    return lax.all_to_all(chunks, ALL, 0, 0, tiled=True)


def core_swap(values):
    return lax.ppermute(values, "core", [(0, 1), (1, 0)])


def row_swaps(near, far):
    devices = lax.axis_size("rows")
    pairs = [(i, i ^ 1) for i in range(devices)]
    odd = [(i, i + 1) for i in range(1, devices - 1, 2)]
    odd = odd + [(j, i) for i, j in odd]
    return lax.ppermute(near, "rows", pairs), lax.ppermute(far, "rows", odd)


def row_swap(values, step):
    devices = lax.axis_size("rows")
    return lax.ppermute(values, "rows", [(i, i ^ step) for i in range(devices)])


def x_swap(values):
    return lax.ppermute(values, "x", [(0, 1), (1, 0)])


def gather_upper(block):
    return [block] + [row_swap(block, 2 * m) for m in range(1, lax.axis_size("rows") // 2)]


def gather_groups(values):
    if lax.axis_size("x") != 2:
        return lax.all_gather(values, ("x", "core"), axis=0)
    x, core = lax.axis_index("x"), lax.axis_index("core")
    pair = jnp.stack([values, core_swap(values)])
    pair = jnp.where(core == 0, pair, pair[::-1])
    both = jnp.stack([pair, x_swap(pair)])
    both = jnp.where(x == 0, both, both[::-1])
    return both.reshape(4, *values.shape)


def first_sum_kernel(mine, got, send_a, keep_a, send_b, keep_b):
    _, x, _ = position()
    low = lax.rem(lax.axis_index("rows"), 2)
    half = send_a.shape[0]
    for i in range(half):
        for k in range(2):
            send_a[i, k] = mine[i, k, 1 - x] + got[i, k, 1 - x]
            keep_a[i, k] = mine[i, k, x] + got[i, k, x]
            send_b[i, k] = mine[half + i, 1 - low, k] + got[half + i, 1 - low, k]
            keep_b[i, k] = mine[half + i, low, k] + got[half + i, low, k]


def second_sum_kernel(keep_a, got_a, keep_b, got_b, send_a, held_a, send_b, held_b):
    _, x, _ = position()
    low = lax.rem(lax.axis_index("rows"), 2)
    for i in range(keep_a.shape[0]):
        send_a[i] = keep_a[i, 1 - low] + got_a[i, 1 - low]
        held_a[i] = keep_a[i, low] + got_a[i, low]
        send_b[i] = keep_b[i, 1 - x] + got_b[i, 1 - x]
        held_b[i] = keep_b[i, x] + got_b[i, x]


def third_sum_kernel(held_a, got_a, held_b, got_b, *outs):
    high = lax.axis_index("rows") // 2
    half = held_a.shape[0]
    for m, out in enumerate(outs):
        at = high ^ m

        @pl.when(at < half)
        def _():
            out[0] = held_a[jnp.minimum(at, half - 1)] + got_a[jnp.minimum(at, half - 1)]

        @pl.when(at >= half)
        def _():
            at_b = jnp.maximum(at - half, 0)
            out[0] = held_b[at_b] + got_b[at_b]


def sum_kernel(*refs):
    *parts, out = refs
    total = parts[0][...]
    for part in parts[1:]:
        total = total + part[...]
    out[...] = total


def tied(values, after):
    return list(lax.optimization_barrier((tuple(values), tuple(after)))[0])


class StagedSum:
    small = 8 * 2**20

    def __init__(self, mine, other, after):
        self.high = lax.axis_size("rows") // 2
        self.tail = mine.shape[1:]
        mine = mine.reshape(self.high, 2, 2, *self.tail)
        got = core_swap(other).reshape(self.high, 2, 2, *self.tail)
        send_a, keep_a, send_b, keep_b = run(
            first_sum_kernel,
            [shape((self.high // 2, 2, *self.tail))] * 4,
            tied([mine, got], after),
            scalars=0,
            limit=self.small,
        )
        self.held = [keep_a, x_swap(send_a), keep_b, row_swap(send_b, 1)]

    def second(self, after):
        send_a, held_a, send_b, held_b = run(
            second_sum_kernel,
            [shape((self.high // 2, *self.tail))] * 4,
            tied(self.held, after),
            scalars=0,
            limit=self.small,
        )
        self.held = [held_a, row_swap(send_a, 1), held_b, x_swap(send_b)]

    def third(self, after):
        parts = run(
            third_sum_kernel,
            [shape((1, *self.tail))] * self.high,
            tied(self.held, after),
            scalars=0,
            limit=self.small,
        )
        self.held = [parts[0]] + [row_swap(parts[m], 2 * m) for m in range(1, self.high)]

    def last(self, after):
        (total,) = run(
            sum_kernel,
            [shape((1, *self.tail))],
            tied(self.held, after),
            scalars=0,
            limit=self.small,
        )
        return total


class PlainSum:
    def __init__(self, mine, other, after):
        self.held = lax.all_to_all(mine + core_swap(other), ("rows", "x"), 0, 0, tiled=True)

    def second(self, after):
        pass

    def third(self, after):
        pass

    def last(self, after):
        return jnp.sum(self.held, axis=0, keepdims=True)


def spread(total):
    if lax.axis_size("x") == 2:
        beside = x_swap(total)
        return total, beside, core_swap(total), core_swap(beside)
    total = lax.all_gather(total, "x", axis=0, tiled=True)
    beyond = core_swap(total)
    return total, total, beyond, beyond


def body(
    image_in,
    condition,
    group_counts,
    out_cotangent,
    power_vectors,
    conv1_weight,
    conv2_weight,
    skip_weight,
    cond_weight,
    out_bias,
    conv1_first,
    conv2_first,
    skip_first,
    cond_first,
    bias_first,
    conv1_second,
    conv2_second,
    skip_second,
    cond_second,
    bias_second,
):
    rows_n = lax.axis_size("rows")
    n_x = lax.axis_size("x")
    groups_n = 2 * n_x
    masters = [conv1_weight, conv2_weight, skip_weight, cond_weight, out_bias]
    s = Sizes(
        image_in.shape, out_cotangent.shape, condition.shape, [m.shape for m in masters], rows_n, n_x
    )
    bind = functools.partial
    scratch = pltpu.VMEM
    n, w = s.images, s.width
    depth = 3 * s.slot

    pay, half_one, half_two, near, far, left_one, left_two, left_skip = run(
        bind(prep_kernel, s),
        [
            shape((s.devices, 1, s.pay_one)),
            shape((s.pack_one, LANES), BF16),
            shape((s.pack_two, LANES), BF16),
            shape((n, 3 * w, LANES), BF16),
            shape((n, 3 * w, LANES), BF16),
            shape((1, s.n_one)),
            shape((1, s.n_two)),
            shape((s.n_skip, 1)),
        ],
        [
            group_counts,
            image_in,
            condition,
            power_vectors,
            conv1_weight.T,
            conv2_weight.T,
            skip_weight,
            cond_weight.T,
            out_bias[None],
        ],
        [scratch((1, s.pay_one), F32)],
        limit=60 * 2**20,
    )
    blocks = gather_upper(half_one)
    near, far = row_swaps(near, far)
    (pay,) = tied([pay], [near, far])
    got_one = share(pay)
    acts, proj, stats_one, spec, near_cot, far_cot = run(
        bind(act_kernel, s),
        [
            shape((n, s.rows + 2, w, 4 * s.chan), BF16),
            shape((n, rows_n * s.cols)),
            shape((2, s.chan)),
            shape((16, s.slot)),
            *[shape((n, 6 * w, LANES), BF16)] * 2,
        ],
        [group_counts, got_one, image_in, near, far],
        [pltpu.SemaphoreType.DMA((2,))],
        flops=0, idle=True,
        whole=[out_cotangent],
        limit=52 * 2**20,
    )
    near_one = jnp.stack(blocks)
    (half_two,) = tied([half_two], [near_one])
    far_one = row_swap(near_one, 1)
    near_two = jnp.stack(gather_upper(half_two))
    far_one, near_two, acts = lax.optimization_barrier((far_one, near_two, acts))
    blocks_one = near_one, far_one, core_swap(near_one), core_swap(far_one)

    far_two = row_swap(near_two, 1)
    near_cot, far_cot = row_swaps(near_cot, far_cot)
    hidden, weight_one, pay = run(
        bind(conv_one_kernel, s),
        [
            shape((n, s.ext, 2, w, s.out)),
            shape((9 * s.chan, s.out), BF16),
            shape((s.devices, 1, s.pay_two)),
        ],
        [group_counts, acts, *blocks_one],
        [scratch((1, s.pay_two), F32), scratch((9 * s.chan, s.out), F32)],
        flops=2 * n * s.ext * 2 * w * 9 * s.chan * s.out,
        limit=52 * 2**20,
    )
    far_two, near_cot, far_cot, pay = lax.optimization_barrier((far_two, near_cot, far_cot, pay))
    blocks_two = near_two, far_two, core_swap(near_two), core_swap(far_two)
    got_two = share(pay)
    dact, phases, grad_low, grad_skip, skip_part, weight_two, weight_skip, misc = run(
        bind(cot_kernel, s),
        [
            shape((n, s.ext, 2, w, s.out)),
            shape((n, 2 * s.rows, 2, w, s.out), BF16),
            shape((n, 2 * s.rows, 2, w, s.out), BF16),
            shape((n, s.rows, w, s.out), BF16),
            shape((n, s.rows, w, s.out)),
            shape((3, depth, s.out), BF16),
            shape((s.chan, s.out), BF16),
            shape((8, s.slot)),
        ],
        [group_counts, out_cotangent, near_cot, far_cot, image_in, *blocks_two, spec],
        [
            scratch((n, 2 * s.rows + 4, w, 4 * s.slot), BF16),
            scratch((9 * s.out + s.chan, s.out), F32),
            scratch((2, 2 * w, LANES), F32),
            scratch((3, depth, s.out), BF16),
        ],
        flops=2 * n * s.ext * 2 * w * 9 * s.out * s.out,
        limit=52 * 2**20,
    )
    stats_two, terms_two, pay, slots_two, dnorm = run(
        bind(norm_two_kernel, s),
        [shape((2, s.slot)), shape((8, 2 * s.slot)), shape((s.devices, 1, s.pay_two))],
        [group_counts, got_two, spec, proj],
        [scratch((1, s.pay_two), F32), pltpu.SemaphoreType.DMA((4, n))],
        whole=[hidden, dact],
        results=[shape((n, s.ext, w, 4 * s.slot), BF16), shape((n, s.ext, 2, w, s.out))],
        limit=53 * 2**20,
    )
    got_three = share(pay)
    sent = shape((s.rows_n * n_x, s.grad_rows, LANES))
    scale_one, other, mine, slots_one = run(
        bind(hidden_grad_kernel, s),
        [shape((8, s.slot))],
        [group_counts, got_three, stats_two, spec, grad_skip, image_in],
        [
            scratch((2, 2, n, s.rows, w, s.out), BF16),
            scratch((s.out, rows_n * s.pitch), F32),
            pltpu.SemaphoreType.DMA((5, max(n, 3))),
        ],
        flops=8 * n * s.rows * w * 9 * s.chan * s.out,
        whole=[dnorm, hidden, acts, slots_two, grad_low],
        results=[sent, sent, shape((n, 2, s.rows + 1, w, 4 * s.slot), BF16)],
        limit=48 * 2**20,
    )
    out_image, scale_two = run(
        bind(conv_two_kernel, s),
        [shape(out_cotangent.shape, BF16), shape((8, LANES))],
        tied([slots_two, weight_two, phases, skip_part, spec], [scale_one]),
        [scratch((2, 2 * w, LANES), F32)],
        scalars=0,
        flops=8 * n * s.rows * 2 * w * 9 * s.out * s.out,
        limit=48 * 2**20,
    )
    sums = (StagedSum if n_x == 2 else PlainSum)(mine, other, [scale_two])
    dnorm_one, pay = run(
        bind(input_grad_kernel, s),
        [shape((n, s.rows, w, s.chan)), shape((s.devices, 1, s.pay_four))],
        [slots_one, weight_one, image_in, stats_one, proj, terms_two, scale_one, scale_two, misc],
        [
            scratch((3, depth, s.chan), BF16),
            scratch((8, rows_n * s.cols), F32),
            scratch((1, s.pay_four), F32),
        ],
        scalars=0,
        flops=8 * n * s.rows * w * 9 * s.chan * s.out,
    )
    sums.second([pay])
    late_condition, pay = lax.optimization_barrier((condition, pay))
    cond_all = gather_groups(late_condition)
    got_four = share(pay)
    sums.third([got_four])
    moments = [cond_weight, cond_first, cond_second]
    biases = [out_bias, bias_first, bias_second]
    image_grad, *rest, scales = run(
        bind(finish_kernel, s),
        [
            shape(image_in.shape),
            *[shape((s.cols, s.cond))] * 3,
            *[shape((1, s.n_bias))] * 3,
            shape((8, LANES)),
        ],
        [
            group_counts,
            got_four,
            cond_all,
            image_in,
            dnorm_one,
            grad_skip,
            weight_skip,
            stats_one,
            proj,
            *[m.T for m in moments],
            *[b[None] for b in biases],
        ],
        [
            scratch((groups_n * n, s.cols), F32),
            scratch((groups_n * n, s.cond), F32),
        ],
        limit=60 * 2**20,
    )
    parts = spread(sums.last([scales]))
    cond_new = [c.T for c in rest[:3]]
    bias_new = [b[0] for b in rest[3:]]
    olds = [
        *[m.T for m in (conv1_weight, conv1_first, conv1_second)],
        *[m.T for m in (conv2_weight, conv2_first, conv2_second)],
        skip_weight,
        skip_first,
        skip_second,
    ]
    news = run(
        bind(weights_kernel, s),
        [shape(o.shape) for o in olds],
        [*parts, scales, spec, left_one, left_two, left_skip, *olds],
        [scratch((s.out, s.pitch), F32)],
        limit=24 * 2**20,
        scalars=0,
    )
    weights_new = [m.T for m in news[:6]] + list(news[6:])
    return (out_image, image_grad, *weights_new, *cond_new, *bias_new)


def solution(mesh):
    rows_n, imgs_n = mesh.devices.shape
    fine = Mesh(np.asarray(mesh.devices).reshape(rows_n, imgs_n // 2, 2), ALL)
    groups = ("x", "core")
    picture = P(groups, "rows", None, None)
    weight = P("rows", None)
    column = P(None, "rows")
    masters = (weight, weight, weight, column, P("rows"))
    return jax.shard_map(
        body,
        mesh=fine,
        in_specs=(picture, P(groups, None), P(), picture, P(), *masters, *masters, *masters),
        out_specs=(
            picture,
            picture,
            *(weight,) * 9,
            *(column,) * 3,
            *(P("rows"),) * 3,
        ),
        check_vma=False,
    )
```

```python
import functools

import jax
import jax.numpy as jnp
import numpy as np
from jax import lax
from jax.experimental import pallas as pl
from jax.experimental.pallas import tpu as pltpu
from jax.sharding import Mesh
from jax.sharding import PartitionSpec as P

STEP = 10
precise = lax.Precision.HIGHEST
NORM_EPS = 1e-05
BETA_ONE = 0.9
BETA_TWO = 0.999
ADAM_EPS = 1e-08
DECAY_RATE = 0.01
LEARN_RATES = (0.02, 0.02, 0.05, 0.03, 0.15)
ALL = ("rows", "x", "core")
F32, BF16 = jnp.float32, jnp.bfloat16
LANES = 128
VMEM_LIMIT = 56 * 2**20


def shape(dims, kind=F32):
    return jax.ShapeDtypeStruct(tuple(dims), kind)


def run(kernel, outs, args, scratch=(), scalars=1, flops=0, limit=VMEM_LIMIT, whole=(), results=(), idle=False):
    spec = pl.BlockSpec(memory_space=pltpu.VMEM)
    specs = [pl.BlockSpec(memory_space=pltpu.SMEM)] * scalars + [spec] * (len(args) - scalars)
    specs += [pl.BlockSpec(memory_space=pl.ANY)] * len(whole)
    moved = sum(a.size * a.dtype.itemsize for a in args)
    moved += sum(np.prod(o.shape) * np.dtype(o.dtype).itemsize for o in outs)
    args = [*args, *whole]
    if idle:
        moved = 0
    scratch = [pltpu.VMEM(a.shape, a.dtype) for a in (*whole, *results)] + list(scratch)
    out_specs = [spec] * len(outs) + [pl.BlockSpec(memory_space=pl.ANY)] * len(results)
    outs = [*outs, *results]
    return pl.pallas_call(
        kernel,
        out_shape=tuple(outs),
        in_specs=specs,
        out_specs=tuple(out_specs),
        scratch_shapes=scratch,
        cost_estimate=pl.CostEstimate(
            flops=int(flops), bytes_accessed=int(moved), transcendentals=0
        ),
        compiler_params=pltpu.CompilerParams(vmem_limit_bytes=limit),
    )(*args)


def round_up(value, step):
    return -(-value // step) * step


class Sizes:
    def __init__(self, image, cot, condition, masters, rows_n, n_x):
        self.images, self.rows, self.width, self.chan = image
        self.out = cot[3]
        self.slot = round_up(self.out, LANES)
        self.ext = 2 * self.rows + 2
        self.cond = condition[1]
        self.n_one, self.n_two, self.n_skip = masters[0][0], masters[1][0], masters[2][0]
        self.cols = masters[3][1]
        self.n_bias = masters[4][0]
        self.rows_n, self.groups = rows_n, 2 * n_x
        self.devices = rows_n * self.groups
        self.h_one = round_up(-(-self.n_one // 2), 8)
        self.h_two = round_up(-(-self.n_two // 2), 8)
        self.h_skip = round_up(-(-self.n_skip // 2), 8)
        self.pack_one = round_up(packed_rows(self.h_one), 16)
        self.pack_two = round_up(packed_rows(self.h_two + self.h_skip), 16)
        self.at_power = 2 * self.chan
        self.at_norm = self.at_power + 3 * self.out
        self.at_bias = self.at_norm + 8
        self.at_proj = round_up(self.at_bias + self.n_bias, LANES)
        self.pay_one = round_up(self.at_proj + self.images * self.cols, LANES)
        self.pay_two = round_up(2 * self.out, LANES)
        self.at_scale = 2 * self.chan
        self.at_gbias = self.at_scale + HALF
        self.at_terms = self.at_gbias + self.out
        self.pay_four = round_up(self.at_terms + self.images * self.cols, LANES)
        self.part = self.out // 2 // n_x
        self.n_x = n_x
        self.wide = self.n_one + self.n_two + self.n_skip
        self.pitch = round_up(self.wide, LANES)
        self.grad_rows = grad_rows(self.part, self.wide)


HALF = LANES // 2


def from_row(near, far, row):
    row_pos = lax.axis_index("rows")
    at = (row_pos // 2) ^ (row // 2)
    same = lax.rem(row_pos, 2) == row % 2
    return jnp.where(same, near[at].astype(F32), far[at].astype(F32))


def packed_rows(rows):
    return rows + round_up(-(-rows // 2), 8)


def pack(values):
    rows = values.shape[0]
    h = round_up(-(-rows // 2), 8)
    right = values[:, LANES:]
    return jnp.concatenate(
        [values[:, :LANES], jnp.concatenate([right[:h], right[rows - h :]], axis=1)], axis=0
    )


def unpack(values, rows):
    h = round_up(-(-rows // 2), 8)
    right = values[rows : rows + h]
    low = jnp.concatenate([right[:, :HALF], right[2 * h - rows :, HALF:]], axis=0)
    return jnp.concatenate([values[:rows], low], axis=1)


def grad_rows(part, width):
    tail = width % LANES
    rows = part * (width // LANES)
    if tail:
        rows += part // 2 if tail <= HALF and part % 16 == 0 else part
    return rows


def pack_grad(ref, lead, grads, here, begin, width):
    part = here.size
    full = width // LANES
    for k in range(full):
        at = begin + k * LANES
        ref[lead, k * part : (k + 1) * part, :] = grads[here, at : at + LANES]
    tail = width - full * LANES
    if not tail:
        return
    at = full * part
    rest = grads[here, begin + full * LANES : begin + (full + 1) * LANES]
    if tail <= HALF and part % 16 == 0:
        h = part // 2
        ref[lead, at : at + h, :] = jnp.concatenate([rest[:h, :HALF], rest[h:, :HALF]], axis=1)
    else:
        ref[lead, at : at + part, :] = rest


def unpack_grad(values, at, part, width):
    full = width // LANES
    pieces = [values[at + k * part : at + (k + 1) * part] for k in range(full)]
    at += full * part
    tail = width - full * LANES
    if tail and tail <= HALF and part % 16 == 0:
        h = part // 2
        both = values[at : at + h]
        pieces.append(
            jnp.concatenate([both[:, :tail], both[:, HALF : HALF + tail]], axis=0)
        )
    elif tail:
        pieces.append(values[at : at + part, :tail])
    return pieces[0] if len(pieces) == 1 else jnp.concatenate(pieces, axis=1)


def position():
    return lax.axis_index("rows"), lax.axis_index("x"), lax.axis_index("core")


def group_position():
    return lax.axis_index("x") * lax.axis_size("core") + lax.axis_index("core")


def live_of(counts, image):
    return jnp.where(image < counts[group_position()], 1.0, 0.0).astype(F32)


def live_total(counts, sizes):
    total = counts[0]
    for g in range(1, sizes.groups):
        total = total + counts[g]
    return total.astype(F32)


def inside(row, sizes, scale):
    at = lax.axis_index("rows") * (scale * sizes.rows) + row
    return jnp.where((at >= 0) & (at < scale * sizes.rows * sizes.rows_n), 1.0, 0.0).astype(F32)


def start(source, target, sem):
    copy = pltpu.make_async_copy(source, target, sem)
    copy.start()
    return copy


def sigmoid(values):
    return 1.0 / (1.0 + jnp.exp(-values))


def shifted(values, step):
    width = values.shape[0]
    rolled = pltpu.roll(values, (-step) % width, 0)
    where = lax.broadcasted_iota(jnp.int32, values.shape, 0)
    edge = 0 if step < 0 else width - 1
    return jnp.where(where == edge, 0.0, rolled)


def padded(values, size):
    rest = size - values.shape[1]
    if not rest:
        return values
    return jnp.concatenate([values, jnp.zeros((values.shape[0], rest), values.dtype)], axis=1)


def fill(ref, where, phase, value, slot):
    value = padded(value, slot)
    at = (1 + phase) * slot
    ref[(*where, slice(None), slice(at, at + slot))] = value.astype(BF16)
    step, at = (-1, 0) if phase else (1, 3 * slot)
    ref[(*where, slice(None), slice(at, at + slot))] = shifted(value, step).astype(BF16)


def dot(a, b, dims=((1,), (0,)), precision=None):
    return lax.dot_general(a, b, (dims, ((), ())), preferred_element_type=F32, precision=precision)


def prep_kernel(sizes, counts, image, cond, vec, one_t, two_t, skip, cond_t, bias,
                pay, half_one, half_two, near, far, left_one, left_two,
                left_skip, line):
    s = sizes
    row_pos, _, core = position()
    even = lax.rem(row_pos, 2) == 0
    last, w = s.rows - 1, s.width

    line[...] = jnp.zeros_like(line)
    vec_t = jnp.transpose(jnp.concatenate([vec[...], jnp.zeros((5, s.out), F32)], axis=0))

    def power(k, low):
        column = jnp.sum(low * vec[k : k + 1, :], axis=1, keepdims=True)
        row = jnp.sum(low * column, axis=0, keepdims=True)
        at = s.at_power + k * s.out
        line[0:1, at : at + s.out] = row
        at = s.at_norm + k
        line[0:1, at : at + 1] = jnp.sum(column * column, axis=0, keepdims=True)
        return column

    low_t = one_t[...].astype(BF16).astype(F32)
    left_one[...] = jnp.sum(low_t * vec_t[:, 0:1], axis=0, keepdims=True)
    low = jnp.transpose(low_t)
    power(0, low)
    n, h = s.n_one, s.h_one
    packed_one = pack(jnp.where(core == 0, low[:h], low[n - h :]))
    low_t = two_t[...].astype(BF16).astype(F32)
    left_two[...] = jnp.sum(low_t * vec_t[:, 1:2], axis=0, keepdims=True)
    low = jnp.transpose(low_t)
    power(1, low)
    n, h = s.n_two, s.h_two
    half_a = jnp.where(core == 0, low[:h], low[n - h :])
    low = skip[...].astype(BF16).astype(F32)
    left_skip[...] = power(2, low)
    n, h = s.n_skip, s.h_skip
    half_b = jnp.where(core == 0, low[:h], low[n - h :])
    packed = pack(jnp.concatenate([half_a, half_b], axis=0))
    if s.pack_two > packed.shape[0]:
        packed = jnp.concatenate(
            [packed, jnp.zeros((s.pack_two - packed.shape[0], LANES), F32)], axis=0
        )
    packed = packed.astype(BF16)
    half_two[...] = packed
    line[0:1, s.at_bias : s.at_bias + s.n_bias] = bias[...].astype(BF16).astype(F32)
    proj = dot(cond[...], cond_t[...].astype(BF16), ((1,), (1,)))
    for b in range(s.images):
        at = s.at_proj + b * s.cols
        line[0:1, at : at + s.cols] = proj[b : b + 1]
    if s.pack_one > packed_one.shape[0]:
        packed_one = jnp.concatenate(
            [packed_one, jnp.zeros((s.pack_one - packed_one.shape[0], LANES), F32)], axis=0
        )
    half_one[...] = packed_one.astype(BF16)

    def edges(ref, row):
        for t in range(3):
            ref[:, t * w : (t + 1) * w, :] = image[:, row, :, t * LANES : (t + 1) * LANES]

    @pl.when(even)
    def _():
        edges(near, last)
        edges(far, 0)

    @pl.when(jnp.logical_not(even))
    def _():
        edges(near, 0)
        edges(far, last)

    sums = jnp.zeros((8, s.chan), F32)
    squares = jnp.zeros((8, s.chan), F32)
    for b in range(s.images):
        part = jnp.zeros((8, s.chan), F32)
        part_sq = jnp.zeros((8, s.chan), F32)
        for i in range(s.rows):
            x = image[b, i].astype(F32).reshape(w // 8, 8, s.chan)
            part += jnp.sum(x, axis=0)
            part_sq += jnp.sum(x * x, axis=0)
        sums += part * live_of(counts, b)
        squares += part_sq * live_of(counts, b)
    line[0:1, : s.chan] = jnp.sum(sums, axis=0, keepdims=True)
    line[0:1, s.chan : 2 * s.chan] = jnp.sum(squares, axis=0, keepdims=True)
    whole = line[...]
    for d in range(s.devices):
        pay[d] = whole


def act_kernel(sizes, counts, got, image, near, far, cot, slots, proj, stats, spec,
               near_cot, far_cot, rows, sems):
    s = sizes
    row_pos, _, _ = position()
    even = lax.rem(row_pos, 2) == 0
    copies = [
        start(cot.at[:, pl.ds(at, 2)], rows.at[:, pl.ds(at, 2)], sems.at[k])
        for k, at in enumerate(sorted({0, 2 * s.rows - 2}))
    ]
    group = group_position()
    sums = jnp.sum(got[:, :, : 2 * s.chan], axis=0)
    count = live_total(counts, s) * (s.width * s.width)
    mean = sums[:, : s.chan] / count
    rstd = lax.rsqrt(sums[:, s.chan :] / count - mean * mean + NORM_EPS)
    stats[0:1, :] = mean
    stats[1:2, :] = rstd

    spec[...] = jnp.zeros_like(spec)
    total = None
    for r in range(s.rows_n):
        piece = got[r * s.groups + group, :, s.at_power :]
        part = piece[:, : s.at_proj - s.at_power]
        total = part if total is None else total + part
        at = s.at_bias - s.at_power
        spec[6:7, r * s.n_bias : (r + 1) * s.n_bias] = piece[:, at : at + s.n_bias]
        for b in range(s.images):
            at = s.at_proj - s.at_power + b * s.cols
            proj[b : b + 1, r * s.cols : (r + 1) * s.cols] = piece[:, at : at + s.cols]
    for k in range(3):
        at = s.at_norm - s.at_power + k
        inv_norm = lax.rsqrt(total[:, at : at + 1])
        row = total[:, k * s.out : (k + 1) * s.out] * inv_norm
        inv_sigma = lax.rsqrt(jnp.sum(row * row, axis=1, keepdims=True))
        spec[k : k + 1, : s.out] = row * inv_sigma
        spec[3 + k : 4 + k, :] = jnp.broadcast_to(inv_sigma, (1, s.slot))
        spec[8 + k : 9 + k, :] = jnp.broadcast_to(inv_norm, (1, s.slot))

    w = s.width

    def one(b, e, x, keep):
        gain = 1.0 + proj[pl.ds(b, 1), : s.chan]
        shift = proj[pl.ds(b, 1), s.chan : 2 * s.chan]
        pre = gain * ((x - mean) * rstd) + shift
        act = pre * sigmoid(pre)
        if keep is not None:
            act = act * keep
        low = act.astype(BF16)
        slots[b, e, :, s.chan : 2 * s.chan] = low
        slots[b, e, :, 2 * s.chan : 3 * s.chan] = low
        slots[b, e, :, : s.chan] = shifted(act, -1).astype(BF16)
        slots[b, e, :, 3 * s.chan :] = shifted(act, 1).astype(BF16)

    def edge(ref, b):
        return jnp.concatenate(
            [ref[b, t * w : (t + 1) * w, :].astype(F32) for t in range(3)], axis=1
        )

    @pl.loop(0, s.images)
    def _(b):
        a, c = edge(near, b), edge(far, b)
        one(b, 0, jnp.where(even, c, a), inside(-1, s, 1))
        for i in range(s.rows):
            one(b, i + 1, image[b, i].astype(F32), None)
        one(b, s.rows + 1, jnp.where(even, a, c), inside(s.rows, s, 1))

    for copy in copies:
        copy.wait()

    def cot_edges(ref, row):
        for b in range(s.images):
            for k in range(2):
                ref[b, 2 * w * k : 2 * w * (k + 1), :] = rows[b, row + k, :, :LANES]
            right = [rows[b, row + k, :, LANES:].astype(F32) for k in range(2)]
            ref[b, 4 * w :, :] = jnp.concatenate(right, axis=1).astype(BF16)

    @pl.when(even)
    def _():
        cot_edges(near_cot, 2 * s.rows - 2)
        cot_edges(far_cot, 0)

    @pl.when(jnp.logical_not(even))
    def _():
        cot_edges(near_cot, 0)
        cot_edges(far_cot, 2 * s.rows - 2)


def conv_one_kernel(sizes, counts, slots, mine_near, mine_far, other_near, other_far, hidden, weight, pay, line, wide):
    s = sizes
    _, _, core = position()
    first = core == 0
    for r in range(s.rows_n):
        a = unpack(from_row(mine_near, mine_far, r), s.h_one)
        b = unpack(from_row(other_near, other_far, r), s.h_one)
        at = r * s.n_one
        wide[at : at + s.h_one, :] = jnp.where(first, a, b)
        at += s.n_one - s.h_one
        wide[at : at + s.h_one, :] = jnp.where(first, b, a)
    for t in range(9):
        weight[t * s.chan : (t + 1) * s.chan] = wide[t * s.chan : (t + 1) * s.chan, :].astype(BF16)
    depth = 3 * s.chan
    rows = s.rows + 1
    sums = jnp.zeros((8, s.out), F32)
    squares = jnp.zeros((8, s.out), F32)
    for phase in range(4):
        a, b = divmod(phase, 2)
        total = None
        for dy in range(3):
            at = (a + dy - 1) // 2 + 1 - a
            lhs = slots[:, at : at + rows, :, b * s.chan : b * s.chan + depth]
            part = dot(
                lhs.reshape(s.images * rows * s.width, depth),
                weight[dy * depth : (dy + 1) * depth, :],
            )
            total = part if total is None else total + part
        total = total.reshape(s.images, rows, s.width, s.out)
        for i in range(s.images):
            part = jnp.zeros((8, s.out), F32)
            part_sq = jnp.zeros((8, s.out), F32)
            for k in range(rows):
                e = 2 * k + 1 - a
                value = total[i, k]
                hidden[i, e, b] = value
                if 0 < e < s.ext - 1:
                    x = value.reshape(s.width // 8, 8, s.out)
                    part += jnp.sum(x, axis=0)
                    part_sq += jnp.sum(x * x, axis=0)
            sums += part * live_of(counts, i)
            squares += part_sq * live_of(counts, i)
    line[...] = jnp.zeros_like(line)
    line[0:1, : s.out] = jnp.sum(sums, axis=0, keepdims=True)
    line[0:1, s.out : 2 * s.out] = jnp.sum(squares, axis=0, keepdims=True)
    whole = line[...]
    for d in range(s.devices):
        pay[d] = whole


def cot_kernel(sizes, counts, cot, near, far, image, mine_near, mine_far, other_near, other_far, spec, dact, phases, grad_low,
               grad_skip, skip_part, two, skip_w, misc, slots, wide, pair, flip):
    s = sizes
    row_pos, _, core = position()
    even = lax.rem(row_pos, 2) == 0
    first = core == 0
    w = s.width
    for r in range(s.rows_n):
        a = unpack(from_row(mine_near, mine_far, r), s.h_two + s.h_skip)
        b = unpack(from_row(other_near, other_far, r), s.h_two + s.h_skip)
        lo, hi = jnp.where(first, a, b), jnp.where(first, b, a)
        at = r * s.n_two
        wide[at : at + s.h_two, :] = lo[: s.h_two]
        at += s.n_two - s.h_two
        wide[at : at + s.h_two, :] = hi[: s.h_two]
        at = 9 * s.out + r * s.n_skip
        wide[at : at + s.h_skip, :] = lo[s.h_two :]
        at += s.n_skip - s.h_skip
        wide[at : at + s.h_skip, :] = hi[s.h_two :]
    two[...] = jnp.zeros_like(two)
    flip[...] = jnp.zeros_like(flip)
    for t in range(9):
        dy, dx = divmod(t, 3)
        tap = wide[t * s.out : (t + 1) * s.out, :]
        two[dy, dx * s.slot : dx * s.slot + s.out, :] = tap.astype(BF16)
        back = jnp.transpose(tap).astype(BF16)
        flip[2 - dy, (2 - dx) * s.slot : (2 - dx) * s.slot + s.out, :] = back
    skip_w[...] = wide[9 * s.out : 9 * s.out + s.chan, :].astype(BF16)

    inv_two = spec[4:5, : s.out]
    inv_skip = spec[5:6, : s.out]

    def split(b, q, row, own):
        pair[0] = row[:, :LANES]
        pair[1, :, : s.out - LANES] = row[:, LANES:]
        both = []
        for ph in range(2):
            value = jnp.concatenate(
                [pair[0, pl.ds(ph, w, 2), :], pair[1, pl.ds(ph, w, 2), :][:, : s.out - LANES]],
                axis=1,
            )
            low = (value * inv_two).astype(BF16)
            both.append(value)
            if own is not None:
                phases[b, own, ph] = value.astype(BF16)
                grad_low[b, own, ph] = low
            fill(slots, (b, q), ph, low.astype(F32), s.slot)
        return both[0] + both[1]

    def edge_row(ref, b, k):
        right = ref[b, 4 * w :, :].astype(F32)
        return jnp.concatenate(
            [
                ref[b, 2 * w * k : 2 * w * (k + 1), :].astype(F32),
                right[:, k * HALF : k * HALF + s.out - LANES],
            ],
            axis=1,
        )

    misc[...] = jnp.zeros_like(misc)

    @pl.loop(0, s.images)
    def _(b):
        live = live_of(counts, b)
        above = inside(-1, s, 1) * live
        below = inside(s.rows, s, 1) * live
        for k in range(2):
            a, c = edge_row(near, b, k), edge_row(far, b, k)
            split(b, k, jnp.where(even, c, a) * above, None)
            split(b, 2 * s.rows + 2 + k, jnp.where(even, a, c) * below, None)
        bias = jnp.zeros((1, s.out), F32)
        skip_sum = jnp.zeros((1, s.out), F32)
        for i in range(s.rows):
            pooled = split(b, 2 * i + 2, cot[b, 2 * i].astype(F32) * live, 2 * i)
            pooled += split(b, 2 * i + 3, cot[b, 2 * i + 1].astype(F32) * live, 2 * i + 1)
            grad_skip[b, i] = (pooled * inv_skip).astype(BF16)
            bias += jnp.sum(pooled, axis=0, keepdims=True)
            raw = dot(image[b, i], skip_w[...])
            skip_part[b, i] = raw * inv_skip
            skip_sum += jnp.sum(pooled * raw, axis=0, keepdims=True)
        misc[0:1, : s.out] += bias
        misc[1:2, : s.out] += skip_sum

    depth = 3 * s.slot
    for ph in range(2):
        total = None
        for dy in range(3):
            lhs = slots[:, dy : dy + s.ext, :, ph * s.slot : ph * s.slot + depth]
            part = dot(lhs.reshape(s.images * s.ext * w, depth), flip[dy])
            total = part if total is None else total + part
        dact[:, :, ph] = total.reshape(s.images, s.ext, w, s.out)


def norm_two_kernel(sizes, counts, got, spec, proj, hidden_from, dact_from, stats, terms, pay,
                    slots_to, dnorm_to, hidden, dact, slots, dnorm, line, sems):
    s = sizes
    w = s.width
    for b in range(s.images):
        start(hidden_from.at[b], hidden.at[b], sems.at[0, b])
        start(dact_from.at[b], dact.at[b], sems.at[1, b])
    inv = spec[3:4, : s.out]
    sums = jnp.sum(got[...], axis=0)
    count = live_total(counts, s) * (4 * w * w)
    mean = sums[:, : s.out] * inv / count
    square = sums[:, s.out : 2 * s.out] * inv * inv / count
    rstd = lax.rsqrt(square - mean * mean + NORM_EPS)
    stats[0:1, : s.out] = mean
    stats[1:2, : s.out] = rstd
    scale = inv * rstd
    offset = mean * rstd
    base = 2 * s.chan

    def one(b, e, keep):
        gain = 1.0 + proj[pl.ds(b, 1), base : base + s.out]
        shift = proj[pl.ds(b, 1), base + s.out : base + 2 * s.out]
        dsum = jnp.zeros((8, s.out), F32)
        dgain = jnp.zeros((8, s.out), F32)
        for ph in range(2):
            normed = hidden[b, e, ph] * scale - offset
            pre = gain * normed + shift
            sig = sigmoid(pre)
            act = pre * sig
            if keep is not None:
                act = act * keep
            fill(slots, (b, e), ph, act, s.slot)
            dpre = dact[b, e, ph] * (sig * (1.0 + pre * (1.0 - sig)))
            dnorm[b, e, ph] = gain * dpre
            if keep is None:
                dsum += jnp.sum(dpre.reshape(w // 8, 8, s.out), axis=0)
                dgain += jnp.sum((dpre * normed).reshape(w // 8, 8, s.out), axis=0)
        return dsum, dgain

    terms[...] = jnp.zeros_like(terms)

    def sent(b):
        return [
            pltpu.make_async_copy(slots.at[b], slots_to.at[b], sems.at[2, b]),
            pltpu.make_async_copy(dnorm.at[b], dnorm_to.at[b], sems.at[3, b]),
        ]

    @pl.loop(0, s.images)
    def _(b):
        pltpu.make_async_copy(hidden_from.at[b], hidden.at[b], sems.at[0, b]).wait()
        pltpu.make_async_copy(dact_from.at[b], dact.at[b], sems.at[1, b]).wait()
        one(b, 0, inside(-1, s, 2))
        dsum = jnp.zeros((8, s.out), F32)
        dgain = jnp.zeros((8, s.out), F32)
        for e in range(1, s.ext - 1):
            a, c = one(b, e, None)
            dsum += a
            dgain += c
        one(b, s.ext - 1, inside(2 * s.rows, s, 2))
        terms[pl.ds(b, 1), : s.out] = jnp.sum(dgain, axis=0, keepdims=True)
        terms[pl.ds(b, 1), s.out : 2 * s.out] = jnp.sum(dsum, axis=0, keepdims=True)
        for copy in sent(b):
            copy.start()

    total = jnp.zeros((1, s.out), F32)
    cross = jnp.zeros((1, s.out), F32)
    for b in range(s.images):
        gain = 1.0 + proj[b : b + 1, base : base + s.out]
        cross += gain * terms[b : b + 1, : s.out]
        total += gain * terms[b : b + 1, s.out : 2 * s.out]
    line[...] = jnp.zeros_like(line)
    line[0:1, : s.out] = total
    line[0:1, s.out : 2 * s.out] = cross
    whole = line[...]
    for d in range(s.devices):
        pay[d] = whole
    for b in range(s.images):
        for copy in sent(b):
            copy.wait()


def conv_two_kernel(sizes, slots, two, phases, skip_part, spec, out, scale, pair):
    s = sizes
    w = s.width
    depth = 3 * s.slot
    own = 2 * s.rows
    inv_two = spec[4:5, : s.out]
    bias = spec[6:7, : s.out]
    dots = jnp.zeros((1, s.out), F32)
    results = []
    for ph in range(2):
        total = None
        for dy in range(3):
            lhs = slots[:, dy : dy + own, :, ph * s.slot : ph * s.slot + depth]
            part = dot(lhs.reshape(s.images * own * w, depth), two[dy])
            total = part if total is None else total + part
        results.append(total.reshape(s.images, own, w, s.out))
    for b in range(s.images):
        for e in range(own):
            for ph in range(2):
                raw = results[ph][b, e]
                dots += jnp.sum(raw * phases[b, e, ph].astype(F32), axis=0, keepdims=True)
                value = raw * inv_two + skip_part[b, e // 2] + bias
                pair[0, pl.ds(ph, w, 2), :] = value[:, :LANES]
                pair[1, pl.ds(ph, w, 2), :] = jnp.concatenate(
                    [value[:, LANES:], jnp.zeros((w, 2 * LANES - s.out), F32)], axis=1
                )
            out[b, e, :, :LANES] = pair[0].astype(BF16)
            out[b, e, :, LANES:] = pair[1][:, : s.out - LANES].astype(BF16)
    scale[...] = jnp.broadcast_to(jnp.sum(dots, axis=1, keepdims=True), scale.shape)


def place(s, grads, values, first, shard, offset):
    end = first + values.shape[1]
    for r in range(first // shard, (end - 1) // shard + 1):
        low, high = max(first, r * shard), min(end, (r + 1) * shard)
        at = r * s.pitch + offset + low - r * shard
        grads[:, at : at + high - low] = values[:, low - first : high - first]


def grads_two(s, slots, grad_low, grad_skip, image, grads):
    w = s.width
    own = 2 * s.rows
    depth = 3 * s.slot
    count = s.images * own * w
    flips = [jnp.transpose(grad_low[:, :, ph].reshape(count, s.out)) for ph in range(2)]
    for dy in range(3):
        total = None
        for ph in range(2):
            rhs = slots[:, dy : dy + own, :, ph * s.slot : ph * s.slot + depth]
            part = dot(flips[ph], rhs.reshape(count, depth))
            total = part if total is None else total + part
        for dx in range(3):
            tap = total[:, dx * s.slot : dx * s.slot + s.out]
            place(s, grads, tap, (3 * dy + dx) * s.out, s.n_two, s.n_one)
    count = s.images * s.rows * w
    flip = jnp.transpose(grad_skip[...].reshape(count, s.out))
    place(s, grads, dot(flip, image[...].reshape(count, s.chan)), 0, s.n_skip, s.n_one + s.n_two)


def hidden_grad_kernel(sizes, counts, got, stats, spec, grad_skip, image,
                       dnorm_from, hidden_from, acts_from, slots_two_from, grad_low_from,
                       scale, other_to, mine_to, slots_to,
                       dnorm, hidden, acts, slots_two, grad_low, other, mine, slots,
                       low, grads, sems):
    s = sizes
    _, _, core = position()
    w = s.width
    for b in range(s.images):
        start(hidden_from.at[b], hidden.at[b], sems.at[0, b])
        start(dnorm_from.at[b], dnorm.at[b], sems.at[1, b])
    fetch_acts = start(acts_from, acts, sems.at[3, 0])
    fetch_two = [
        start(slots_two_from, slots_two, sems.at[3, 1]),
        start(grad_low_from, grad_low, sems.at[3, 2]),
    ]
    sums = jnp.sum(got[...], axis=0)
    count = live_total(counts, s) * (4 * w * w)
    mean, rstd = stats[0:1, : s.out], stats[1:2, : s.out]
    inv = spec[3:4, : s.out]
    total = sums[:, : s.out] / count
    cross = sums[:, s.out : 2 * s.out] / count
    norm_scale = inv * rstd
    offset = mean * rstd

    def one(b, e, keep, own):
        par, k = e % 2, e // 2
        dots = jnp.zeros((8, s.out), F32)
        for ph in range(2):
            raw = hidden[b, e, ph]
            normed = raw * norm_scale - offset
            grad = keep * (rstd * (dnorm[b, e, ph] - total - normed * cross))
            if own:
                dots += jnp.sum((grad * raw).reshape(w // 8, 8, s.out), axis=0)
            value = grad * inv
            fill(slots, (b, par, k), ph, value, s.slot)
            if own:
                low[1 - par, ph, b, (e - 1) // 2] = value.astype(BF16)
        return dots

    scale[...] = jnp.zeros_like(scale)

    def sent(b):
        return pltpu.make_async_copy(slots.at[b], slots_to.at[b], sems.at[2, b])

    @pl.loop(0, s.images)
    def _(b):
        pltpu.make_async_copy(hidden_from.at[b], hidden.at[b], sems.at[0, b]).wait()
        pltpu.make_async_copy(dnorm_from.at[b], dnorm.at[b], sems.at[1, b]).wait()
        live = live_of(counts, b)
        one(b, 0, live * inside(-1, s, 2), False)
        dots = jnp.zeros((8, s.out), F32)
        for e in range(1, s.ext - 1):
            dots += one(b, e, live, True)
        one(b, s.ext - 1, live * inside(2 * s.rows, s, 2), False)
        scale[0:1, : s.out] += jnp.sum(dots, axis=0, keepdims=True)
        sent(b).start()

    fetch_acts.wait()
    count = s.images * s.rows * w
    depth = 3 * s.chan
    for dy in range(3):
        total = None
        for phase in range(4):
            a, b = divmod(phase, 2)
            flip = jnp.transpose(low[a, b].reshape(count, s.out))
            first = 1 + (a + dy - 1) // 2
            rhs = acts[:, first : first + s.rows, :, b * s.chan : b * s.chan + depth]
            part = dot(flip, rhs.reshape(count, depth))
            total = part if total is None else total + part
        place(s, grads, total, dy * depth, s.n_one, 0)
    for copy in fetch_two:
        copy.wait()
    grads_two(s, slots_two, grad_low, grad_skip, image, grads)
    copies = []
    for ref, to, which in ((other, other_to, 1 - core), (mine, mine_to, core)):
        for x in range(s.n_x):
            at = pl.multiple_of((which * s.n_x + x) * s.part, 8)
            here = pl.ds(at, s.part)
            for r in range(s.rows_n):
                pack_grad(ref, r * s.n_x + x, grads, here, r * s.pitch, s.wide)
        copies.append(start(ref, to, sems.at[4, len(copies)]))
    for b in range(s.images):
        copies.append(sent(b))
    for copy in copies:
        copy.wait()


def input_grad_kernel(sizes, slots, weight, image, stats, proj, terms_two, scale_one, scale_two,
                      misc, dnorm, pay, back, terms, line):
    s = sizes
    w = s.width
    depth = 3 * s.slot
    back[...] = jnp.zeros_like(back)
    for t in range(9):
        dy, dx = divmod(t, 3)
        tap = weight[t * s.chan : (t + 1) * s.chan, :].astype(F32)
        at = (2 - dx) * s.slot
        back[dy, at : at + s.out, :] = jnp.transpose(tap).astype(BF16)
    total = None
    for a in range(2):
        for dy in range(3):
            par, k = (a + 2 - dy) % 2, (a + 2 - dy) // 2
            for ph in range(2):
                lhs = slots[:, par, k : k + s.rows, :, ph * s.slot : ph * s.slot + depth]
                part = dot(lhs.reshape(s.images * s.rows * w, depth), back[dy])
                total = part if total is None else total + part
    total = total.reshape(s.images, s.rows, w, s.chan)
    mean, rstd = stats[0:1, :], stats[1:2, :]
    all_sum = jnp.zeros((1, s.chan), F32)
    all_cross = jnp.zeros((1, s.chan), F32)
    for b in range(s.images):
        gain = 1.0 + proj[b : b + 1, : s.chan]
        shift = proj[b : b + 1, s.chan : 2 * s.chan]
        dsum = jnp.zeros((8, s.chan), F32)
        dgain = jnp.zeros((8, s.chan), F32)
        for i in range(s.rows):
            normed = (image[b, i].astype(F32) - mean) * rstd
            pre = gain * normed + shift
            sig = sigmoid(pre)
            dpre = total[b, i] * (sig * (1.0 + pre * (1.0 - sig)))
            dnorm[b, i] = gain * dpre
            dsum += jnp.sum(dpre.reshape(w // 8, 8, s.chan), axis=0)
            dgain += jnp.sum((dpre * normed).reshape(w // 8, 8, s.chan), axis=0)
        dsum = jnp.sum(dsum, axis=0, keepdims=True)
        dgain = jnp.sum(dgain, axis=0, keepdims=True)
        terms[b : b + 1, : s.chan] = dgain
        terms[b : b + 1, s.chan : 2 * s.chan] = dsum
        terms[b : b + 1, 2 * s.chan :] = terms_two[b : b + 1, : 2 * s.out]
        all_sum += gain * dsum
        all_cross += gain * dgain
    line[...] = jnp.zeros_like(line)
    line[0:1, : s.chan] = all_sum
    line[0:1, s.chan : 2 * s.chan] = all_cross
    at = s.at_scale
    line[0:1, at : at + 1] = jnp.sum(scale_one[0:1, : s.out], axis=1, keepdims=True)
    line[0:1, at + 1 : at + 2] = scale_two[0:1, 0:1]
    line[0:1, at + 2 : at + 3] = jnp.sum(misc[1:2, : s.out], axis=1, keepdims=True)
    at = s.at_gbias
    line[0:1, at : at + s.out] = misc[0:1, : s.out]
    for r in range(s.rows_n):
        for b in range(s.images):
            at = s.at_terms + b * s.cols
            line[0:1, at : at + s.cols] = terms[b : b + 1, r * s.cols : (r + 1) * s.cols]
        whole = line[...]
        for g in range(s.groups):
            pay[r * s.groups + g] = whole


def adamw(weight, first_old, second, gradient, learn_rate):
    first_new = BETA_ONE * first_old + (1.0 - BETA_ONE) * gradient
    second_new = BETA_TWO * second + (1.0 - BETA_TWO) * gradient * gradient
    first_hat = first_new / (1.0 - BETA_ONE**STEP)
    second_hat = second_new / (1.0 - BETA_TWO**STEP)
    weight_new = weight - learn_rate * (
        first_hat / (jnp.sqrt(second_hat) + ADAM_EPS) + DECAY_RATE * weight
    )
    return (weight_new, first_new, second_new)


def store_adamw(refs, olds, gradient, rate):
    for ref, value in zip(refs, adamw(*(old[...] for old in olds), gradient, rate)):
        ref[...] = value


def finish_kernel(sizes, counts, got, cond_all, image, dnorm, grad_skip, skip_w, stats, proj,
                  cw, cm, cv, bw, bm, bv,
                  image_grad, cw_new, cm_new, cv_new, bw_new, bm_new, bv_new, scales, terms, conds):
    s = sizes
    w = s.width
    row_pos, _, _ = position()
    sums = jnp.sum(got[:, :, : s.at_terms], axis=0)
    scales[...] = jnp.broadcast_to(sums[:, s.at_scale : s.at_scale + LANES], scales.shape)
    count = live_total(counts, s) * (w * w)
    total = sums[:, : s.chan] / count
    cross = sums[:, s.chan : 2 * s.chan] / count
    mean, rstd = stats[0:1, :], stats[1:2, :]
    grad = dot(
        grad_skip[...].reshape(s.images * s.rows * w, s.out), skip_w[...], ((1,), (1,))
    ).reshape(s.images, s.rows, w, s.chan)
    for b in range(s.images):
        keep = live_of(counts, b) * rstd
        for i in range(s.rows):
            normed = (image[b, i].astype(F32) - mean) * rstd
            image_grad[b, i] = keep * (dnorm[b, i] - total - normed * cross) + grad[b, i]
    for g in range(s.groups):
        part = got[g, :, s.at_terms :]
        for r in range(1, s.rows_n):
            part = part + got[r * s.groups + g, :, s.at_terms :]
        for b in range(s.images):
            k = g * s.images + b
            terms[k : k + 1, :] = part[:, b * s.cols : (b + 1) * s.cols]
            conds[k : k + 1, :] = cond_all[g, b : b + 1, :].astype(F32)
    grad = dot(terms[...], conds[...], ((0,), (0,)), precise)
    store_adamw((cw_new, cm_new, cv_new), (cw, cm, cv), grad, LEARN_RATES[3])
    grad = sums[:, s.at_gbias : s.at_gbias + s.n_bias]
    for r in range(1, s.rows_n):
        at = s.at_gbias + r * s.n_bias
        grad = jnp.where(row_pos == r, sums[:, at : at + s.n_bias], grad)
    store_adamw((bw_new, bm_new, bv_new), (bw, bm, bv), grad, LEARN_RATES[4])


def weights_kernel(sizes, own, beside, beyond, across, scales, spec, left_one, left_two, left_skip,
                   ow, om, ov, tw, tm, tv, sw, sm, sv,
                   ow_new, om_new, ov_new, tw_new, tm_new, tv_new, sw_new, sm_new, sv_new, grads):
    s = sizes
    _, x_pos, core = position()
    columns = jnp.transpose(spec[...])

    def factor(k):
        inv = spec[3 + k : 4 + k, 0:1]
        return scales[0:1, k : k + 1] * inv * inv * spec[8 + k : 9 + k, 0:1]

    def place(parts, which):
        for x, part in enumerate(parts):
            at = pl.multiple_of((which * s.n_x + x) * s.part, 8)
            here = pl.ds(at, s.part)
            grads[here, : s.wide] = unpack_grad(part, 0, s.part, s.wide)

    def ordered(mine, other):
        if s.n_x != 2:
            return [mine[x] for x in range(s.n_x)]
        a, b = mine[0], other[0]
        return [jnp.where(x_pos == 0, a, b), jnp.where(x_pos == 0, b, a)]

    place(ordered(own, beside), core)
    place(ordered(beyond, across), 1 - core)

    grad = grads[:, : s.n_one] - columns[: s.out, 0:1] * (left_one[...] * factor(0))
    store_adamw((ow_new, om_new, ov_new), (ow, om, ov), grad, LEARN_RATES[0])
    grad = grads[:, s.n_one : s.n_one + s.n_two] - columns[: s.out, 1:2] * (left_two[...] * factor(1))
    store_adamw((tw_new, tm_new, tv_new), (tw, tm, tv), grad, LEARN_RATES[1])
    grad = jnp.transpose(grads[:, s.n_one + s.n_two : s.wide])
    grad = grad - (left_skip[...] * factor(2)) * spec[2:3, : s.out]
    store_adamw((sw_new, sm_new, sv_new), (sw, sm, sv), grad, LEARN_RATES[2])


def share(chunks):
    return lax.all_to_all(chunks, ALL, 0, 0, tiled=True)


def core_swap(values):
    return lax.ppermute(values, "core", [(0, 1), (1, 0)])


def row_swaps(near, far):
    devices = lax.axis_size("rows")
    pairs = [(i, i ^ 1) for i in range(devices)]
    odd = [(i, i + 1) for i in range(1, devices - 1, 2)]
    odd = odd + [(j, i) for i, j in odd]
    return lax.ppermute(near, "rows", pairs), lax.ppermute(far, "rows", odd)


def row_swap(values, step):
    devices = lax.axis_size("rows")
    return lax.ppermute(values, "rows", [(i, i ^ step) for i in range(devices)])


def x_swap(values):
    return lax.ppermute(values, "x", [(0, 1), (1, 0)])


def gather_upper(block):
    return [block] + [row_swap(block, 2 * m) for m in range(1, lax.axis_size("rows") // 2)]


def gather_groups(values):
    if lax.axis_size("x") != 2:
        return lax.all_gather(values, ("x", "core"), axis=0)
    x, core = lax.axis_index("x"), lax.axis_index("core")
    pair = jnp.stack([values, core_swap(values)])
    pair = jnp.where(core == 0, pair, pair[::-1])
    both = jnp.stack([pair, x_swap(pair)])
    both = jnp.where(x == 0, both, both[::-1])
    return both.reshape(4, *values.shape)


def first_sum_kernel(mine, got, send_a, keep_a, send_b, keep_b):
    _, x, _ = position()
    low = lax.rem(lax.axis_index("rows"), 2)
    half = send_a.shape[0]
    for i in range(half):
        for k in range(2):
            send_a[i, k] = mine[i, k, 1 - x] + got[i, k, 1 - x]
            keep_a[i, k] = mine[i, k, x] + got[i, k, x]
            send_b[i, k] = mine[half + i, 1 - low, k] + got[half + i, 1 - low, k]
            keep_b[i, k] = mine[half + i, low, k] + got[half + i, low, k]


def second_sum_kernel(keep_a, got_a, keep_b, got_b, send_a, held_a, send_b, held_b):
    _, x, _ = position()
    low = lax.rem(lax.axis_index("rows"), 2)
    for i in range(keep_a.shape[0]):
        send_a[i] = keep_a[i, 1 - low] + got_a[i, 1 - low]
        held_a[i] = keep_a[i, low] + got_a[i, low]
        send_b[i] = keep_b[i, 1 - x] + got_b[i, 1 - x]
        held_b[i] = keep_b[i, x] + got_b[i, x]


def third_sum_kernel(held_a, got_a, held_b, got_b, *outs):
    high = lax.axis_index("rows") // 2
    half = held_a.shape[0]
    for m, out in enumerate(outs):
        at = high ^ m

        @pl.when(at < half)
        def _():
            out[0] = held_a[jnp.minimum(at, half - 1)] + got_a[jnp.minimum(at, half - 1)]

        @pl.when(at >= half)
        def _():
            at_b = jnp.maximum(at - half, 0)
            out[0] = held_b[at_b] + got_b[at_b]


def sum_kernel(*refs):
    *parts, out = refs
    total = parts[0][...]
    for part in parts[1:]:
        total = total + part[...]
    out[...] = total


def tied(values, after):
    return list(lax.optimization_barrier((tuple(values), tuple(after)))[0])


class StagedSum:
    small = 8 * 2**20

    def __init__(self, mine, other, after):
        self.high = lax.axis_size("rows") // 2
        self.tail = mine.shape[1:]
        mine = mine.reshape(self.high, 2, 2, *self.tail)
        got = core_swap(other).reshape(self.high, 2, 2, *self.tail)
        send_a, keep_a, send_b, keep_b = run(
            first_sum_kernel,
            [shape((self.high // 2, 2, *self.tail))] * 4,
            tied([mine, got], after),
            scalars=0,
            limit=self.small,
        )
        self.held = [keep_a, x_swap(send_a), keep_b, row_swap(send_b, 1)]

    def second(self, after):
        send_a, held_a, send_b, held_b = run(
            second_sum_kernel,
            [shape((self.high // 2, *self.tail))] * 4,
            tied(self.held, after),
            scalars=0,
            limit=self.small,
        )
        self.held = [held_a, row_swap(send_a, 1), held_b, x_swap(send_b)]

    def third(self, after):
        parts = run(
            third_sum_kernel,
            [shape((1, *self.tail))] * self.high,
            tied(self.held, after),
            scalars=0,
            limit=self.small,
        )
        self.held = [parts[0]] + [row_swap(parts[m], 2 * m) for m in range(1, self.high)]

    def last(self, after):
        (total,) = run(
            sum_kernel,
            [shape((1, *self.tail))],
            tied(self.held, after),
            scalars=0,
            limit=self.small,
        )
        return total


class PlainSum:
    def __init__(self, mine, other, after):
        self.held = lax.all_to_all(mine + core_swap(other), ("rows", "x"), 0, 0, tiled=True)

    def second(self, after):
        pass

    def third(self, after):
        pass

    def last(self, after):
        return jnp.sum(self.held, axis=0, keepdims=True)


def spread(total):
    if lax.axis_size("x") == 2:
        beside = x_swap(total)
        return total, beside, core_swap(total), core_swap(beside)
    total = lax.all_gather(total, "x", axis=0, tiled=True)
    beyond = core_swap(total)
    return total, total, beyond, beyond


def body(
    image_in,
    condition,
    group_counts,
    out_cotangent,
    power_vectors,
    conv1_weight,
    conv2_weight,
    skip_weight,
    cond_weight,
    out_bias,
    conv1_first,
    conv2_first,
    skip_first,
    cond_first,
    bias_first,
    conv1_second,
    conv2_second,
    skip_second,
    cond_second,
    bias_second,
):
    rows_n = lax.axis_size("rows")
    n_x = lax.axis_size("x")
    groups_n = 2 * n_x
    masters = [conv1_weight, conv2_weight, skip_weight, cond_weight, out_bias]
    s = Sizes(
        image_in.shape, out_cotangent.shape, condition.shape, [m.shape for m in masters], rows_n, n_x
    )
    bind = functools.partial
    scratch = pltpu.VMEM
    n, w = s.images, s.width
    depth = 3 * s.slot

    pay, half_one, half_two, near, far, left_one, left_two, left_skip = run(
        bind(prep_kernel, s),
        [
            shape((s.devices, 1, s.pay_one)),
            shape((s.pack_one, LANES), BF16),
            shape((s.pack_two, LANES), BF16),
            shape((n, 3 * w, LANES), BF16),
            shape((n, 3 * w, LANES), BF16),
            shape((1, s.n_one)),
            shape((1, s.n_two)),
            shape((s.n_skip, 1)),
        ],
        [
            group_counts,
            image_in,
            condition,
            power_vectors,
            conv1_weight.T,
            conv2_weight.T,
            skip_weight,
            cond_weight.T,
            out_bias[None],
        ],
        [scratch((1, s.pay_one), F32)],
        limit=60 * 2**20,
    )
    blocks = gather_upper(half_one)
    near, far = row_swaps(near, far)
    (pay,) = tied([pay], [near])
    got_one = share(pay)
    acts, proj, stats_one, spec, near_cot, far_cot = run(
        bind(act_kernel, s),
        [
            shape((n, s.rows + 2, w, 4 * s.chan), BF16),
            shape((n, rows_n * s.cols)),
            shape((2, s.chan)),
            shape((16, s.slot)),
            *[shape((n, 6 * w, LANES), BF16)] * 2,
        ],
        [group_counts, got_one, image_in, near, far],
        [pltpu.SemaphoreType.DMA((2,))],
        flops=0, idle=True,
        whole=[out_cotangent],
        limit=52 * 2**20,
    )
    near_one = jnp.stack(blocks)
    (half_two,) = tied([half_two], [near_one])
    far_one = row_swap(near_one, 1)
    near_two = jnp.stack(gather_upper(half_two))
    far_one, near_two, acts = lax.optimization_barrier((far_one, near_two, acts))
    blocks_one = near_one, far_one, core_swap(near_one), core_swap(far_one)

    far_two = row_swap(near_two, 1)
    near_cot, far_cot = row_swaps(near_cot, far_cot)
    hidden, weight_one, pay = run(
        bind(conv_one_kernel, s),
        [
            shape((n, s.ext, 2, w, s.out)),
            shape((9 * s.chan, s.out), BF16),
            shape((s.devices, 1, s.pay_two)),
        ],
        [group_counts, acts, *blocks_one],
        [scratch((1, s.pay_two), F32), scratch((9 * s.chan, s.out), F32)],
        flops=2 * n * s.ext * 2 * w * 9 * s.chan * s.out,
        limit=52 * 2**20,
    )
    far_two, near_cot, far_cot, pay = lax.optimization_barrier((far_two, near_cot, far_cot, pay))
    blocks_two = near_two, far_two, core_swap(near_two), core_swap(far_two)
    got_two = share(pay)
    dact, phases, grad_low, grad_skip, skip_part, weight_two, weight_skip, misc = run(
        bind(cot_kernel, s),
        [
            shape((n, s.ext, 2, w, s.out)),
            shape((n, 2 * s.rows, 2, w, s.out), BF16),
            shape((n, 2 * s.rows, 2, w, s.out), BF16),
            shape((n, s.rows, w, s.out), BF16),
            shape((n, s.rows, w, s.out)),
            shape((3, depth, s.out), BF16),
            shape((s.chan, s.out), BF16),
            shape((8, s.slot)),
        ],
        [group_counts, out_cotangent, near_cot, far_cot, image_in, *blocks_two, spec],
        [
            scratch((n, 2 * s.rows + 4, w, 4 * s.slot), BF16),
            scratch((9 * s.out + s.chan, s.out), F32),
            scratch((2, 2 * w, LANES), F32),
            scratch((3, depth, s.out), BF16),
        ],
        flops=2 * n * s.ext * 2 * w * 9 * s.out * s.out,
        limit=52 * 2**20,
    )
    stats_two, terms_two, pay, slots_two, dnorm = run(
        bind(norm_two_kernel, s),
        [shape((2, s.slot)), shape((8, 2 * s.slot)), shape((s.devices, 1, s.pay_two))],
        [group_counts, got_two, spec, proj],
        [scratch((1, s.pay_two), F32), pltpu.SemaphoreType.DMA((4, n))],
        whole=[hidden, dact],
        results=[shape((n, s.ext, w, 4 * s.slot), BF16), shape((n, s.ext, 2, w, s.out))],
        limit=53 * 2**20,
    )
    got_three = share(pay)
    sent = shape((s.rows_n * n_x, s.grad_rows, LANES))
    scale_one, other, mine, slots_one = run(
        bind(hidden_grad_kernel, s),
        [shape((8, s.slot))],
        [group_counts, got_three, stats_two, spec, grad_skip, image_in],
        [
            scratch((2, 2, n, s.rows, w, s.out), BF16),
            scratch((s.out, rows_n * s.pitch), F32),
            pltpu.SemaphoreType.DMA((5, max(n, 3))),
        ],
        flops=8 * n * s.rows * w * 9 * s.chan * s.out,
        whole=[dnorm, hidden, acts, slots_two, grad_low],
        results=[sent, sent, shape((n, 2, s.rows + 1, w, 4 * s.slot), BF16)],
        limit=48 * 2**20,
    )
    out_image, scale_two = run(
        bind(conv_two_kernel, s),
        [shape(out_cotangent.shape, BF16), shape((8, LANES))],
        tied([slots_two, weight_two, phases, skip_part, spec], [scale_one]),
        [scratch((2, 2 * w, LANES), F32)],
        scalars=0,
        flops=8 * n * s.rows * 2 * w * 9 * s.out * s.out,
        limit=48 * 2**20,
    )
    sums = (StagedSum if n_x == 2 else PlainSum)(mine, other, [scale_two])
    dnorm_one, pay = run(
        bind(input_grad_kernel, s),
        [shape((n, s.rows, w, s.chan)), shape((s.devices, 1, s.pay_four))],
        [slots_one, weight_one, image_in, stats_one, proj, terms_two, scale_one, scale_two, misc],
        [
            scratch((3, depth, s.chan), BF16),
            scratch((8, rows_n * s.cols), F32),
            scratch((1, s.pay_four), F32),
        ],
        scalars=0,
        flops=8 * n * s.rows * w * 9 * s.chan * s.out,
    )
    sums.second([pay])
    late_condition, pay = lax.optimization_barrier((condition, pay))
    cond_all = gather_groups(late_condition)
    got_four = share(pay)
    sums.third([got_four])
    moments = [cond_weight, cond_first, cond_second]
    biases = [out_bias, bias_first, bias_second]
    image_grad, *rest, scales = run(
        bind(finish_kernel, s),
        [
            shape(image_in.shape),
            *[shape((s.cols, s.cond))] * 3,
            *[shape((1, s.n_bias))] * 3,
            shape((8, LANES)),
        ],
        [
            group_counts,
            got_four,
            cond_all,
            image_in,
            dnorm_one,
            grad_skip,
            weight_skip,
            stats_one,
            proj,
            *[m.T for m in moments],
            *[b[None] for b in biases],
        ],
        [
            scratch((groups_n * n, s.cols), F32),
            scratch((groups_n * n, s.cond), F32),
        ],
        limit=60 * 2**20,
    )
    parts = spread(sums.last([scales]))
    cond_new = [c.T for c in rest[:3]]
    bias_new = [b[0] for b in rest[3:]]
    olds = [
        *[m.T for m in (conv1_weight, conv1_first, conv1_second)],
        *[m.T for m in (conv2_weight, conv2_first, conv2_second)],
        skip_weight,
        skip_first,
        skip_second,
    ]
    news = run(
        bind(weights_kernel, s),
        [shape(o.shape) for o in olds],
        [*parts, scales, spec, left_one, left_two, left_skip, *olds],
        [scratch((s.out, s.pitch), F32)],
        limit=24 * 2**20,
        scalars=0,
    )
    weights_new = [m.T for m in news[:6]] + list(news[6:])
    return (out_image, image_grad, *weights_new, *cond_new, *bias_new)


def solution(mesh):
    rows_n, imgs_n = mesh.devices.shape
    fine = Mesh(np.asarray(mesh.devices).reshape(rows_n, imgs_n // 2, 2), ALL)
    groups = ("x", "core")
    picture = P(groups, "rows", None, None)
    weight = P("rows", None)
    column = P(None, "rows")
    masters = (weight, weight, weight, column, P("rows"))
    return jax.shard_map(
        body,
        mesh=fine,
        in_specs=(picture, P(groups, None), P(), picture, P(), *masters, *masters, *masters),
        out_specs=(
            picture,
            picture,
            *(weight,) * 9,
            *(column,) * 3,
            *(P("rows"),) * 3,
        ),
        check_vma=False,
    )
```

```python
import functools

import jax
import jax.numpy as jnp
import numpy as np
from jax import lax
from jax.experimental import pallas as pl
from jax.experimental.pallas import tpu as pltpu
from jax.sharding import Mesh
from jax.sharding import PartitionSpec as P

STEP = 10
precise = lax.Precision.HIGHEST
NORM_EPS = 1e-05
BETA_ONE = 0.9
BETA_TWO = 0.999
ADAM_EPS = 1e-08
DECAY_RATE = 0.01
LEARN_RATES = (0.02, 0.02, 0.05, 0.03, 0.15)
ALL = ("rows", "x", "core")
F32, BF16 = jnp.float32, jnp.bfloat16
LANES = 128
VMEM_LIMIT = 56 * 2**20


def shape(dims, kind=F32):
    return jax.ShapeDtypeStruct(tuple(dims), kind)


def run(kernel, outs, args, scratch=(), scalars=1, flops=0, limit=VMEM_LIMIT, whole=(), results=(), idle=False):
    spec = pl.BlockSpec(memory_space=pltpu.VMEM)
    specs = [pl.BlockSpec(memory_space=pltpu.SMEM)] * scalars + [spec] * (len(args) - scalars)
    specs += [pl.BlockSpec(memory_space=pl.ANY)] * len(whole)
    moved = sum(a.size * a.dtype.itemsize for a in args)
    moved += sum(np.prod(o.shape) * np.dtype(o.dtype).itemsize for o in outs)
    args = [*args, *whole]
    if idle:
        moved = 0
    scratch = [pltpu.VMEM(a.shape, a.dtype) for a in (*whole, *results)] + list(scratch)
    out_specs = [spec] * len(outs) + [pl.BlockSpec(memory_space=pl.ANY)] * len(results)
    outs = [*outs, *results]
    return pl.pallas_call(
        kernel,
        out_shape=tuple(outs),
        in_specs=specs,
        out_specs=tuple(out_specs),
        scratch_shapes=scratch,
        cost_estimate=pl.CostEstimate(
            flops=int(flops), bytes_accessed=int(moved), transcendentals=0
        ),
        compiler_params=pltpu.CompilerParams(vmem_limit_bytes=limit),
    )(*args)


def round_up(value, step):
    return -(-value // step) * step


class Sizes:
    def __init__(self, image, cot, condition, masters, rows_n, n_x):
        self.images, self.rows, self.width, self.chan = image
        self.out = cot[3]
        self.slot = round_up(self.out, LANES)
        self.ext = 2 * self.rows + 2
        self.cond = condition[1]
        self.n_one, self.n_two, self.n_skip = masters[0][0], masters[1][0], masters[2][0]
        self.cols = masters[3][1]
        self.n_bias = masters[4][0]
        self.rows_n, self.groups = rows_n, 2 * n_x
        self.devices = rows_n * self.groups
        self.h_one = round_up(-(-self.n_one // 2), 8)
        self.h_two = round_up(-(-self.n_two // 2), 8)
        self.h_skip = round_up(-(-self.n_skip // 2), 8)
        self.pack_one = round_up(packed_rows(self.h_one), 16)
        self.pack_two = round_up(packed_rows(self.h_two + self.h_skip), 16)
        self.at_power = 2 * self.chan
        self.at_norm = self.at_power + 3 * self.out
        self.at_bias = self.at_norm + 8
        self.at_proj = round_up(self.at_bias + self.n_bias, LANES)
        self.pay_one = round_up(self.at_proj + self.images * self.cols, LANES)
        self.pay_two = round_up(2 * self.out, LANES)
        self.at_scale = 2 * self.chan
        self.at_gbias = self.at_scale + HALF
        self.at_terms = self.at_gbias + self.out
        self.pay_four = round_up(self.at_terms + self.images * self.cols, LANES)
        self.part = self.out // 2 // n_x
        self.n_x = n_x
        self.wide = self.n_one + self.n_two + self.n_skip
        self.pitch = round_up(self.wide, LANES)
        self.grad_rows = grad_rows(self.part, self.wide)


HALF = LANES // 2


def from_row(near, far, row):
    row_pos = lax.axis_index("rows")
    at = (row_pos // 2) ^ (row // 2)
    same = lax.rem(row_pos, 2) == row % 2
    return jnp.where(same, near[at].astype(F32), far[at].astype(F32))


def packed_rows(rows):
    return rows + round_up(-(-rows // 2), 8)


def pack(values):
    rows = values.shape[0]
    h = round_up(-(-rows // 2), 8)
    right = values[:, LANES:]
    return jnp.concatenate(
        [values[:, :LANES], jnp.concatenate([right[:h], right[rows - h :]], axis=1)], axis=0
    )


def unpack(values, rows):
    h = round_up(-(-rows // 2), 8)
    right = values[rows : rows + h]
    low = jnp.concatenate([right[:, :HALF], right[2 * h - rows :, HALF:]], axis=0)
    return jnp.concatenate([values[:rows], low], axis=1)


def grad_rows(part, width):
    tail = width % LANES
    rows = part * (width // LANES)
    if tail:
        rows += part // 2 if tail <= HALF and part % 16 == 0 else part
    return rows


def pack_grad(ref, lead, grads, here, begin, width):
    part = here.size
    full = width // LANES
    for k in range(full):
        at = begin + k * LANES
        ref[lead, k * part : (k + 1) * part, :] = grads[here, at : at + LANES]
    tail = width - full * LANES
    if not tail:
        return
    at = full * part
    rest = grads[here, begin + full * LANES : begin + (full + 1) * LANES]
    if tail <= HALF and part % 16 == 0:
        h = part // 2
        ref[lead, at : at + h, :] = jnp.concatenate([rest[:h, :HALF], rest[h:, :HALF]], axis=1)
    else:
        ref[lead, at : at + part, :] = rest


def unpack_grad(values, at, part, width):
    full = width // LANES
    pieces = [values[at + k * part : at + (k + 1) * part] for k in range(full)]
    at += full * part
    tail = width - full * LANES
    if tail and tail <= HALF and part % 16 == 0:
        h = part // 2
        both = values[at : at + h]
        pieces.append(
            jnp.concatenate([both[:, :tail], both[:, HALF : HALF + tail]], axis=0)
        )
    elif tail:
        pieces.append(values[at : at + part, :tail])
    return pieces[0] if len(pieces) == 1 else jnp.concatenate(pieces, axis=1)


def position():
    return lax.axis_index("rows"), lax.axis_index("x"), lax.axis_index("core")


def group_position():
    return lax.axis_index("x") * lax.axis_size("core") + lax.axis_index("core")


def live_of(counts, image):
    return jnp.where(image < counts[group_position()], 1.0, 0.0).astype(F32)


def live_total(counts, sizes):
    total = counts[0]
    for g in range(1, sizes.groups):
        total = total + counts[g]
    return total.astype(F32)


def inside(row, sizes, scale):
    at = lax.axis_index("rows") * (scale * sizes.rows) + row
    return jnp.where((at >= 0) & (at < scale * sizes.rows * sizes.rows_n), 1.0, 0.0).astype(F32)


def start(source, target, sem):
    copy = pltpu.make_async_copy(source, target, sem)
    copy.start()
    return copy


def sigmoid(values):
    return 1.0 / (1.0 + jnp.exp(-values))


def shifted(values, step):
    width = values.shape[0]
    rolled = pltpu.roll(values, (-step) % width, 0)
    where = lax.broadcasted_iota(jnp.int32, values.shape, 0)
    edge = 0 if step < 0 else width - 1
    return jnp.where(where == edge, 0.0, rolled)


def padded(values, size):
    rest = size - values.shape[1]
    if not rest:
        return values
    return jnp.concatenate([values, jnp.zeros((values.shape[0], rest), values.dtype)], axis=1)


def fill(ref, where, phase, value, slot):
    value = padded(value, slot)
    at = (1 + phase) * slot
    ref[(*where, slice(None), slice(at, at + slot))] = value.astype(BF16)
    step, at = (-1, 0) if phase else (1, 3 * slot)
    ref[(*where, slice(None), slice(at, at + slot))] = shifted(value, step).astype(BF16)


def dot(a, b, dims=((1,), (0,)), precision=None):
    return lax.dot_general(a, b, (dims, ((), ())), preferred_element_type=F32, precision=precision)


def prep_kernel(sizes, counts, image, cond, vec, one_t, two_t, skip, cond_t, bias,
                pay, half_one, half_two, near, far, left_one, left_two,
                left_skip, line):
    s = sizes
    row_pos, _, core = position()
    even = lax.rem(row_pos, 2) == 0
    last, w = s.rows - 1, s.width

    line[...] = jnp.zeros_like(line)
    vec_t = jnp.transpose(jnp.concatenate([vec[...], jnp.zeros((5, s.out), F32)], axis=0))

    def power(k, low):
        column = jnp.sum(low * vec[k : k + 1, :], axis=1, keepdims=True)
        row = jnp.sum(low * column, axis=0, keepdims=True)
        at = s.at_power + k * s.out
        line[0:1, at : at + s.out] = row
        at = s.at_norm + k
        line[0:1, at : at + 1] = jnp.sum(column * column, axis=0, keepdims=True)
        return column

    low_t = one_t[...].astype(BF16).astype(F32)
    left_one[...] = jnp.sum(low_t * vec_t[:, 0:1], axis=0, keepdims=True)
    low = jnp.transpose(low_t)
    power(0, low)
    n, h = s.n_one, s.h_one
    packed_one = pack(jnp.where(core == 0, low[:h], low[n - h :]))
    low_t = two_t[...].astype(BF16).astype(F32)
    left_two[...] = jnp.sum(low_t * vec_t[:, 1:2], axis=0, keepdims=True)
    low = jnp.transpose(low_t)
    power(1, low)
    n, h = s.n_two, s.h_two
    half_a = jnp.where(core == 0, low[:h], low[n - h :])
    low = skip[...].astype(BF16).astype(F32)
    left_skip[...] = power(2, low)
    n, h = s.n_skip, s.h_skip
    half_b = jnp.where(core == 0, low[:h], low[n - h :])
    packed = pack(jnp.concatenate([half_a, half_b], axis=0))
    if s.pack_two > packed.shape[0]:
        packed = jnp.concatenate(
            [packed, jnp.zeros((s.pack_two - packed.shape[0], LANES), F32)], axis=0
        )
    packed = packed.astype(BF16)
    half_two[...] = packed
    line[0:1, s.at_bias : s.at_bias + s.n_bias] = bias[...].astype(BF16).astype(F32)
    proj = dot(cond[...], cond_t[...].astype(BF16), ((1,), (1,)))
    for b in range(s.images):
        at = s.at_proj + b * s.cols
        line[0:1, at : at + s.cols] = proj[b : b + 1]
    if s.pack_one > packed_one.shape[0]:
        packed_one = jnp.concatenate(
            [packed_one, jnp.zeros((s.pack_one - packed_one.shape[0], LANES), F32)], axis=0
        )
    half_one[...] = packed_one.astype(BF16)

    def edges(ref, row):
        for t in range(3):
            ref[:, t * w : (t + 1) * w, :] = image[:, row, :, t * LANES : (t + 1) * LANES]

    @pl.when(even)
    def _():
        edges(near, last)
        edges(far, 0)

    @pl.when(jnp.logical_not(even))
    def _():
        edges(near, 0)
        edges(far, last)

    sums = jnp.zeros((8, s.chan), F32)
    squares = jnp.zeros((8, s.chan), F32)
    for b in range(s.images):
        part = jnp.zeros((8, s.chan), F32)
        part_sq = jnp.zeros((8, s.chan), F32)
        for i in range(s.rows):
            x = image[b, i].astype(F32).reshape(w // 8, 8, s.chan)
            part += jnp.sum(x, axis=0)
            part_sq += jnp.sum(x * x, axis=0)
        sums += part * live_of(counts, b)
        squares += part_sq * live_of(counts, b)
    line[0:1, : s.chan] = jnp.sum(sums, axis=0, keepdims=True)
    line[0:1, s.chan : 2 * s.chan] = jnp.sum(squares, axis=0, keepdims=True)
    whole = line[...]
    for d in range(s.devices):
        pay[d] = whole


def act_kernel(sizes, counts, got, image, near, far, cot, slots, proj, stats, spec,
               near_cot, far_cot, rows, sems):
    s = sizes
    row_pos, _, _ = position()
    even = lax.rem(row_pos, 2) == 0
    copies = [
        start(cot.at[:, pl.ds(at, 2)], rows.at[:, pl.ds(at, 2)], sems.at[k])
        for k, at in enumerate(sorted({0, 2 * s.rows - 2}))
    ]
    group = group_position()
    sums = jnp.sum(got[:, :, : 2 * s.chan], axis=0)
    count = live_total(counts, s) * (s.width * s.width)
    mean = sums[:, : s.chan] / count
    rstd = lax.rsqrt(sums[:, s.chan :] / count - mean * mean + NORM_EPS)
    stats[0:1, :] = mean
    stats[1:2, :] = rstd

    spec[...] = jnp.zeros_like(spec)
    total = None
    for r in range(s.rows_n):
        piece = got[r * s.groups + group, :, s.at_power :]
        part = piece[:, : s.at_proj - s.at_power]
        total = part if total is None else total + part
        at = s.at_bias - s.at_power
        spec[6:7, r * s.n_bias : (r + 1) * s.n_bias] = piece[:, at : at + s.n_bias]
        for b in range(s.images):
            at = s.at_proj - s.at_power + b * s.cols
            proj[b : b + 1, r * s.cols : (r + 1) * s.cols] = piece[:, at : at + s.cols]
    for k in range(3):
        at = s.at_norm - s.at_power + k
        inv_norm = lax.rsqrt(total[:, at : at + 1])
        row = total[:, k * s.out : (k + 1) * s.out] * inv_norm
        inv_sigma = lax.rsqrt(jnp.sum(row * row, axis=1, keepdims=True))
        spec[k : k + 1, : s.out] = row * inv_sigma
        spec[3 + k : 4 + k, :] = jnp.broadcast_to(inv_sigma, (1, s.slot))
        spec[8 + k : 9 + k, :] = jnp.broadcast_to(inv_norm, (1, s.slot))

    w = s.width

    def one(b, e, x, keep):
        gain = 1.0 + proj[pl.ds(b, 1), : s.chan]
        shift = proj[pl.ds(b, 1), s.chan : 2 * s.chan]
        pre = gain * ((x - mean) * rstd) + shift
        act = pre * sigmoid(pre)
        if keep is not None:
            act = act * keep
        low = act.astype(BF16)
        slots[b, e, :, s.chan : 2 * s.chan] = low
        slots[b, e, :, 2 * s.chan : 3 * s.chan] = low
        slots[b, e, :, : s.chan] = shifted(act, -1).astype(BF16)
        slots[b, e, :, 3 * s.chan :] = shifted(act, 1).astype(BF16)

    def edge(ref, b):
        return jnp.concatenate(
            [ref[b, t * w : (t + 1) * w, :].astype(F32) for t in range(3)], axis=1
        )

    @pl.loop(0, s.images)
    def _(b):
        a, c = edge(near, b), edge(far, b)
        one(b, 0, jnp.where(even, c, a), inside(-1, s, 1))
        for i in range(s.rows):
            one(b, i + 1, image[b, i].astype(F32), None)
        one(b, s.rows + 1, jnp.where(even, a, c), inside(s.rows, s, 1))

    for copy in copies:
        copy.wait()

    def cot_edges(ref, row):
        for b in range(s.images):
            for k in range(2):
                ref[b, 2 * w * k : 2 * w * (k + 1), :] = rows[b, row + k, :, :LANES]
            right = [rows[b, row + k, :, LANES:].astype(F32) for k in range(2)]
            ref[b, 4 * w :, :] = jnp.concatenate(right, axis=1).astype(BF16)

    @pl.when(even)
    def _():
        cot_edges(near_cot, 2 * s.rows - 2)
        cot_edges(far_cot, 0)

    @pl.when(jnp.logical_not(even))
    def _():
        cot_edges(near_cot, 0)
        cot_edges(far_cot, 2 * s.rows - 2)


def conv_one_kernel(sizes, counts, slots, mine_near, mine_far, other_near, other_far, hidden, weight, pay, line, wide):
    s = sizes
    _, _, core = position()
    first = core == 0
    for r in range(s.rows_n):
        a = unpack(from_row(mine_near, mine_far, r), s.h_one)
        b = unpack(from_row(other_near, other_far, r), s.h_one)
        at = r * s.n_one
        wide[at : at + s.h_one, :] = jnp.where(first, a, b)
        at += s.n_one - s.h_one
        wide[at : at + s.h_one, :] = jnp.where(first, b, a)
    for t in range(9):
        weight[t * s.chan : (t + 1) * s.chan] = wide[t * s.chan : (t + 1) * s.chan, :].astype(BF16)
    depth = 3 * s.chan
    rows = s.rows + 1
    sums = jnp.zeros((8, s.out), F32)
    squares = jnp.zeros((8, s.out), F32)
    for phase in range(4):
        a, b = divmod(phase, 2)
        total = None
        for dy in range(3):
            at = (a + dy - 1) // 2 + 1 - a
            lhs = slots[:, at : at + rows, :, b * s.chan : b * s.chan + depth]
            part = dot(
                lhs.reshape(s.images * rows * s.width, depth),
                weight[dy * depth : (dy + 1) * depth, :],
            )
            total = part if total is None else total + part
        total = total.reshape(s.images, rows, s.width, s.out)
        for i in range(s.images):
            part = jnp.zeros((8, s.out), F32)
            part_sq = jnp.zeros((8, s.out), F32)
            for k in range(rows):
                e = 2 * k + 1 - a
                value = total[i, k]
                hidden[i, e, b] = value
                if 0 < e < s.ext - 1:
                    x = value.reshape(s.width // 8, 8, s.out)
                    part += jnp.sum(x, axis=0)
                    part_sq += jnp.sum(x * x, axis=0)
            sums += part * live_of(counts, i)
            squares += part_sq * live_of(counts, i)
    line[...] = jnp.zeros_like(line)
    line[0:1, : s.out] = jnp.sum(sums, axis=0, keepdims=True)
    line[0:1, s.out : 2 * s.out] = jnp.sum(squares, axis=0, keepdims=True)
    whole = line[...]
    for d in range(s.devices):
        pay[d] = whole


def cot_kernel(sizes, counts, cot, near, far, image, mine_near, mine_far, other_near, other_far, spec, dact, phases, grad_low,
               grad_skip, skip_part, two, skip_w, misc, slots, wide, pair, flip):
    s = sizes
    row_pos, _, core = position()
    even = lax.rem(row_pos, 2) == 0
    first = core == 0
    w = s.width
    for r in range(s.rows_n):
        a = unpack(from_row(mine_near, mine_far, r), s.h_two + s.h_skip)
        b = unpack(from_row(other_near, other_far, r), s.h_two + s.h_skip)
        lo, hi = jnp.where(first, a, b), jnp.where(first, b, a)
        at = r * s.n_two
        wide[at : at + s.h_two, :] = lo[: s.h_two]
        at += s.n_two - s.h_two
        wide[at : at + s.h_two, :] = hi[: s.h_two]
        at = 9 * s.out + r * s.n_skip
        wide[at : at + s.h_skip, :] = lo[s.h_two :]
        at += s.n_skip - s.h_skip
        wide[at : at + s.h_skip, :] = hi[s.h_two :]
    two[...] = jnp.zeros_like(two)
    flip[...] = jnp.zeros_like(flip)
    for t in range(9):
        dy, dx = divmod(t, 3)
        tap = wide[t * s.out : (t + 1) * s.out, :]
        two[dy, dx * s.slot : dx * s.slot + s.out, :] = tap.astype(BF16)
        back = jnp.transpose(tap).astype(BF16)
        flip[2 - dy, (2 - dx) * s.slot : (2 - dx) * s.slot + s.out, :] = back
    skip_w[...] = wide[9 * s.out : 9 * s.out + s.chan, :].astype(BF16)

    inv_two = spec[4:5, : s.out]
    inv_skip = spec[5:6, : s.out]

    def split(b, q, row, own):
        pair[0] = row[:, :LANES]
        pair[1, :, : s.out - LANES] = row[:, LANES:]
        both = []
        for ph in range(2):
            value = jnp.concatenate(
                [pair[0, pl.ds(ph, w, 2), :], pair[1, pl.ds(ph, w, 2), :][:, : s.out - LANES]],
                axis=1,
            )
            low = (value * inv_two).astype(BF16)
            both.append(value)
            if own is not None:
                phases[b, own, ph] = value.astype(BF16)
                grad_low[b, own, ph] = low
            fill(slots, (b, q), ph, low.astype(F32), s.slot)
        return both[0] + both[1]

    def edge_row(ref, b, k):
        right = ref[b, 4 * w :, :].astype(F32)
        return jnp.concatenate(
            [
                ref[b, 2 * w * k : 2 * w * (k + 1), :].astype(F32),
                right[:, k * HALF : k * HALF + s.out - LANES],
            ],
            axis=1,
        )

    misc[...] = jnp.zeros_like(misc)

    @pl.loop(0, s.images)
    def _(b):
        live = live_of(counts, b)
        above = inside(-1, s, 1) * live
        below = inside(s.rows, s, 1) * live
        for k in range(2):
            a, c = edge_row(near, b, k), edge_row(far, b, k)
            split(b, k, jnp.where(even, c, a) * above, None)
            split(b, 2 * s.rows + 2 + k, jnp.where(even, a, c) * below, None)
        bias = jnp.zeros((1, s.out), F32)
        skip_sum = jnp.zeros((1, s.out), F32)
        for i in range(s.rows):
            pooled = split(b, 2 * i + 2, cot[b, 2 * i].astype(F32) * live, 2 * i)
            pooled += split(b, 2 * i + 3, cot[b, 2 * i + 1].astype(F32) * live, 2 * i + 1)
            grad_skip[b, i] = (pooled * inv_skip).astype(BF16)
            bias += jnp.sum(pooled, axis=0, keepdims=True)
            raw = dot(image[b, i], skip_w[...])
            skip_part[b, i] = raw * inv_skip
            skip_sum += jnp.sum(pooled * raw, axis=0, keepdims=True)
        misc[0:1, : s.out] += bias
        misc[1:2, : s.out] += skip_sum

    depth = 3 * s.slot
    for ph in range(2):
        total = None
        for dy in range(3):
            lhs = slots[:, dy : dy + s.ext, :, ph * s.slot : ph * s.slot + depth]
            part = dot(lhs.reshape(s.images * s.ext * w, depth), flip[dy])
            total = part if total is None else total + part
        dact[:, :, ph] = total.reshape(s.images, s.ext, w, s.out)


def norm_two_kernel(sizes, counts, got, spec, proj, hidden_from, dact_from, stats, terms, pay,
                    slots_to, dnorm_to, hidden, dact, slots, dnorm, line, sems):
    s = sizes
    w = s.width
    for b in range(s.images):
        start(hidden_from.at[b], hidden.at[b], sems.at[0, b])
        start(dact_from.at[b], dact.at[b], sems.at[1, b])
    inv = spec[3:4, : s.out]
    sums = jnp.sum(got[...], axis=0)
    count = live_total(counts, s) * (4 * w * w)
    mean = sums[:, : s.out] * inv / count
    square = sums[:, s.out : 2 * s.out] * inv * inv / count
    rstd = lax.rsqrt(square - mean * mean + NORM_EPS)
    stats[0:1, : s.out] = mean
    stats[1:2, : s.out] = rstd
    scale = inv * rstd
    offset = mean * rstd
    base = 2 * s.chan

    def one(b, e, keep):
        gain = 1.0 + proj[pl.ds(b, 1), base : base + s.out]
        shift = proj[pl.ds(b, 1), base + s.out : base + 2 * s.out]
        dsum = jnp.zeros((8, s.out), F32)
        dgain = jnp.zeros((8, s.out), F32)
        for ph in range(2):
            normed = hidden[b, e, ph] * scale - offset
            pre = gain * normed + shift
            sig = sigmoid(pre)
            act = pre * sig
            if keep is not None:
                act = act * keep
            fill(slots, (b, e), ph, act, s.slot)
            dpre = dact[b, e, ph] * (sig * (1.0 + pre * (1.0 - sig)))
            dnorm[b, e, ph] = gain * dpre
            if keep is None:
                dsum += jnp.sum(dpre.reshape(w // 8, 8, s.out), axis=0)
                dgain += jnp.sum((dpre * normed).reshape(w // 8, 8, s.out), axis=0)
        return dsum, dgain

    terms[...] = jnp.zeros_like(terms)

    def sent(b):
        return [
            pltpu.make_async_copy(slots.at[b], slots_to.at[b], sems.at[2, b]),
            pltpu.make_async_copy(dnorm.at[b], dnorm_to.at[b], sems.at[3, b]),
        ]

    @pl.loop(0, s.images)
    def _(b):
        pltpu.make_async_copy(hidden_from.at[b], hidden.at[b], sems.at[0, b]).wait()
        pltpu.make_async_copy(dact_from.at[b], dact.at[b], sems.at[1, b]).wait()
        one(b, 0, inside(-1, s, 2))
        dsum = jnp.zeros((8, s.out), F32)
        dgain = jnp.zeros((8, s.out), F32)
        for e in range(1, s.ext - 1):
            a, c = one(b, e, None)
            dsum += a
            dgain += c
        one(b, s.ext - 1, inside(2 * s.rows, s, 2))
        terms[pl.ds(b, 1), : s.out] = jnp.sum(dgain, axis=0, keepdims=True)
        terms[pl.ds(b, 1), s.out : 2 * s.out] = jnp.sum(dsum, axis=0, keepdims=True)
        for copy in sent(b):
            copy.start()

    total = jnp.zeros((1, s.out), F32)
    cross = jnp.zeros((1, s.out), F32)
    for b in range(s.images):
        gain = 1.0 + proj[b : b + 1, base : base + s.out]
        cross += gain * terms[b : b + 1, : s.out]
        total += gain * terms[b : b + 1, s.out : 2 * s.out]
    line[...] = jnp.zeros_like(line)
    line[0:1, : s.out] = total
    line[0:1, s.out : 2 * s.out] = cross
    whole = line[...]
    for d in range(s.devices):
        pay[d] = whole
    for b in range(s.images):
        for copy in sent(b):
            copy.wait()


def conv_two_kernel(sizes, slots, two, phases, skip_part, spec, out, scale, pair):
    s = sizes
    w = s.width
    depth = 3 * s.slot
    own = 2 * s.rows
    inv_two = spec[4:5, : s.out]
    bias = spec[6:7, : s.out]
    dots = jnp.zeros((1, s.out), F32)
    results = []
    for ph in range(2):
        total = None
        for dy in range(3):
            lhs = slots[:, dy : dy + own, :, ph * s.slot : ph * s.slot + depth]
            part = dot(lhs.reshape(s.images * own * w, depth), two[dy])
            total = part if total is None else total + part
        results.append(total.reshape(s.images, own, w, s.out))
    for b in range(s.images):
        for e in range(own):
            for ph in range(2):
                raw = results[ph][b, e]
                dots += jnp.sum(raw * phases[b, e, ph].astype(F32), axis=0, keepdims=True)
                value = raw * inv_two + skip_part[b, e // 2] + bias
                pair[0, pl.ds(ph, w, 2), :] = value[:, :LANES]
                pair[1, pl.ds(ph, w, 2), :] = jnp.concatenate(
                    [value[:, LANES:], jnp.zeros((w, 2 * LANES - s.out), F32)], axis=1
                )
            out[b, e, :, :LANES] = pair[0].astype(BF16)
            out[b, e, :, LANES:] = pair[1][:, : s.out - LANES].astype(BF16)
    scale[...] = jnp.broadcast_to(jnp.sum(dots, axis=1, keepdims=True), scale.shape)


def place(s, grads, values, first, shard, offset):
    end = first + values.shape[1]
    for r in range(first // shard, (end - 1) // shard + 1):
        low, high = max(first, r * shard), min(end, (r + 1) * shard)
        at = r * s.pitch + offset + low - r * shard
        grads[:, at : at + high - low] = values[:, low - first : high - first]


def grads_two(s, slots, grad_low, grad_skip, image, grads):
    w = s.width
    own = 2 * s.rows
    depth = 3 * s.slot
    count = s.images * own * w
    flips = [jnp.transpose(grad_low[:, :, ph].reshape(count, s.out)) for ph in range(2)]
    for dy in range(3):
        total = None
        for ph in range(2):
            rhs = slots[:, dy : dy + own, :, ph * s.slot : ph * s.slot + depth]
            part = dot(flips[ph], rhs.reshape(count, depth))
            total = part if total is None else total + part
        for dx in range(3):
            tap = total[:, dx * s.slot : dx * s.slot + s.out]
            place(s, grads, tap, (3 * dy + dx) * s.out, s.n_two, s.n_one)
    count = s.images * s.rows * w
    flip = jnp.transpose(grad_skip[...].reshape(count, s.out))
    place(s, grads, dot(flip, image[...].reshape(count, s.chan)), 0, s.n_skip, s.n_one + s.n_two)


def hidden_grad_kernel(sizes, counts, got, stats, spec, grad_skip, image,
                       dnorm_from, hidden_from, acts_from, slots_two_from, grad_low_from,
                       scale, other_to, mine_to, slots_to,
                       dnorm, hidden, acts, slots_two, grad_low, other, mine, slots,
                       low, grads, sems):
    s = sizes
    _, _, core = position()
    w = s.width
    for b in range(s.images):
        start(hidden_from.at[b], hidden.at[b], sems.at[0, b])
        start(dnorm_from.at[b], dnorm.at[b], sems.at[1, b])
    fetch_acts = start(acts_from, acts, sems.at[3, 0])
    fetch_two = [
        start(slots_two_from, slots_two, sems.at[3, 1]),
        start(grad_low_from, grad_low, sems.at[3, 2]),
    ]
    sums = jnp.sum(got[...], axis=0)
    count = live_total(counts, s) * (4 * w * w)
    mean, rstd = stats[0:1, : s.out], stats[1:2, : s.out]
    inv = spec[3:4, : s.out]
    total = sums[:, : s.out] / count
    cross = sums[:, s.out : 2 * s.out] / count
    norm_scale = inv * rstd
    offset = mean * rstd

    def one(b, e, keep, own):
        par, k = e % 2, e // 2
        dots = jnp.zeros((8, s.out), F32)
        for ph in range(2):
            raw = hidden[b, e, ph]
            normed = raw * norm_scale - offset
            grad = keep * (rstd * (dnorm[b, e, ph] - total - normed * cross))
            if own:
                dots += jnp.sum((grad * raw).reshape(w // 8, 8, s.out), axis=0)
            value = grad * inv
            fill(slots, (b, par, k), ph, value, s.slot)
            if own:
                low[1 - par, ph, b, (e - 1) // 2] = value.astype(BF16)
        return dots

    scale[...] = jnp.zeros_like(scale)

    def sent(b):
        return pltpu.make_async_copy(slots.at[b], slots_to.at[b], sems.at[2, b])

    @pl.loop(0, s.images)
    def _(b):
        pltpu.make_async_copy(hidden_from.at[b], hidden.at[b], sems.at[0, b]).wait()
        pltpu.make_async_copy(dnorm_from.at[b], dnorm.at[b], sems.at[1, b]).wait()
        live = live_of(counts, b)
        one(b, 0, live * inside(-1, s, 2), False)
        dots = jnp.zeros((8, s.out), F32)
        for e in range(1, s.ext - 1):
            dots += one(b, e, live, True)
        one(b, s.ext - 1, live * inside(2 * s.rows, s, 2), False)
        scale[0:1, : s.out] += jnp.sum(dots, axis=0, keepdims=True)
        sent(b).start()

    fetch_acts.wait()
    count = s.images * s.rows * w
    depth = 3 * s.chan
    for dy in range(3):
        total = None
        for phase in range(4):
            a, b = divmod(phase, 2)
            flip = jnp.transpose(low[a, b].reshape(count, s.out))
            first = 1 + (a + dy - 1) // 2
            rhs = acts[:, first : first + s.rows, :, b * s.chan : b * s.chan + depth]
            part = dot(flip, rhs.reshape(count, depth))
            total = part if total is None else total + part
        place(s, grads, total, dy * depth, s.n_one, 0)
    for copy in fetch_two:
        copy.wait()
    grads_two(s, slots_two, grad_low, grad_skip, image, grads)
    copies = []
    for ref, to, which in ((other, other_to, 1 - core), (mine, mine_to, core)):
        for x in range(s.n_x):
            at = pl.multiple_of((which * s.n_x + x) * s.part, 8)
            here = pl.ds(at, s.part)
            for r in range(s.rows_n):
                pack_grad(ref, r * s.n_x + x, grads, here, r * s.pitch, s.wide)
        copies.append(start(ref, to, sems.at[4, len(copies)]))
    for b in range(s.images):
        copies.append(sent(b))
    for copy in copies:
        copy.wait()


def input_grad_kernel(sizes, slots, weight, image, stats, proj, terms_two, scale_one, scale_two,
                      misc, dnorm, pay, back, terms, line):
    s = sizes
    w = s.width
    depth = 3 * s.slot
    back[...] = jnp.zeros_like(back)
    for t in range(9):
        dy, dx = divmod(t, 3)
        tap = weight[t * s.chan : (t + 1) * s.chan, :].astype(F32)
        at = (2 - dx) * s.slot
        back[dy, at : at + s.out, :] = jnp.transpose(tap).astype(BF16)
    total = None
    for a in range(2):
        for dy in range(3):
            par, k = (a + 2 - dy) % 2, (a + 2 - dy) // 2
            for ph in range(2):
                lhs = slots[:, par, k : k + s.rows, :, ph * s.slot : ph * s.slot + depth]
                part = dot(lhs.reshape(s.images * s.rows * w, depth), back[dy])
                total = part if total is None else total + part
    total = total.reshape(s.images, s.rows, w, s.chan)
    mean, rstd = stats[0:1, :], stats[1:2, :]
    all_sum = jnp.zeros((1, s.chan), F32)
    all_cross = jnp.zeros((1, s.chan), F32)
    for b in range(s.images):
        gain = 1.0 + proj[b : b + 1, : s.chan]
        shift = proj[b : b + 1, s.chan : 2 * s.chan]
        dsum = jnp.zeros((8, s.chan), F32)
        dgain = jnp.zeros((8, s.chan), F32)
        for i in range(s.rows):
            normed = (image[b, i].astype(F32) - mean) * rstd
            pre = gain * normed + shift
            sig = sigmoid(pre)
            dpre = total[b, i] * (sig * (1.0 + pre * (1.0 - sig)))
            dnorm[b, i] = gain * dpre
            dsum += jnp.sum(dpre.reshape(w // 8, 8, s.chan), axis=0)
            dgain += jnp.sum((dpre * normed).reshape(w // 8, 8, s.chan), axis=0)
        dsum = jnp.sum(dsum, axis=0, keepdims=True)
        dgain = jnp.sum(dgain, axis=0, keepdims=True)
        terms[b : b + 1, : s.chan] = dgain
        terms[b : b + 1, s.chan : 2 * s.chan] = dsum
        terms[b : b + 1, 2 * s.chan :] = terms_two[b : b + 1, : 2 * s.out]
        all_sum += gain * dsum
        all_cross += gain * dgain
    line[...] = jnp.zeros_like(line)
    line[0:1, : s.chan] = all_sum
    line[0:1, s.chan : 2 * s.chan] = all_cross
    at = s.at_scale
    line[0:1, at : at + 1] = jnp.sum(scale_one[0:1, : s.out], axis=1, keepdims=True)
    line[0:1, at + 1 : at + 2] = scale_two[0:1, 0:1]
    line[0:1, at + 2 : at + 3] = jnp.sum(misc[1:2, : s.out], axis=1, keepdims=True)
    at = s.at_gbias
    line[0:1, at : at + s.out] = misc[0:1, : s.out]
    for r in range(s.rows_n):
        for b in range(s.images):
            at = s.at_terms + b * s.cols
            line[0:1, at : at + s.cols] = terms[b : b + 1, r * s.cols : (r + 1) * s.cols]
        whole = line[...]
        for g in range(s.groups):
            pay[r * s.groups + g] = whole


def adamw(weight, first_old, second, gradient, learn_rate):
    first_new = BETA_ONE * first_old + (1.0 - BETA_ONE) * gradient
    second_new = BETA_TWO * second + (1.0 - BETA_TWO) * gradient * gradient
    first_hat = first_new / (1.0 - BETA_ONE**STEP)
    second_hat = second_new / (1.0 - BETA_TWO**STEP)
    weight_new = weight - learn_rate * (
        first_hat / (jnp.sqrt(second_hat) + ADAM_EPS) + DECAY_RATE * weight
    )
    return (weight_new, first_new, second_new)


def store_adamw(refs, olds, gradient, rate):
    for ref, value in zip(refs, adamw(*(old[...] for old in olds), gradient, rate)):
        ref[...] = value


def finish_kernel(sizes, counts, got, cond_all, image, dnorm, grad_skip, skip_w, stats, proj,
                  cw, cm, cv, bw, bm, bv,
                  image_grad, cw_new, cm_new, cv_new, bw_new, bm_new, bv_new, scales, terms, conds):
    s = sizes
    w = s.width
    row_pos, _, _ = position()
    sums = jnp.sum(got[:, :, : s.at_terms], axis=0)
    scales[...] = jnp.broadcast_to(sums[:, s.at_scale : s.at_scale + LANES], scales.shape)
    count = live_total(counts, s) * (w * w)
    total = sums[:, : s.chan] / count
    cross = sums[:, s.chan : 2 * s.chan] / count
    mean, rstd = stats[0:1, :], stats[1:2, :]
    grad = dot(
        grad_skip[...].reshape(s.images * s.rows * w, s.out), skip_w[...], ((1,), (1,))
    ).reshape(s.images, s.rows, w, s.chan)
    for b in range(s.images):
        keep = live_of(counts, b) * rstd
        for i in range(s.rows):
            normed = (image[b, i].astype(F32) - mean) * rstd
            image_grad[b, i] = keep * (dnorm[b, i] - total - normed * cross) + grad[b, i]
    for g in range(s.groups):
        part = got[g, :, s.at_terms :]
        for r in range(1, s.rows_n):
            part = part + got[r * s.groups + g, :, s.at_terms :]
        for b in range(s.images):
            k = g * s.images + b
            terms[k : k + 1, :] = part[:, b * s.cols : (b + 1) * s.cols]
            conds[k : k + 1, :] = cond_all[g, b : b + 1, :].astype(F32)
    grad = dot(terms[...], conds[...], ((0,), (0,)), precise)
    store_adamw((cw_new, cm_new, cv_new), (cw, cm, cv), grad, LEARN_RATES[3])
    grad = sums[:, s.at_gbias : s.at_gbias + s.n_bias]
    for r in range(1, s.rows_n):
        at = s.at_gbias + r * s.n_bias
        grad = jnp.where(row_pos == r, sums[:, at : at + s.n_bias], grad)
    store_adamw((bw_new, bm_new, bv_new), (bw, bm, bv), grad, LEARN_RATES[4])


def weights_kernel(sizes, own, beside, beyond, across, scales, spec, left_one, left_two, left_skip,
                   ow, om, ov, tw, tm, tv, sw, sm, sv,
                   ow_new, om_new, ov_new, tw_new, tm_new, tv_new, sw_new, sm_new, sv_new, grads):
    s = sizes
    _, x_pos, core = position()
    columns = jnp.transpose(spec[...])

    def factor(k):
        inv = spec[3 + k : 4 + k, 0:1]
        return scales[0:1, k : k + 1] * inv * inv * spec[8 + k : 9 + k, 0:1]

    def place(parts, which):
        for x, part in enumerate(parts):
            at = pl.multiple_of((which * s.n_x + x) * s.part, 8)
            here = pl.ds(at, s.part)
            grads[here, : s.wide] = unpack_grad(part, 0, s.part, s.wide)

    def ordered(mine, other):
        if s.n_x != 2:
            return [mine[x] for x in range(s.n_x)]
        a, b = mine[0], other[0]
        return [jnp.where(x_pos == 0, a, b), jnp.where(x_pos == 0, b, a)]

    place(ordered(own, beside), core)
    place(ordered(beyond, across), 1 - core)

    grad = grads[:, : s.n_one] - columns[: s.out, 0:1] * (left_one[...] * factor(0))
    store_adamw((ow_new, om_new, ov_new), (ow, om, ov), grad, LEARN_RATES[0])
    grad = grads[:, s.n_one : s.n_one + s.n_two] - columns[: s.out, 1:2] * (left_two[...] * factor(1))
    store_adamw((tw_new, tm_new, tv_new), (tw, tm, tv), grad, LEARN_RATES[1])
    grad = jnp.transpose(grads[:, s.n_one + s.n_two : s.wide])
    grad = grad - (left_skip[...] * factor(2)) * spec[2:3, : s.out]
    store_adamw((sw_new, sm_new, sv_new), (sw, sm, sv), grad, LEARN_RATES[2])


def share(chunks):
    return lax.all_to_all(chunks, ALL, 0, 0, tiled=True)


def core_swap(values):
    return lax.ppermute(values, "core", [(0, 1), (1, 0)])


def row_swaps(near, far):
    devices = lax.axis_size("rows")
    pairs = [(i, i ^ 1) for i in range(devices)]
    odd = [(i, i + 1) for i in range(1, devices - 1, 2)]
    odd = odd + [(j, i) for i, j in odd]
    return lax.ppermute(near, "rows", pairs), lax.ppermute(far, "rows", odd)


def row_swap(values, step):
    devices = lax.axis_size("rows")
    return lax.ppermute(values, "rows", [(i, i ^ step) for i in range(devices)])


def x_swap(values):
    return lax.ppermute(values, "x", [(0, 1), (1, 0)])


def gather_upper(block):
    return [block] + [row_swap(block, 2 * m) for m in range(1, lax.axis_size("rows") // 2)]


def gather_groups(values):
    if lax.axis_size("x") != 2:
        return lax.all_gather(values, ("x", "core"), axis=0)
    x, core = lax.axis_index("x"), lax.axis_index("core")
    pair = jnp.stack([values, core_swap(values)])
    pair = jnp.where(core == 0, pair, pair[::-1])
    both = jnp.stack([pair, x_swap(pair)])
    both = jnp.where(x == 0, both, both[::-1])
    return both.reshape(4, *values.shape)


def first_sum_kernel(mine, got, send_a, keep_a, send_b, keep_b):
    _, x, _ = position()
    low = lax.rem(lax.axis_index("rows"), 2)
    half = send_a.shape[0]
    for i in range(half):
        for k in range(2):
            send_a[i, k] = mine[i, k, 1 - x] + got[i, k, 1 - x]
            keep_a[i, k] = mine[i, k, x] + got[i, k, x]
            send_b[i, k] = mine[half + i, 1 - low, k] + got[half + i, 1 - low, k]
            keep_b[i, k] = mine[half + i, low, k] + got[half + i, low, k]


def second_sum_kernel(keep_a, got_a, keep_b, got_b, send_a, held_a, send_b, held_b):
    _, x, _ = position()
    low = lax.rem(lax.axis_index("rows"), 2)
    for i in range(keep_a.shape[0]):
        send_a[i] = keep_a[i, 1 - low] + got_a[i, 1 - low]
        held_a[i] = keep_a[i, low] + got_a[i, low]
        send_b[i] = keep_b[i, 1 - x] + got_b[i, 1 - x]
        held_b[i] = keep_b[i, x] + got_b[i, x]


def third_sum_kernel(held_a, got_a, held_b, got_b, *outs):
    high = lax.axis_index("rows") // 2
    half = held_a.shape[0]
    for m, out in enumerate(outs):
        at = high ^ m

        @pl.when(at < half)
        def _():
            out[0] = held_a[jnp.minimum(at, half - 1)] + got_a[jnp.minimum(at, half - 1)]

        @pl.when(at >= half)
        def _():
            at_b = jnp.maximum(at - half, 0)
            out[0] = held_b[at_b] + got_b[at_b]


def sum_kernel(*refs):
    *parts, out = refs
    total = parts[0][...]
    for part in parts[1:]:
        total = total + part[...]
    out[...] = total


def tied(values, after):
    return list(lax.optimization_barrier((tuple(values), tuple(after)))[0])


class StagedSum:
    small = 8 * 2**20

    def __init__(self, mine, other, after):
        self.high = lax.axis_size("rows") // 2
        self.tail = mine.shape[1:]
        mine = mine.reshape(self.high, 2, 2, *self.tail)
        got = core_swap(other).reshape(self.high, 2, 2, *self.tail)
        send_a, keep_a, send_b, keep_b = run(
            first_sum_kernel,
            [shape((self.high // 2, 2, *self.tail))] * 4,
            tied([mine, got], after),
            scalars=0,
            limit=self.small,
        )
        self.held = [keep_a, x_swap(send_a), keep_b, row_swap(send_b, 1)]

    def second(self, after):
        send_a, held_a, send_b, held_b = run(
            second_sum_kernel,
            [shape((self.high // 2, *self.tail))] * 4,
            tied(self.held, after),
            scalars=0,
            limit=self.small,
        )
        self.held = [held_a, row_swap(send_a, 1), held_b, x_swap(send_b)]

    def third(self, after):
        parts = run(
            third_sum_kernel,
            [shape((1, *self.tail))] * self.high,
            tied(self.held, after),
            scalars=0,
            limit=self.small,
        )
        self.held = [parts[0]] + [row_swap(parts[m], 2 * m) for m in range(1, self.high)]

    def last(self, after):
        (total,) = run(
            sum_kernel,
            [shape((1, *self.tail))],
            tied(self.held, after),
            scalars=0,
            limit=self.small,
        )
        return total


class PlainSum:
    def __init__(self, mine, other, after):
        self.held = lax.all_to_all(mine + core_swap(other), ("rows", "x"), 0, 0, tiled=True)

    def second(self, after):
        pass

    def third(self, after):
        pass

    def last(self, after):
        return jnp.sum(self.held, axis=0, keepdims=True)


def spread(total):
    if lax.axis_size("x") == 2:
        beside = x_swap(total)
        return total, beside, core_swap(total), core_swap(beside)
    total = lax.all_gather(total, "x", axis=0, tiled=True)
    beyond = core_swap(total)
    return total, total, beyond, beyond


def body(
    image_in,
    condition,
    group_counts,
    out_cotangent,
    power_vectors,
    conv1_weight,
    conv2_weight,
    skip_weight,
    cond_weight,
    out_bias,
    conv1_first,
    conv2_first,
    skip_first,
    cond_first,
    bias_first,
    conv1_second,
    conv2_second,
    skip_second,
    cond_second,
    bias_second,
):
    rows_n = lax.axis_size("rows")
    n_x = lax.axis_size("x")
    groups_n = 2 * n_x
    masters = [conv1_weight, conv2_weight, skip_weight, cond_weight, out_bias]
    s = Sizes(
        image_in.shape, out_cotangent.shape, condition.shape, [m.shape for m in masters], rows_n, n_x
    )
    bind = functools.partial
    scratch = pltpu.VMEM
    n, w = s.images, s.width
    depth = 3 * s.slot

    pay, half_one, half_two, near, far, left_one, left_two, left_skip = run(
        bind(prep_kernel, s),
        [
            shape((s.devices, 1, s.pay_one)),
            shape((s.pack_one, LANES), BF16),
            shape((s.pack_two, LANES), BF16),
            shape((n, 3 * w, LANES), BF16),
            shape((n, 3 * w, LANES), BF16),
            shape((1, s.n_one)),
            shape((1, s.n_two)),
            shape((s.n_skip, 1)),
        ],
        [
            group_counts,
            image_in,
            condition,
            power_vectors,
            conv1_weight.T,
            conv2_weight.T,
            skip_weight,
            cond_weight.T,
            out_bias[None],
        ],
        [scratch((1, s.pay_one), F32)],
        limit=60 * 2**20,
    )
    blocks = gather_upper(half_one)
    near, far = row_swaps(near, far)
    (pay,) = tied([pay], [near])
    got_one = share(pay)
    acts, proj, stats_one, spec, near_cot, far_cot = run(
        bind(act_kernel, s),
        [
            shape((n, s.rows + 2, w, 4 * s.chan), BF16),
            shape((n, rows_n * s.cols)),
            shape((2, s.chan)),
            shape((16, s.slot)),
            *[shape((n, 6 * w, LANES), BF16)] * 2,
        ],
        [group_counts, got_one, image_in, near, far],
        [pltpu.SemaphoreType.DMA((2,))],
        flops=0, idle=True,
        whole=[out_cotangent],
        limit=52 * 2**20,
    )
    near_one = jnp.stack(blocks)
    (half_two,) = tied([half_two], [near_one])
    far_one = row_swap(near_one, 1)
    near_two = jnp.stack(gather_upper(half_two))
    far_one, near_two, acts = lax.optimization_barrier((far_one, near_two, acts))
    blocks_one = near_one, far_one, core_swap(near_one), core_swap(far_one)

    far_two = row_swap(near_two, 1)
    near_cot, far_cot = row_swaps(near_cot, far_cot)
    hidden, weight_one, pay = run(
        bind(conv_one_kernel, s),
        [
            shape((n, s.ext, 2, w, s.out)),
            shape((9 * s.chan, s.out), BF16),
            shape((s.devices, 1, s.pay_two)),
        ],
        [group_counts, acts, *blocks_one],
        [scratch((1, s.pay_two), F32), scratch((9 * s.chan, s.out), F32)],
        flops=2 * n * s.ext * 2 * w * 9 * s.chan * s.out,
        limit=52 * 2**20,
    )
    far_two, near_cot, pay = lax.optimization_barrier((far_two, near_cot, pay))
    blocks_two = near_two, far_two, core_swap(near_two), core_swap(far_two)
    got_two = share(pay)
    dact, phases, grad_low, grad_skip, skip_part, weight_two, weight_skip, misc = run(
        bind(cot_kernel, s),
        [
            shape((n, s.ext, 2, w, s.out)),
            shape((n, 2 * s.rows, 2, w, s.out), BF16),
            shape((n, 2 * s.rows, 2, w, s.out), BF16),
            shape((n, s.rows, w, s.out), BF16),
            shape((n, s.rows, w, s.out)),
            shape((3, depth, s.out), BF16),
            shape((s.chan, s.out), BF16),
            shape((8, s.slot)),
        ],
        [group_counts, out_cotangent, near_cot, far_cot, image_in, *blocks_two, spec],
        [
            scratch((n, 2 * s.rows + 4, w, 4 * s.slot), BF16),
            scratch((9 * s.out + s.chan, s.out), F32),
            scratch((2, 2 * w, LANES), F32),
            scratch((3, depth, s.out), BF16),
        ],
        flops=2 * n * s.ext * 2 * w * 9 * s.out * s.out,
        limit=52 * 2**20,
    )
    stats_two, terms_two, pay, slots_two, dnorm = run(
        bind(norm_two_kernel, s),
        [shape((2, s.slot)), shape((8, 2 * s.slot)), shape((s.devices, 1, s.pay_two))],
        [group_counts, got_two, spec, proj],
        [scratch((1, s.pay_two), F32), pltpu.SemaphoreType.DMA((4, n))],
        whole=[hidden, dact],
        results=[shape((n, s.ext, w, 4 * s.slot), BF16), shape((n, s.ext, 2, w, s.out))],
        limit=53 * 2**20,
    )
    got_three = share(pay)
    sent = shape((s.rows_n * n_x, s.grad_rows, LANES))
    scale_one, other, mine, slots_one = run(
        bind(hidden_grad_kernel, s),
        [shape((8, s.slot))],
        [group_counts, got_three, stats_two, spec, grad_skip, image_in],
        [
            scratch((2, 2, n, s.rows, w, s.out), BF16),
            scratch((s.out, rows_n * s.pitch), F32),
            pltpu.SemaphoreType.DMA((5, max(n, 3))),
        ],
        flops=8 * n * s.rows * w * 9 * s.chan * s.out,
        whole=[dnorm, hidden, acts, slots_two, grad_low],
        results=[sent, sent, shape((n, 2, s.rows + 1, w, 4 * s.slot), BF16)],
        limit=48 * 2**20,
    )
    out_image, scale_two = run(
        bind(conv_two_kernel, s),
        [shape(out_cotangent.shape, BF16), shape((8, LANES))],
        tied([slots_two, weight_two, phases, skip_part, spec], [scale_one]),
        [scratch((2, 2 * w, LANES), F32)],
        scalars=0,
        flops=8 * n * s.rows * 2 * w * 9 * s.out * s.out,
        limit=48 * 2**20,
    )
    sums = (StagedSum if n_x == 2 else PlainSum)(mine, other, [scale_two])
    dnorm_one, pay = run(
        bind(input_grad_kernel, s),
        [shape((n, s.rows, w, s.chan)), shape((s.devices, 1, s.pay_four))],
        [slots_one, weight_one, image_in, stats_one, proj, terms_two, scale_one, scale_two, misc],
        [
            scratch((3, depth, s.chan), BF16),
            scratch((8, rows_n * s.cols), F32),
            scratch((1, s.pay_four), F32),
        ],
        scalars=0,
        flops=8 * n * s.rows * w * 9 * s.chan * s.out,
    )
    sums.second([pay])
    late_condition, pay = lax.optimization_barrier((condition, pay))
    cond_all = gather_groups(late_condition)
    got_four = share(pay)
    sums.third([got_four])
    moments = [cond_weight, cond_first, cond_second]
    biases = [out_bias, bias_first, bias_second]
    image_grad, *rest, scales = run(
        bind(finish_kernel, s),
        [
            shape(image_in.shape),
            *[shape((s.cols, s.cond))] * 3,
            *[shape((1, s.n_bias))] * 3,
            shape((8, LANES)),
        ],
        [
            group_counts,
            got_four,
            cond_all,
            image_in,
            dnorm_one,
            grad_skip,
            weight_skip,
            stats_one,
            proj,
            *[m.T for m in moments],
            *[b[None] for b in biases],
        ],
        [
            scratch((groups_n * n, s.cols), F32),
            scratch((groups_n * n, s.cond), F32),
        ],
        limit=60 * 2**20,
    )
    parts = spread(sums.last([scales]))
    cond_new = [c.T for c in rest[:3]]
    bias_new = [b[0] for b in rest[3:]]
    olds = [
        *[m.T for m in (conv1_weight, conv1_first, conv1_second)],
        *[m.T for m in (conv2_weight, conv2_first, conv2_second)],
        skip_weight,
        skip_first,
        skip_second,
    ]
    news = run(
        bind(weights_kernel, s),
        [shape(o.shape) for o in olds],
        [*parts, scales, spec, left_one, left_two, left_skip, *olds],
        [scratch((s.out, s.pitch), F32)],
        limit=24 * 2**20,
        scalars=0,
    )
    weights_new = [m.T for m in news[:6]] + list(news[6:])
    return (out_image, image_grad, *weights_new, *cond_new, *bias_new)


def solution(mesh):
    rows_n, imgs_n = mesh.devices.shape
    fine = Mesh(np.asarray(mesh.devices).reshape(rows_n, imgs_n // 2, 2), ALL)
    groups = ("x", "core")
    picture = P(groups, "rows", None, None)
    weight = P("rows", None)
    column = P(None, "rows")
    masters = (weight, weight, weight, column, P("rows"))
    return jax.shard_map(
        body,
        mesh=fine,
        in_specs=(picture, P(groups, None), P(), picture, P(), *masters, *masters, *masters),
        out_specs=(
            picture,
            picture,
            *(weight,) * 9,
            *(column,) * 3,
            *(P("rows"),) * 3,
        ),
        check_vma=False,
    )
```
